32 devices in a mesh: dom: 32 (over z, y, x, core).
Axes of the slice: x: 2, y: 2, z: 4, core: 2. Of those that a mesh axis runs over, the one named last changes fastest.
Arguments:
- features: float32 [131072, 100], P('dom'), may hold values from -6 to 6
- labels: int32 [131072], P('dom'), may hold values from 0 to 46
- train_mask: int32 [131072], P('dom'), may hold values from 0 to 1, as said below
- boundary: int32 [3, 4096], P(None, 'dom'), may hold values from 0 to 4095
- neighbours: int32 [3, 131072, 16], P(None, 'dom'), may hold values from 0 to 8191, as said below
- counts: int32 [3, 131072], P(None, 'dom'), may hold values from 1 to 16, as said below
- first_weight: float32 [200, 256], P(None, 'dom'), may hold values from -0.4375 to 0.4375
- rest_weight: float32 [2, 512, 256], P(None, None, 'dom'), may hold values from -0.25 to 0.25
- head_weight: float32 [256, 47], P('dom'), may hold values from -0.375 to 0.375
- norm_params: float32 [3, 2, 256], replicated
- head_bias: float32 [47], replicated, may hold values from -3 to 3
- first_row: float32 [200], replicated, may hold values from 6.1035155e-09 to 2.4414062e-08
- first_col: float32 [256], P('dom'), may hold values from 6.1035155e-09 to 2.4414062e-08
- rest_row: float32 [2, 512], replicated, may hold values from 5.340576e-09 to 2.1362304e-08
- rest_col: float32 [2, 256], P(None, 'dom'), may hold values from 5.340576e-09 to 2.1362304e-08
- head_row: float32 [256], P('dom'), may hold values from 1.14440915e-07 to 4.5776366e-07
- head_col: float32 [47], replicated, may hold values from 1.14440915e-07 to 4.5776366e-07
- norm_state: float32 [3, 2, 256], replicated, may hold values from 7.629395e-09 to 6.103516e-08
- bias_state: float32 [47], replicated, may hold values from 3.0517577e-07 to 1.2207031e-06
Outputs:
- loss_sum: float32 [], replicated
- label_count: float32 [], replicated
- first_new: float32 [200, 256], P(None, 'dom')
- rest_new: float32 [2, 512, 256], P(None, None, 'dom')
- head_new: float32 [256, 47], P('dom')
- norm_new: float32 [3, 2, 256], replicated
- bias_new: float32 [47], replicated
- first_grad: float32 [200, 256], P(None, 'dom')
- rest_grad: float32 [2, 512, 256], P(None, None, 'dom')
- head_grad: float32 [256, 47], P('dom')
- norm_grad: float32 [3, 2, 256], replicated
- bias_grad: float32 [47], replicated
- first_row_new: float32 [200], replicated
- first_col_new: float32 [256], P('dom')
- rest_row_new: float32 [2, 512], replicated
- rest_col_new: float32 [2, 256], P(None, 'dom')
- head_row_new: float32 [256], P('dom')
- head_col_new: float32 [47], replicated
- norm_state_new: float32 [3, 2, 256], replicated
- bias_state_new: float32 [47], replicated
- first_copy: bfloat16 [200, 256], P(None, 'dom')
- rest_copy: bfloat16 [2, 512, 256], P(None, None, 'dom')
- head_copy: bfloat16 [256, 47], P('dom')
- norm_copy: bfloat16 [3, 2, 256], replicated
The draws below stay inside these ranges and needn't reach their ends.
Inputs may be any that keep to these rules, and one draw needn't show every extreme that they name: `neighbours`: entries at slots k >= counts are 0. A value t + 4096 names boundary slot t; the slots that partition q publishes are used only below a kept number that runs from 42 to 128 over the partitions, both ends reached; the last partition keeps all 128. In each layer, node 0's slot 0 names the last boundary slot. `counts`: each layer's first node has 16 kept neighbours. `train_mask`: node 0 is labelled.
All inputs are finite; a program needn't handle non-finite values.
Results may differ from the reference program's by a relative error of at most 0.012.
The reference program's roundings to bfloat16 on the way count: a program that leaves them out, or rounds other values in their place, can miss the bound.
Values may be sent and summed in bfloat16 or wider, within the bound.
No kernel may reach another device: no remote copies, remote signals or barrier semaphores. Data moves between devices by JAX's collectives and lax.ppermute only.
A program may use at most 256 MiB of HBM per device.

```python
import math
import jax
import jax.numpy as jnp
from jax import lax

F_IN = 100
HID = 256
CLS = 47
LAYERS = 3
K = 16
NODE_DEV = 4096
BND = 128
NODES = 131072
BND_ALL = 4096


def graph_plan(key):
    base_key = jax.random.fold_in(key, 7)
    part_count = NODES // NODE_DEV
    spread_den = max(part_count - 1, 1)
    lower_ranks = jax.random.permutation(jax.random.fold_in(base_key, 1), part_count - 1)
    rank_order = jnp.concatenate([lower_ranks, jnp.full((1,), part_count - 1, jnp.int32)]).astype(jnp.int32)
    kept_sizes = BND // 3 + (BND - BND // 3) * rank_order // spread_den
    remote_order = jax.random.permutation(jax.random.fold_in(base_key, 2), part_count)
    remote_pct = 10 + 30 * remote_order // spread_den
    kept_count = jax.random.randint(jax.random.fold_in(base_key, 3), (LAYERS, NODES), 1, K + 1)
    kept_count = kept_count.at[:, 0].set(K)
    shape_all = (LAYERS, NODES, K)
    local_ids = jax.random.randint(jax.random.fold_in(base_key, 4), shape_all, 0, NODE_DEV)
    peer_part = jax.random.randint(jax.random.fold_in(base_key, 5), shape_all, 0, part_count)
    fraction = jax.random.randint(jax.random.fold_in(base_key, 6), shape_all, 0, 2 ** 20)
    slot_pick = fraction * kept_sizes[peer_part] // 2 ** 20
    remote = NODE_DEV + peer_part * BND + slot_pick
    dice_roll = jax.random.randint(jax.random.fold_in(base_key, 8), shape_all, 0, 100)
    owner_part = jnp.arange(NODES, dtype=jnp.int32) // NODE_DEV
    is_remote = dice_roll < remote_pct[owner_part][None, :, None]
    slot_ids = jnp.where(is_remote, remote, local_ids)
    slot_live = jnp.arange(K, dtype=jnp.int32)[None, None, :] < kept_count[:, :, None]
    slot_ids = jnp.where(slot_live, slot_ids, 0)
    slot_ids = slot_ids.at[:, 0, 0].set(NODE_DEV + part_count * BND - 1)
    return (slot_ids.astype(jnp.int32), kept_count.astype(jnp.int32))


def draw_neighbours(key, part):
    return graph_plan(key)[0]


def draw_counts(key, part):
    return graph_plan(key)[1]


def draw_train_mask(key, part):
    key = jax.random.fold_in(key, 21)
    part_count = NODES // NODE_DEV
    owner_part = jnp.arange(NODES, dtype=jnp.int32) // NODE_DEV
    threshold = 250 + 500 * owner_part // max(part_count - 1, 1)
    marks = (jax.random.randint(key, (NODES,), 0, 1000) < threshold).astype(jnp.int32)
    return marks.at[0].set(1).astype(jnp.int32)


def draw_norm_params(key, part):
    key_gain = jax.random.fold_in(key, 11)
    key_shift = jax.random.fold_in(key, 12)
    gains = 1.0 + 0.15 * jnp.clip(jax.random.normal(key_gain, (LAYERS, 1, HID), jnp.float32), -3.0, 3.0)
    shifts = 0.3 * jnp.clip(jax.random.normal(key_shift, (LAYERS, 1, HID), jnp.float32), -3.0, 3.0)
    return jnp.concatenate([gains, shifts], axis=1)


def with_ends(values, stream_key, smallest, top_value):
    shape = values.shape
    index_at = [jax.random.randint(jax.random.fold_in(stream_key, axis), (), 0, shape[axis]) for axis in range(len(shape))]
    values = values.at[tuple(index_at)].set(smallest)
    longest = shape.index(max(shape))
    index_at[longest] = (index_at[longest] + 1) % shape[longest]
    return values.at[tuple(index_at)].set(top_value)


def steps_of(rng, extent, cuts, least, largest):
    level, own = 1.0, jax.random.fold_in(rng, 6)
    for dim, blocks in cuts:
        steps = jnp.exp(jax.random.uniform(jax.random.fold_in(own, dim), (blocks,), jnp.float32, least / len(cuts), largest / len(cuts)))
        level = level * jnp.repeat(steps, extent[dim] // blocks).reshape([-1 if axis == dim else 1 for axis in range(len(extent))])
    return level


def centred(own_key, dims, width, reach, cuts=(), kind=jnp.bfloat16):
    array = width * jax.random.normal(own_key, dims, jnp.float32)
    if cuts:
        array = array * steps_of(own_key, dims, cuts, -0.22, 0.18)
    return jnp.clip(array, -reach, reach).astype(kind)


def setup_inputs(seed: int = 0) -> dict:
    splits = jax.random.split(jax.random.key(seed), 20)
    features = centred(splits[0], (NODES, F_IN), 1.0, 6.0, ((0, 32),), jnp.float32)
    labels = with_ends(jax.random.randint(splits[1], (NODES,), 0, CLS), jax.random.fold_in(splits[1], 1), 0, CLS - 1).astype(jnp.int32)
    train_mask = draw_train_mask(jax.random.fold_in(splits[19], 71), 0)
    boundary = with_ends(jax.random.randint(splits[3], (LAYERS, BND_ALL), 0, NODE_DEV), jax.random.fold_in(splits[3], 1), 0, NODE_DEV - 1).astype(jnp.int32)
    neighbours = draw_neighbours(jax.random.fold_in(splits[19], 71), 0)
    counts = draw_counts(jax.random.fold_in(splits[19], 71), 0)
    first_weight = centred(splits[6], (2 * F_IN, HID), (2 * F_IN) ** -0.5, 0.4375, ((1, 32),), jnp.float32)
    rest_weight = centred(splits[7], (LAYERS - 1, 2 * HID, HID), (2 * HID) ** -0.5, 0.25, ((2, 32),), jnp.float32)
    head_weight = centred(splits[8], (HID, CLS), HID ** -0.5, 0.375, ((0, 32),), jnp.float32)
    norm_params = draw_norm_params(jax.random.fold_in(splits[19], 71), 0)
    head_bias = centred(splits[10], (CLS,), 0.5, 3.0, (), jnp.float32)
    first_row = jnp.clip(jnp.exp(jax.random.uniform(splits[11], (2 * F_IN,), jnp.float32, math.log(6.103515470812226e-09), math.log(2.4414061883248905e-08))), 6.103515470812226e-09, 2.4414061883248905e-08)
    first_col = jnp.clip(jnp.exp(math.log(2.4414061883248905e-08) - 1.3862944 * jax.random.uniform(splits[12], (HID,), jnp.float32) ** steps_of(splits[12], (HID,), ((0, 32),), -0.2, 0.2)), 6.103515470812226e-09, 2.4414061883248905e-08)
    rest_row = jnp.clip(jnp.exp(jax.random.uniform(splits[13], (LAYERS - 1, 2 * HID), jnp.float32, math.log(5.340575981449547e-09), math.log(2.1362303925798187e-08))), 5.340575981449547e-09, 2.1362303925798187e-08)
    rest_col = jnp.clip(jnp.exp(math.log(2.1362303925798187e-08) - 1.3862944 * jax.random.uniform(splits[14], (LAYERS - 1, HID), jnp.float32) ** steps_of(splits[14], (LAYERS - 1, HID), ((1, 32),), -0.2, 0.2)), 5.340575981449547e-09, 2.1362303925798187e-08)
    head_row = jnp.clip(jnp.exp(math.log(4.577636616431846e-07) - 1.3862944 * jax.random.uniform(splits[15], (HID,), jnp.float32) ** steps_of(splits[15], (HID,), ((0, 32),), -0.2, 0.2)), 1.1444091541079615e-07, 4.577636616431846e-07)
    head_col = jnp.clip(jnp.exp(jax.random.uniform(splits[16], (CLS,), jnp.float32, math.log(1.1444091541079615e-07), math.log(4.577636616431846e-07))), 1.1444091541079615e-07, 4.577636616431846e-07)
    norm_state = jnp.clip(jnp.exp(jax.random.uniform(splits[17], (LAYERS, 2, HID), jnp.float32, math.log(7.629394893626795e-09), math.log(6.103515914901436e-08))), 7.629394893626795e-09, 6.103515914901436e-08)
    bias_state = jnp.clip(jnp.exp(jax.random.uniform(splits[18], (CLS,), jnp.float32, math.log(3.0517577442878974e-07), math.log(1.220703097715159e-06))), 3.0517577442878974e-07, 1.220703097715159e-06)
    return dict(features=features, labels=labels, train_mask=train_mask, boundary=boundary, neighbours=neighbours, counts=counts, first_weight=first_weight, rest_weight=rest_weight, head_weight=head_weight, norm_params=norm_params, head_bias=head_bias, first_row=first_row, first_col=first_col, rest_row=rest_row, rest_col=rest_col, head_row=head_row, head_col=head_col, norm_state=norm_state, bias_state=bias_state)


@jax.custom_vjp
def low(v):
    return lax.optimization_barrier(v.astype(jnp.bfloat16)).astype(jnp.float32)

@jax.custom_vjp
def low_back(v):
    return v

def low_keep(v):
    return (low(v), None)

def low_pass(kept, grad):
    return (grad,)

def back_keep(v):
    return (v, None)

def back_low(kept, grad):
    return (low(grad),)
low.defvjp(low_keep, low_pass)
low_back.defvjp(back_keep, back_low)
LEARN_RATE = 0.03
VECTOR_RATE = 0.25
SQUARE_EPS = 1e-30

def product(left, right):
    return jnp.dot(left, right, preferred_element_type=jnp.float32, precision=lax.Precision.HIGHEST)

def sage_loss(weights_all, features, labels, train_mask, boundary, neighbours, counts):
    first_weight, rest_weight, head_weight, norm_params, head_bias = weights_all
    owner_part = jnp.arange(NODES, dtype=jnp.int32) // NODE_DEV
    hidden = features
    for layer_id in range(LAYERS):
        weight = first_weight if layer_id == 0 else rest_weight[layer_id - 1]
        rounded = low(hidden)
        slot_ids = neighbours[layer_id]
        table_slot = jnp.clip(slot_ids - NODE_DEV, 0, BND_ALL - 1)
        remote = table_slot // BND * NODE_DEV + boundary[layer_id][table_slot]
        node_ids = jnp.where(slot_ids < NODE_DEV, owner_part[:, None] * NODE_DEV + slot_ids, remote)
        kept_count = counts[layer_id]
        slot_live = (jnp.arange(K, dtype=jnp.int32)[None, :] < kept_count[:, None]).astype(jnp.float32)
        slot_total = jnp.zeros(rounded.shape, jnp.float32)
        for slot_no in range(K):
            slot_total = slot_total + slot_live[:, slot_no:slot_no + 1] * rounded[node_ids[:, slot_no]]
        mean_in = low(slot_total / kept_count[:, None].astype(jnp.float32))
        pre_norm = low_back(product(jnp.concatenate([rounded, mean_in], axis=1), low(weight)))
        centre = pre_norm - lax.optimization_barrier(jnp.mean(pre_norm, axis=1, keepdims=True))
        normed = centre * lax.rsqrt(lax.optimization_barrier(jnp.mean(centre * centre, axis=1, keepdims=True)) + 1e-05)
        hidden = jax.nn.silu(normed * norm_params[layer_id, 0] + norm_params[layer_id, 1])
    logits = low_back(product(low(hidden), low(head_weight)) + head_bias)
    log_total = jax.nn.logsumexp(logits, axis=1)
    picked = jnp.take_along_axis(logits, labels[:, None].astype(jnp.int32), axis=1)[:, 0]
    label_live = train_mask.astype(jnp.float32)
    loss_sum = jnp.sum(label_live * (log_total - picked))
    label_count = jnp.sum(label_live)
    return (loss_sum / label_count, (loss_sum, label_count))

def factored_step(weight, gradient, row_old, col_old):
    squares = gradient * gradient + SQUARE_EPS
    row_new = 0.5 * row_old + 0.5 * lax.optimization_barrier(jnp.mean(squares, axis=-1))
    col_new = 0.5 * col_old + 0.5 * lax.optimization_barrier(jnp.mean(squares, axis=-2))
    row_mean = lax.optimization_barrier(jnp.mean(row_new, axis=-1))
    estimate = row_new[..., :, None] * col_new[..., None, :] / row_mean[..., None, None]
    return (weight - LEARN_RATE * gradient * lax.rsqrt(estimate), row_new, col_new)

def vector_step(param, gradient, state):
    state_new = 0.5 * state + 0.5 * (gradient * gradient + SQUARE_EPS)
    return (param - VECTOR_RATE * gradient * lax.rsqrt(state_new), state_new)

def reference(features, labels, train_mask, boundary, neighbours, counts, first_weight, rest_weight, head_weight, norm_params, head_bias, first_row, first_col, rest_row, rest_col, head_row, head_col, norm_state, bias_state):
    weights_all = (first_weight, rest_weight, head_weight, norm_params, head_bias)

    def closed(weights_in):
        return sage_loss(weights_in, features, labels, train_mask, boundary, neighbours, counts)
    mean_loss, pullback, sums = jax.vjp(closed, weights_all, has_aux=True)
    loss_sum, label_count = sums
    grads = pullback(jnp.ones((), mean_loss.dtype))[0]
    first_grad, rest_grad, head_grad, norm_grad, bias_grad = grads
    first_new, first_row_new, first_col_new = factored_step(first_weight, first_grad, first_row, first_col)
    rest_new, rest_row_new, rest_col_new = factored_step(rest_weight, rest_grad, rest_row, rest_col)
    head_new, head_row_new, head_col_new = factored_step(head_weight, head_grad, head_row, head_col)
    norm_new, norm_state_new = vector_step(norm_params, norm_grad, norm_state)
    bias_new, bias_state_new = vector_step(head_bias, bias_grad, bias_state)
    return (loss_sum, label_count, first_new, rest_new, head_new, norm_new, bias_new, first_grad, rest_grad, head_grad, norm_grad, bias_grad, first_row_new, first_col_new, rest_row_new, rest_col_new, head_row_new, head_col_new, norm_state_new, bias_state_new, first_new.astype(jnp.bfloat16), rest_new.astype(jnp.bfloat16), head_new.astype(jnp.bfloat16), norm_new.astype(jnp.bfloat16))
```

```python
import functools

import jax
import jax.numpy as jnp
from jax import lax
from jax.experimental import pallas as pl
from jax.experimental.pallas import tpu as pltpu
from jax.sharding import PartitionSpec as P

LEARN_RATE = 0.03
VECTOR_RATE = 0.25
SQUARE_EPS = 1e-30
NORM_EPS = 1e-05

BF = jnp.bfloat16
F32 = jnp.float32
F8 = jnp.float8_e4m3fn
I32 = jnp.int32

D00 = (((0,), (0,)), ((), ()))
D11 = (((1,), (1,)), ((), ()))
D10 = (((1,), (0,)), ((), ()))

LO = 256
BUILD_NODES = 256
GROUP_NODES = 16
FWD_NODES = 512
BWD_COLS = 1024


def mm(left, right, dims):
    return lax.dot_general(left, right, dims, preferred_element_type=F32)


def iota(shape, dim):
    return lax.broadcasted_iota(I32, shape, dim)


def params():
    return pltpu.CompilerParams(vmem_limit_bytes=56 << 20)


def whole(shape):
    return pl.BlockSpec(shape, lambda i: (0,) * len(shape))


def hop(value, mask, total):
    return lax.ppermute(value, "dom", [(i, i ^ mask) for i in range(total)])


def reverse_bits(value, bits):
    out = 0
    for b in range(bits):
        out = out | (((value >> b) & 1) << (bits - 1 - b))
    return out


def gather_rows(rows, total):
    mask = total // 2
    while mask:
        rows = jnp.concatenate([rows, hop(rows, mask, total)], axis=0)
        mask //= 2
    return rows


def scatter_rows(rows, total):
    mask = 1
    while mask < total:
        half = rows.shape[0] // 2
        rows = rows[:half] + hop(rows[half:], mask, total)
        mask *= 2
    return rows


def sum_all(value, total):
    mask = 1
    while mask < total:
        value = value + hop(value, mask, total)
        mask *= 2
    return value


def build_kernel(me_ref, ids_ref, cnt_ref, loc_ref, bnd_ref, base_ref, low_ref, *, layer, bits, own):
    slots, nodes = ids_ref.shape[1:]
    loc_blocks = loc_ref.shape[1] // LO
    bnd_blocks = bnd_ref.shape[1] // LO
    node_total = loc_ref.shape[1]
    ids = ids_ref[0]
    count = cnt_ref[layer : layer + 1, :]
    table = ids - node_total
    part = reverse_bits((table // own) ^ me_ref[0], bits)
    moved = node_total + part * own + table % own
    ids = jnp.where(ids < node_total, ids, moved)
    ids = jnp.where(iota((slots, nodes), 0) < count, ids, -1)
    high = (ids >> 8).astype(F32).astype(BF)
    low = (ids & 255).astype(F32).astype(BF)
    width = slots * GROUP_NODES
    spread = (iota((slots, width), 0) == iota((slots, width), 1) // GROUP_NODES).astype(F32).astype(BF)
    high_wide = mm(high, spread, D00)
    low_wide = mm(low, spread, D00)
    same = iota((nodes, width), 0) % GROUP_NODES == iota((nodes, width), 1) % GROUP_NODES
    base_ref[...] = jnp.where(same, high_wide, -1.0).astype(BF)
    low_ref[...] = jnp.where(same, low_wide, 0.0)
    low_iota = iota((LO, width), 0).astype(F32).astype(BF)
    one = jnp.ones((), BF)
    zero = jnp.zeros((), BF)

    def chunk(start, groups):
        outs = []
        for g in range(groups):
            r = start + g * GROUP_NODES
            base = base_ref[pl.ds(r, GROUP_NODES), :]
            low_row = jnp.sum(low_ref[pl.ds(r, GROUP_NODES), :], axis=0, keepdims=True).astype(BF)
            right = jnp.where(low_row == low_iota, one, zero)
            left = jnp.concatenate(
                [jnp.where(base == jnp.asarray(h, BF), one, zero) for h in range(loc_blocks + bnd_blocks)], axis=0
            )
            outs.append(mm(left, right, D11))
        for h in range(loc_blocks + bnd_blocks):
            rows = jnp.concatenate([o[h * GROUP_NODES : (h + 1) * GROUP_NODES] for o in outs], axis=0).astype(F8)
            where = pl.ds(start, groups * GROUP_NODES)
            if h < loc_blocks:
                loc_ref[where, h * LO : (h + 1) * LO] = rows
            else:
                b = h - loc_blocks
                bnd_ref[where, b * LO : (b + 1) * LO] = rows

    step = 2 * GROUP_NODES
    if loc_blocks + bnd_blocks <= 32:
        for s in range(nodes // step):
            chunk(s * step, 2)
    else:

        def body(s, carry):
            chunk(pl.multiple_of(s * step, step), 2)
            return carry

        lax.fori_loop(0, nodes // step, body, 0)


def build(me, ids, counts, layer, total, own):
    slots, node_total = ids.shape[1:]
    bnd_total = total * own
    nodes = BUILD_NODES if total <= 32 else 64
    nodes = max(nodes, 128)
    width = slots * GROUP_NODES
    return pl.pallas_call(
        functools.partial(build_kernel, layer=layer, bits=total.bit_length() - 1, own=own),
        grid=(node_total // nodes,),
        in_specs=[
            pl.BlockSpec(memory_space=pltpu.SMEM),
            pl.BlockSpec((1, slots, nodes), lambda i: (layer, 0, i)),
            pl.BlockSpec((counts.shape[0], nodes), lambda i: (0, i)),
        ],
        out_specs=[
            pl.BlockSpec((nodes, node_total), lambda i: (i, 0)),
            pl.BlockSpec((nodes, bnd_total), lambda i: (i, 0)),
        ],
        out_shape=[
            jax.ShapeDtypeStruct((node_total, node_total), F8),
            jax.ShapeDtypeStruct((node_total, bnd_total), F8),
        ],
        scratch_shapes=[pltpu.VMEM((nodes, width), BF), pltpu.VMEM((nodes, width), F32)],
        compiler_params=params(),
        cost_estimate=pl.CostEstimate(
            flops=2 * node_total * (node_total + bnd_total) * 256,
            bytes_accessed=node_total * (node_total + bnd_total),
            transcendentals=0,
        ),
        name="build_counts",
    )(me, ids, counts)


def local_kernel(a_ref, table_ref, out_ref):
    out_ref[...] = mm(a_ref[...].astype(BF), table_ref[...], D10)


def local_sum(a_loc, table):
    node_total, feat = table.shape
    return pl.pallas_call(
        local_kernel,
        grid=(node_total // FWD_NODES,),
        in_specs=[
            pl.BlockSpec((FWD_NODES, node_total), lambda i: (i, 0)),
            whole((node_total, feat)),
        ],
        out_specs=pl.BlockSpec((FWD_NODES, feat), lambda i: (i, 0)),
        out_shape=jax.ShapeDtypeStruct((node_total, feat), F32),
        compiler_params=params(),
        cost_estimate=pl.CostEstimate(
            flops=2 * node_total * node_total * 256, bytes_accessed=node_total * node_total, transcendentals=0
        ),
        name="local_sum",
    )(a_loc, table)


def columns(rows, width):
    nodes = rows[0].shape[1]
    pick = iota((16, nodes), 0)
    stacked = jnp.zeros((16, nodes), F32)
    for r, row in enumerate(rows):
        stacked = jnp.where(pick == r, row.astype(F32), stacked)
    stacked = stacked.astype(BF)
    outs = []
    for r in range(len(rows)):
        take = (iota((16, width), 0) == r).astype(F32).astype(BF)
        outs.append(mm(stacked, take, D00))
    return outs


def normalise(pre):
    centre = pre - jnp.mean(pre, axis=1, keepdims=True)
    inv = lax.rsqrt(jnp.mean(centre * centre, axis=1, keepdims=True) + NORM_EPS)
    return centre * inv, inv


def row_hot(brow, start, nodes):
    return (iota((nodes, brow.shape[1]), 0) + start == brow).astype(F32).astype(BF)


def forward_block(a_ref, shared_ref, part_ref, hid_ref, cnt_ref, self_ref, neigh_ref, norm_ref, layer):
    feat = hid_ref.shape[1]
    (count,) = columns([cnt_ref[layer : layer + 1, :]], feat)
    total = part_ref[...] + mm(a_ref[...].astype(BF), shared_ref[...], D10)
    agg = (total / count).astype(BF)
    pre = mm(hid_ref[...], self_ref[...], D11) + mm(agg, neigh_ref[...], D11)
    unit, inv = normalise(pre)
    y = unit * norm_ref[layer, 0:1, :] + norm_ref[layer, 1:2, :]
    return agg, pre, unit, inv, y, count


def layer_kernel(
    a_ref, shared_ref, part_ref, hid_ref, cnt_ref, self_ref, neigh_ref, norm_ref, brow_ref,
    next_ref, agg_ref, pre_ref, pub_ref, acc_ref, *, layer
):
    step = pl.program_id(0)
    agg, pre, _, _, y, _ = forward_block(
        a_ref, shared_ref, part_ref, hid_ref, cnt_ref, self_ref, neigh_ref, norm_ref, layer
    )
    nodes = hid_ref.shape[0]
    agg_ref[...] = agg
    pre_ref[...] = pre
    new = (y * jax.nn.sigmoid(y)).astype(BF)
    next_ref[...] = new
    hot = row_hot(brow_ref[layer + 1 : layer + 2, :], step * nodes, nodes)

    @pl.when(step == 0)
    def _():
        acc_ref[...] = jnp.zeros_like(acc_ref)

    acc_ref[...] += mm(hot, new, D00)

    @pl.when(step == pl.num_programs(0) - 1)
    def _():
        pub_ref[...] = acc_ref[...].astype(BF)


def forward_specs(node_total, bnd_total, feat, hid, depth, own):
    return [
        pl.BlockSpec((FWD_NODES, bnd_total), lambda i: (i, 0)),
        whole((bnd_total, feat)),
        pl.BlockSpec((FWD_NODES, feat), lambda i: (i, 0)),
        pl.BlockSpec((FWD_NODES, feat), lambda i: (i, 0)),
        pl.BlockSpec((depth, FWD_NODES), lambda i: (0, i)),
        whole((hid, feat)),
        whole((hid, feat)),
        whole((depth, 2, hid)),
    ]


def rows_spec(width):
    return pl.BlockSpec((FWD_NODES, width), lambda i: (i, 0))


def layer_forward(layer, a_bnd, shared, part, hidden, counts, w_self, w_neigh, norms, boundary):
    node_total, feat = hidden.shape
    bnd_total = shared.shape[0]
    hid = w_self.shape[0]
    depth, own = boundary.shape
    return pl.pallas_call(
        functools.partial(layer_kernel, layer=layer),
        grid=(node_total // FWD_NODES,),
        in_specs=forward_specs(node_total, bnd_total, feat, hid, depth, own) + [whole((depth, own))],
        out_specs=[rows_spec(hid), rows_spec(feat), rows_spec(hid), whole((own, hid))],
        out_shape=[
            jax.ShapeDtypeStruct((node_total, hid), BF),
            jax.ShapeDtypeStruct((node_total, feat), BF),
            jax.ShapeDtypeStruct((node_total, hid), F32),
            jax.ShapeDtypeStruct((own, hid), BF),
        ],
        scratch_shapes=[pltpu.VMEM((own, hid), F32)],
        compiler_params=params(),
        cost_estimate=pl.CostEstimate(
            flops=2 * node_total * (bnd_total + 1024) * 256,
            bytes_accessed=node_total * (bnd_total + 4096),
            transcendentals=0,
        ),
        name="layer_step",
    )(a_bnd, shared, part, hidden, counts, w_self, w_neigh, norms, boundary)


def backward_block(d_hidden, unit, inv, y, gain):
    sig = jax.nn.sigmoid(y)
    d_out = d_hidden * sig * (1.0 + y * (1.0 - sig))
    d_gain = jnp.sum(d_out * unit, axis=0, keepdims=True)
    d_shift = jnp.sum(d_out, axis=0, keepdims=True)
    d_unit = d_out * gain
    d_pre = inv * (
        d_unit
        - jnp.mean(d_unit, axis=1, keepdims=True)
        - unit * jnp.mean(d_unit * unit, axis=1, keepdims=True)
    )
    return d_pre.astype(BF), d_gain, d_shift


def add_weight_sums(dw_ref, dnorm_ref, d_pre, perm, hidden, agg, d_gain, d_shift, step):
    @pl.when(step == 0)
    def _():
        dw_ref[...] = jnp.zeros_like(dw_ref)
        dnorm_ref[...] = jnp.zeros_like(dnorm_ref)

    feat = hidden.shape[1]
    offset = dw_ref.shape[1] // 2
    moved = mm(d_pre, perm, D10).astype(BF)
    dw_ref[:, 0:feat] += mm(moved, hidden, D00)
    dw_ref[:, offset : offset + feat] += mm(moved, agg, D00)
    dnorm_ref[0:1, :] += d_gain
    dnorm_ref[1:2, :] += d_shift


def top_kernel(
    lc_ref, a_ref, shared_ref, part_ref, hid_ref, cnt_ref, self_ref, neigh_ref, norm_ref,
    lab_ref, mask_ref, head_ref, bias_ref, perm_ref,
    ds_ref, da_ref, dw_ref, dnorm_ref, dhead_ref, dbias_ref, loss_ref, *, layer
):
    step = pl.program_id(0)
    agg, _, unit, inv, y, count = forward_block(
        a_ref, shared_ref, part_ref, hid_ref, cnt_ref, self_ref, neigh_ref, norm_ref, layer
    )
    classes = head_ref.shape[1]
    top = (y * jax.nn.sigmoid(y)).astype(BF)
    logits = mm(top, head_ref[...], D10) + bias_ref[...]
    label, live = columns([lab_ref[...], mask_ref[...]], classes)
    peak = jnp.max(logits, axis=1, keepdims=True)
    log_total = peak + jnp.log(jnp.sum(jnp.exp(logits - peak), axis=1, keepdims=True))
    hot = label == iota(label.shape, 1).astype(F32)
    part_loss = jnp.sum(jnp.where(hot, live * (log_total - logits), 0.0), axis=0, keepdims=True)
    probs = jnp.exp(logits - log_total)
    d_logits = ((probs - hot.astype(F32)) * live / lc_ref[0]).astype(BF)
    perm = perm_ref[...]
    moved_top = mm(top, perm, D10).astype(BF)

    @pl.when(step == 0)
    def _():
        dhead_ref[...] = jnp.zeros_like(dhead_ref)
        dbias_ref[...] = jnp.zeros_like(dbias_ref)
        loss_ref[...] = jnp.zeros_like(loss_ref)

    loss_ref[...] += part_loss
    dbias_ref[...] += jnp.sum(d_logits.astype(F32), axis=0, keepdims=True)
    dhead_ref[...] += mm(moved_top, d_logits, D00)
    d_hidden = mm(d_logits, head_ref[...], D11)
    d_pre, d_gain, d_shift = backward_block(d_hidden, unit, inv, y, norm_ref[layer, 0:1, :])
    add_weight_sums(dw_ref, dnorm_ref, d_pre, perm, hid_ref[...], agg, d_gain, d_shift, step)
    ds_ref[...] = mm(d_pre, self_ref[...], D10)
    da_ref[...] = (mm(d_pre, neigh_ref[...], D10) / count).astype(BF)


def top_layer(layer, label_count, a_bnd, shared, part, hidden, counts, w_self, w_neigh, norms, labels, live, head, bias, perm):
    node_total, feat = hidden.shape
    bnd_total = shared.shape[0]
    hid = w_self.shape[0]
    depth = norms.shape[0]
    classes = head.shape[1]
    row = pl.BlockSpec((1, FWD_NODES), lambda i: (0, i))
    return pl.pallas_call(
        functools.partial(top_kernel, layer=layer),
        grid=(node_total // FWD_NODES,),
        in_specs=[pl.BlockSpec(memory_space=pltpu.SMEM)]
        + forward_specs(node_total, bnd_total, feat, hid, depth, 0)
        + [row, row, whole((hid, classes)), whole((1, classes)), whole((hid, hid))],
        out_specs=[
            rows_spec(feat),
            rows_spec(feat),
            whole((hid, 2 * hid)),
            whole((2, hid)),
            whole((hid, classes)),
            whole((1, classes)),
            whole((1, classes)),
        ],
        out_shape=[
            jax.ShapeDtypeStruct((node_total, feat), F32),
            jax.ShapeDtypeStruct((node_total, feat), BF),
            jax.ShapeDtypeStruct((hid, 2 * hid), F32),
            jax.ShapeDtypeStruct((2, hid), F32),
            jax.ShapeDtypeStruct((hid, classes), F32),
            jax.ShapeDtypeStruct((1, classes), F32),
            jax.ShapeDtypeStruct((1, classes), F32),
        ],
        compiler_params=params(),
        cost_estimate=pl.CostEstimate(
            flops=2 * node_total * (bnd_total + 3072) * 256,
            bytes_accessed=node_total * (bnd_total + 4096),
            transcendentals=0,
        ),
        name="top_step",
    )(label_count, a_bnd, shared, part, hidden, counts, w_self, w_neigh, norms, labels, live, head, bias, perm)


def lower_kernel(
    dh_ref, dshared_ref, brow_ref, pre_ref, hid_ref, agg_ref, cnt_ref, norm_ref, perm_ref, self_ref, neigh_ref,
    *outs, layer
):
    step = pl.program_id(0)
    nodes = dh_ref.shape[0]
    hot = row_hot(brow_ref[layer + 1 : layer + 2, :], step * nodes, nodes)
    shared = dshared_ref[...]
    shared_top = shared.astype(BF)
    shared_rest = (shared - shared_top.astype(F32)).astype(BF)
    d_hidden = dh_ref[...] + mm(hot, shared_top, D10) + mm(hot, shared_rest, D10)
    unit, inv = normalise(pre_ref[...])
    gain = norm_ref[layer, 0:1, :]
    y = unit * gain + norm_ref[layer, 1:2, :]
    d_pre, d_gain, d_shift = backward_block(d_hidden, unit, inv, y, gain)
    dw_ref, dnorm_ref = outs[0], outs[1]
    add_weight_sums(dw_ref, dnorm_ref, d_pre, perm_ref[...], hid_ref[...], agg_ref[...], d_gain, d_shift, step)
    if len(outs) > 2:
        (count,) = columns([cnt_ref[layer : layer + 1, :]], hid_ref.shape[1])
        outs[2][...] = mm(d_pre, self_ref[...], D10)
        outs[3][...] = (mm(d_pre, neigh_ref[...], D10) / count).astype(BF)


def layer_backward(layer, d_hidden, d_shared, boundary, pre, hidden, agg, counts, norms, perm, w_self, w_neigh):
    node_total, hid = d_hidden.shape
    feat = hidden.shape[1]
    depth, own = boundary.shape
    wide = 2 * (-(-feat // 128) * 128)
    out_specs = [whole((hid, wide)), whole((2, hid))]
    out_shape = [jax.ShapeDtypeStruct((hid, wide), F32), jax.ShapeDtypeStruct((2, hid), F32)]
    if layer:
        out_specs += [rows_spec(feat), rows_spec(feat)]
        out_shape += [
            jax.ShapeDtypeStruct((node_total, feat), F32),
            jax.ShapeDtypeStruct((node_total, feat), BF),
        ]
    return pl.pallas_call(
        functools.partial(lower_kernel, layer=layer),
        grid=(node_total // FWD_NODES,),
        in_specs=[
            rows_spec(hid),
            whole((own, hid)),
            whole((depth, own)),
            rows_spec(hid),
            rows_spec(feat),
            rows_spec(feat),
            pl.BlockSpec((depth, FWD_NODES), lambda i: (0, i)),
            whole((depth, 2, hid)),
            whole((hid, hid)),
            whole((hid, feat)),
            whole((hid, feat)),
        ],
        out_specs=out_specs,
        out_shape=out_shape,
        compiler_params=params(),
        cost_estimate=pl.CostEstimate(
            flops=2 * node_total * 2048 * 256, bytes_accessed=node_total * 6144, transcendentals=0
        ),
        name="lower_step",
    )(d_hidden, d_shared, boundary, pre, hidden, agg, counts, norms, perm, w_self, w_neigh)


def spread_kernel(a_ref, d_ref, *refs):
    total = mm(a_ref[...].astype(BF), d_ref[...], D00)
    if len(refs) > 1:
        total = total + refs[0][...]
    refs[-1][...] = total.astype(refs[-1].dtype)


def spread(a, d_rows, extra, kind, name):
    node_total, cols = a.shape
    feat = d_rows.shape[1]
    block = pl.BlockSpec((BWD_COLS, feat), lambda i: (i, 0))
    return pl.pallas_call(
        spread_kernel,
        grid=(cols // BWD_COLS,),
        in_specs=[pl.BlockSpec((node_total, BWD_COLS), lambda i: (0, i)), whole((node_total, feat))]
        + [block] * len(extra),
        out_specs=block,
        out_shape=jax.ShapeDtypeStruct((cols, feat), kind),
        compiler_params=params(),
        cost_estimate=pl.CostEstimate(
            flops=2 * node_total * cols * 256, bytes_accessed=node_total * cols, transcendentals=0
        ),
        name=name,
    )(a, d_rows, *extra)


def factored_step(weight, gradient, row_new, col_new, row_mean):
    estimate = row_new[..., None, :] * col_new[..., :, None] / row_mean[..., None, None]
    return weight - LEARN_RATE * gradient * lax.rsqrt(estimate)


def vector_step(param, gradient, state):
    state_new = 0.5 * state + 0.5 * (gradient * gradient + SQUARE_EPS)
    return (param - VECTOR_RATE * gradient * lax.rsqrt(state_new), state_new)


def on_device(
    features,
    labels,
    train_mask,
    boundary,
    neighbours,
    counts,
    first_weight,
    rest_weight,
    head_weight,
    norm_params,
    head_bias,
    first_row,
    first_col,
    rest_row,
    rest_col,
    head_row,
    head_col,
    norm_state,
    bias_state,
    *,
    total,
):
    bits = total.bit_length() - 1
    me = lax.axis_index("dom").astype(I32)
    me_ref = me[None]
    depth = norm_params.shape[0]
    own = boundary.shape[1]
    node_total, f_in = features.shape
    hid = norm_params.shape[2]
    classes = head_bias.shape[0]
    cols_own = hid // total

    first_t = first_weight.T
    rest_t = jnp.swapaxes(rest_weight, 1, 2)
    ids = jnp.swapaxes(neighbours, 1, 2)

    label_count = sum_all(jnp.sum(train_mask.astype(F32), keepdims=True).reshape(1, 1), total).reshape(1)

    col = jnp.arange(hid, dtype=I32)
    place = reverse_bits((col // cols_own) ^ me, bits) * cols_own + col % cols_own
    perm = (place[:, None] == jnp.arange(hid, dtype=I32)[None, :]).astype(BF)

    packed = jnp.concatenate(
        [first_t.astype(BF)] + [rest_t[k].astype(BF) for k in range(depth - 1)] + [head_weight.astype(BF)], axis=1
    )
    packed = mm(perm, gather_rows(packed, total), D10).astype(BF)
    first_full = packed[:, : 2 * f_in]
    at = 2 * f_in
    weights = [(first_full[:, :f_in], first_full[:, f_in:])]
    for _ in range(depth - 1):
        weights.append((packed[:, at : at + hid], packed[:, at + hid : at + 2 * hid]))
        at += 2 * hid
    head = packed[:, at:]

    hidden = features.astype(BF)
    published = hidden[boundary[0]]
    saved = []
    for layer in range(depth):
        shared = gather_rows(published, total)
        a_loc, a_bnd = build(me_ref, ids, counts, layer, total, own)
        part = local_sum(a_loc, hidden)
        w_self, w_neigh = weights[layer]
        if layer < depth - 1:
            new, agg, pre, published = layer_forward(
                layer, a_bnd, shared, part, hidden, counts, w_self, w_neigh, norm_params, boundary
            )
            saved.append((a_loc, a_bnd, hidden, agg, pre))
            hidden = new
    ds, da, dw, dnorm, dhead, dbias, loss = top_layer(
        depth - 1, label_count, a_bnd, shared, part, hidden, counts, w_self, w_neigh, norm_params,
        labels[None], train_mask[None], head, head_bias[None], perm,
    )
    d_weights = [None] * depth
    d_norms = [None] * depth
    d_weights[-1], d_norms[-1] = dw, dnorm
    for layer in reversed(range(depth - 1)):
        d_far = spread(a_bnd, da, (), BF, "spread_far")
        d_near = spread(a_loc, da, (ds,), F32, "spread_near")
        d_shared = scatter_rows(d_far, total).astype(F32)
        a_loc, a_bnd, hidden, agg, pre = saved[layer]
        w_self, w_neigh = weights[layer]
        outs = layer_backward(
            layer, d_near, d_shared, boundary, pre, hidden, agg, counts, norm_params, perm, w_self, w_neigh
        )
        d_weights[layer], d_norms[layer] = outs[0], outs[1]
        if layer:
            ds, da = outs[2:]

    g_head = scatter_rows(dhead, total)
    g_rest = jnp.stack([scatter_rows(d_weights[k], total) for k in range(1, depth)])
    g_wide = scatter_rows(d_weights[0], total)
    half = g_wide.shape[1] // 2
    g_first = jnp.concatenate([g_wide[:, :f_in], g_wide[:, half : half + f_in]], axis=1)

    sq_first = g_first * g_first + SQUARE_EPS
    sq_rest = g_rest * g_rest + SQUARE_EPS
    sq_head = g_head * g_head + SQUARE_EPS
    head_row_new = 0.5 * head_row + 0.5 * jnp.mean(sq_head, axis=1)
    pieces = [
        jnp.stack(d_norms).reshape(-1),
        dbias.reshape(-1),
        jnp.sum(sq_first, axis=0),
        jnp.sum(sq_rest, axis=1).reshape(-1),
        jnp.sum(sq_head, axis=0),
        jnp.sum(head_row_new, keepdims=True),
        jnp.sum(loss, keepdims=True).reshape(1),
    ]
    sums = sum_all(jnp.concatenate(pieces), total)
    parts = []
    at = 0
    for piece in pieces:
        parts.append(sums[at : at + piece.shape[0]])
        at += piece.shape[0]
    g_norms = parts[0].reshape(norm_params.shape)
    g_bias = parts[1]
    first_sums = parts[2]
    rest_sums = parts[3].reshape(rest_row.shape)
    head_sums = parts[4]
    head_row_mean = parts[5][0] / hid
    loss_sum = parts[6][0]

    first_row_new = 0.5 * first_row + 0.5 * first_sums / hid
    first_col_new = 0.5 * first_col + 0.5 * jnp.mean(sq_first, axis=1)
    rest_row_new = 0.5 * rest_row + 0.5 * rest_sums / hid
    rest_col_new = 0.5 * rest_col + 0.5 * jnp.mean(sq_rest, axis=2)
    head_col_new = 0.5 * head_col + 0.5 * head_sums / hid
    first_new = factored_step(first_t, g_first, first_row_new, first_col_new, jnp.mean(first_row_new))
    rest_new = factored_step(rest_t, g_rest, rest_row_new, rest_col_new, jnp.mean(rest_row_new, axis=1))
    head_new = head_weight - LEARN_RATE * g_head * lax.rsqrt(
        head_row_new[:, None] * head_col_new[None, :] / head_row_mean
    )
    norm_new, norm_state_new = vector_step(norm_params, g_norms, norm_state)
    bias_new, bias_state_new = vector_step(head_bias, g_bias, bias_state)
    first_new = first_new.T
    rest_new = jnp.swapaxes(rest_new, 1, 2)
    return (
        loss_sum,
        label_count[0],
        first_new,
        rest_new,
        head_new,
        norm_new,
        bias_new,
        g_first.T,
        jnp.swapaxes(g_rest, 1, 2),
        g_head,
        g_norms,
        g_bias,
        first_row_new,
        first_col_new,
        rest_row_new,
        rest_col_new,
        head_row_new,
        head_col_new,
        norm_state_new,
        bias_state_new,
        first_new.astype(BF),
        rest_new.astype(BF),
        head_new.astype(BF),
        norm_new.astype(BF),
    )


def solution(mesh):
    placed = (
        P("dom", None),
        P("dom"),
        P("dom"),
        P(None, "dom"),
        P(None, "dom", None),
        P(None, "dom"),
        P(None, "dom"),
        P(None, None, "dom"),
        P("dom", None),
        P(),
        P(),
        P(),
        P("dom"),
        P(),
        P(None, "dom"),
        P("dom"),
        P(),
        P(),
        P(),
    )
    return jax.shard_map(
        functools.partial(on_device, total=mesh.shape["dom"]),
        mesh=mesh,
        in_specs=placed,
        out_specs=(
            P(),
            P(),
            P(None, "dom"),
            P(None, None, "dom"),
            P("dom", None),
            P(),
            P(),
            P(None, "dom"),
            P(None, None, "dom"),
            P("dom", None),
            P(),
            P(),
            P(),
            P("dom"),
            P(),
            P(None, "dom"),
            P("dom"),
            P(),
            P(),
            P(),
            P(None, "dom"),
            P(None, None, "dom"),
            P("dom", None),
            P(),
        ),
        check_vma=False,
    )
```

```python
import functools

import jax
import jax.numpy as jnp
from jax import lax
from jax.experimental import pallas as pl
from jax.experimental.pallas import tpu as pltpu
from jax.sharding import PartitionSpec as P

LEARN_RATE = 0.03
VECTOR_RATE = 0.25
SQUARE_EPS = 1e-30
NORM_EPS = 1e-05

BF = jnp.bfloat16
F32 = jnp.float32
F8 = jnp.float8_e4m3fn
I32 = jnp.int32

D00 = (((0,), (0,)), ((), ()))
D11 = (((1,), (1,)), ((), ()))
D10 = (((1,), (0,)), ((), ()))

LO = 256
BUILD_NODES = 256
GROUP_NODES = 16
FWD_NODES = 512
BWD_COLS = 1024


def mm(left, right, dims):
    return lax.dot_general(left, right, dims, preferred_element_type=F32)


def iota(shape, dim):
    return lax.broadcasted_iota(I32, shape, dim)


def params():
    return pltpu.CompilerParams(vmem_limit_bytes=56 << 20)


def whole(shape):
    return pl.BlockSpec(shape, lambda i: (0,) * len(shape))


def hop(value, mask, total):
    return lax.ppermute(value, "dom", [(i, i ^ mask) for i in range(total)])


def bit_groups(total):
    bits = total.bit_length() - 1
    groups = [(0, 2)]
    at = 1
    while at < bits:
        wide = min(2, bits - at)
        groups.append((at, 1 << wide))
        at += wide
    return groups[::-1]


def place(relative, total):
    out, scale = 0, 1
    for low, size in bit_groups(total):
        out = out + ((relative >> low) & (size - 1)) * scale
        scale *= size
    return out


def after(value, *others):
    return lax.optimization_barrier((value, *others))[0]


def gather_rows(rows, total, works):
    groups = bit_groups(total)
    works = [None] * (len(groups) - len(works)) + list(works)
    for i, (low, size) in enumerate(groups):
        got = [hop(rows, d << low, total) for d in range(1, size)]
        done = works[i](rows) if works[i] else rows
        if i == len(groups) - 1:
            return rows, got[0]
        rows = after(jnp.concatenate([rows] + got, axis=0), done)


def exchange_sum(parts, low, total):
    return [parts[0]] + [hop(part, d << low, total) for d, part in enumerate(parts) if d]


def add_up(parts):
    out = parts[0].astype(F32)
    for part in parts[1:]:
        out = out + part.astype(F32)
    return out.astype(parts[0].dtype)


def scatter_rows(rows, total, groups=None):
    for low, size in groups if groups is not None else bit_groups(total)[::-1]:
        step = rows.shape[0] // size
        rows = add_up(exchange_sum([rows[d * step : (d + 1) * step] for d in range(size)], low, total))
    return rows


def sum_all(value, total):
    mask = 1
    while mask < total:
        value = value + hop(value, mask, total)
        mask *= 2
    return value


def build_kernel(me_ref, ids_ref, cnt_ref, out_ref, base_ref, low_ref, *, layer, total, own, far):
    slots, nodes = ids_ref.shape[1:]
    blocks = out_ref.shape[1] // LO
    ids = ids_ref[0]
    count = cnt_ref[layer : layer + 1, :]
    if far:
        node_total = pl.num_programs(0) * nodes
        table = ids - node_total
        moved = place((table // own) ^ me_ref[0], total) * own + table % own
        ids = jnp.where(table < 0, -1, moved)
    ids = jnp.where(iota((slots, nodes), 0) < count, ids, -1)
    high = (ids >> 8).astype(F32).astype(BF)
    low = (ids & 255).astype(F32).astype(BF)
    width = slots * GROUP_NODES
    spread = (iota((slots, width), 0) == iota((slots, width), 1) // GROUP_NODES).astype(F32).astype(BF)
    high_wide = mm(high, spread, D00)
    low_wide = mm(low, spread, D00)
    same = iota((nodes, width), 0) % GROUP_NODES == iota((nodes, width), 1) % GROUP_NODES
    base_ref[...] = jnp.where(same, high_wide, -1.0).astype(BF)
    low_ref[...] = jnp.where(same, low_wide, 0.0)
    low_iota = iota((LO, width), 0).astype(F32).astype(BF)
    one = jnp.ones((), BF)
    zero = jnp.zeros((), BF)

    def chunk(start, groups):
        outs = []
        for g in range(groups):
            r = start + g * GROUP_NODES
            base = base_ref[pl.ds(r, GROUP_NODES), :]
            low_row = jnp.sum(low_ref[pl.ds(r, GROUP_NODES), :], axis=0, keepdims=True).astype(BF)
            right = jnp.where(low_row == low_iota, one, zero)
            left = jnp.concatenate([jnp.where(base == jnp.asarray(h, BF), one, zero) for h in range(blocks)], axis=0)
            outs.append(mm(left, right, D11))
        for h in range(blocks):
            rows = jnp.concatenate([o[h * GROUP_NODES : (h + 1) * GROUP_NODES] for o in outs], axis=0).astype(F8)
            out_ref[pl.ds(start, groups * GROUP_NODES), h * LO : (h + 1) * LO] = rows

    step = 2 * GROUP_NODES
    if blocks <= 32:
        for s in range(nodes // step):
            chunk(s * step, 2)
    else:

        def body(s, carry):
            chunk(pl.multiple_of(s * step, step), 2)
            return carry

        lax.fori_loop(0, nodes // step, body, 0)


def build(me, ids, counts, layer, total, own, far):
    slots, node_total = ids.shape[1:]
    cols = total * own if far else node_total
    nodes = BUILD_NODES if cols <= 8192 else 128
    width = slots * GROUP_NODES
    return pl.pallas_call(
        functools.partial(build_kernel, layer=layer, total=total, own=own, far=far),
        grid=(node_total // nodes,),
        in_specs=[
            pl.BlockSpec(memory_space=pltpu.SMEM),
            pl.BlockSpec((1, slots, nodes), lambda i: (layer, 0, i)),
            pl.BlockSpec((counts.shape[0], nodes), lambda i: (0, i)),
        ],
        out_specs=pl.BlockSpec((nodes, cols), lambda i: (i, 0)),
        out_shape=jax.ShapeDtypeStruct((node_total, cols), F8),
        scratch_shapes=[pltpu.VMEM((nodes, width), BF), pltpu.VMEM((nodes, width), F32)],
        compiler_params=params(),
        cost_estimate=pl.CostEstimate(
            flops=2 * node_total * cols * 256, bytes_accessed=node_total * cols, transcendentals=0
        ),
        name="build_far" if far else "build_near",
    )(me, ids, counts)


def local_kernel(a_ref, table_ref, out_ref):
    out_ref[...] = mm(a_ref[...].astype(BF), table_ref[...], D10)


def local_sum(a_loc, table):
    node_total, feat = table.shape
    return pl.pallas_call(
        local_kernel,
        grid=(node_total // FWD_NODES,),
        in_specs=[
            pl.BlockSpec((FWD_NODES, node_total), lambda i: (i, 0)),
            whole((node_total, feat)),
        ],
        out_specs=pl.BlockSpec((FWD_NODES, feat), lambda i: (i, 0)),
        out_shape=jax.ShapeDtypeStruct((node_total, feat), F32),
        compiler_params=params(),
        cost_estimate=pl.CostEstimate(
            flops=2 * node_total * node_total * 256, bytes_accessed=node_total * node_total, transcendentals=0
        ),
        name="local_sum",
    )(a_loc, table)


def columns(rows, width):
    nodes = rows[0].shape[1]
    pick = iota((16, nodes), 0)
    stacked = jnp.zeros((16, nodes), F32)
    for r, row in enumerate(rows):
        stacked = jnp.where(pick == r, row.astype(F32), stacked)
    stacked = stacked.astype(BF)
    outs = []
    for r in range(len(rows)):
        take = (iota((16, width), 0) == r).astype(F32).astype(BF)
        outs.append(mm(stacked, take, D00))
    return outs


def normalise(pre):
    centre = pre - jnp.mean(pre, axis=1, keepdims=True)
    inv = lax.rsqrt(jnp.mean(centre * centre, axis=1, keepdims=True) + NORM_EPS)
    return centre * inv, inv


def row_hot(brow, start, nodes):
    return (iota((nodes, brow.shape[1]), 0) + start == brow).astype(F32).astype(BF)


def forward_block(a_ref, near_ref, far_ref, part_ref, hid_ref, cnt_ref, self_ref, neigh_ref, norm_ref, layer):
    feat = hid_ref.shape[1]
    (count,) = columns([cnt_ref[layer : layer + 1, :]], feat)
    half = near_ref.shape[0]
    total = part_ref[...] + mm(a_ref[:, :half].astype(BF), near_ref[...], D10)
    total = total + mm(a_ref[:, half:].astype(BF), far_ref[...], D10)
    agg = (total / count).astype(BF)
    pre = mm(hid_ref[...], self_ref[...], D11) + mm(agg, neigh_ref[...], D11)
    unit, inv = normalise(pre)
    y = unit * norm_ref[layer, 0:1, :] + norm_ref[layer, 1:2, :]
    return agg, pre, unit, inv, y, count


def layer_kernel(
    a_ref, near_ref, far_ref, part_ref, hid_ref, cnt_ref, self_ref, neigh_ref, norm_ref, brow_ref,
    next_ref, agg_ref, pre_ref, pub_ref, acc_ref, *, layer
):
    step = pl.program_id(0)
    agg, pre, _, _, y, _ = forward_block(
        a_ref, near_ref, far_ref, part_ref, hid_ref, cnt_ref, self_ref, neigh_ref, norm_ref, layer
    )
    nodes = hid_ref.shape[0]
    agg_ref[...] = agg
    pre_ref[...] = pre
    new = (y * jax.nn.sigmoid(y)).astype(BF)
    next_ref[...] = new
    hot = row_hot(brow_ref[layer + 1 : layer + 2, :], step * nodes, nodes)

    @pl.when(step == 0)
    def _():
        acc_ref[...] = jnp.zeros_like(acc_ref)

    acc_ref[...] += mm(hot, new, D00)

    @pl.when(step == pl.num_programs(0) - 1)
    def _():
        pub_ref[...] = acc_ref[...].astype(BF)


def forward_specs(node_total, bnd_total, feat, hid, depth, own):
    return [
        pl.BlockSpec((FWD_NODES, bnd_total), lambda i: (i, 0)),
        whole((bnd_total // 2, feat)),
        whole((bnd_total // 2, feat)),
        pl.BlockSpec((FWD_NODES, feat), lambda i: (i, 0)),
        pl.BlockSpec((FWD_NODES, feat), lambda i: (i, 0)),
        pl.BlockSpec((depth, FWD_NODES), lambda i: (0, i)),
        whole((hid, feat)),
        whole((hid, feat)),
        whole((depth, 2, hid)),
    ]


def rows_spec(width):
    return pl.BlockSpec((FWD_NODES, width), lambda i: (i, 0))


def layer_forward(layer, a_bnd, shared, part, hidden, counts, w_self, w_neigh, norms, boundary):
    node_total, feat = hidden.shape
    bnd_total = a_bnd.shape[1]
    hid = w_self.shape[0]
    depth, own = boundary.shape
    return pl.pallas_call(
        functools.partial(layer_kernel, layer=layer),
        grid=(node_total // FWD_NODES,),
        in_specs=forward_specs(node_total, bnd_total, feat, hid, depth, own) + [whole((depth, own))],
        out_specs=[rows_spec(hid), rows_spec(feat), rows_spec(hid), whole((own, hid))],
        out_shape=[
            jax.ShapeDtypeStruct((node_total, hid), BF),
            jax.ShapeDtypeStruct((node_total, feat), BF),
            jax.ShapeDtypeStruct((node_total, hid), F32),
            jax.ShapeDtypeStruct((own, hid), BF),
        ],
        scratch_shapes=[pltpu.VMEM((own, hid), F32)],
        compiler_params=params(),
        cost_estimate=pl.CostEstimate(
            flops=2 * node_total * (bnd_total + 1024) * 256,
            bytes_accessed=node_total * (bnd_total + 4096),
            transcendentals=0,
        ),
        name="layer_step",
    )(a_bnd, *shared, part, hidden, counts, w_self, w_neigh, norms, boundary)


def backward_block(d_hidden, unit, inv, y, gain):
    sig = jax.nn.sigmoid(y)
    d_out = d_hidden * sig * (1.0 + y * (1.0 - sig))
    d_gain = jnp.sum(d_out * unit, axis=0, keepdims=True)
    d_shift = jnp.sum(d_out, axis=0, keepdims=True)
    d_unit = d_out * gain
    d_pre = inv * (
        d_unit
        - jnp.mean(d_unit, axis=1, keepdims=True)
        - unit * jnp.mean(d_unit * unit, axis=1, keepdims=True)
    )
    return d_pre.astype(BF), d_gain, d_shift


def add_weight_sums(dw_ref, dnorm_ref, d_pre, hidden, agg, d_gain, d_shift, step):
    @pl.when(step == 0)
    def _():
        dw_ref[...] = jnp.zeros_like(dw_ref)
        dnorm_ref[...] = jnp.zeros_like(dnorm_ref)

    feat = hidden.shape[1]
    dw_ref[:, 0:feat] += mm(d_pre, hidden, D00)
    dw_ref[:, feat : 2 * feat] += mm(d_pre, agg, D00)
    dnorm_ref[0:1, :] += d_gain
    dnorm_ref[1:2, :] += d_shift


def into_places(dw_ref, perm_ref):
    @pl.when(pl.program_id(0) == pl.num_programs(0) - 1)
    def _():
        perm = perm_ref[...]
        rest = dw_ref[...]
        moved = jnp.zeros_like(rest)
        for _ in range(3):
            term = rest.astype(BF)
            moved = moved + mm(perm, term, D00)
            rest = rest - term.astype(F32)
        dw_ref[...] = moved


def top_kernel(
    lc_ref, a_ref, near_ref, far_ref, part_ref, hid_ref, cnt_ref, self_ref, neigh_ref, norm_ref,
    lab_ref, mask_ref, head_ref, bias_ref, perm_ref,
    ds_ref, da_ref, dw_ref, dnorm_ref, dbias_ref, loss_ref, *, layer
):
    step = pl.program_id(0)
    agg, _, unit, inv, y, count = forward_block(
        a_ref, near_ref, far_ref, part_ref, hid_ref, cnt_ref, self_ref, neigh_ref, norm_ref, layer
    )
    classes = head_ref.shape[1]
    top = (y * jax.nn.sigmoid(y)).astype(BF)
    logits = mm(top, head_ref[...], D10) + bias_ref[...]
    label, live = columns([lab_ref[...], mask_ref[...]], classes)
    peak = jnp.max(logits, axis=1, keepdims=True)
    log_total = peak + jnp.log(jnp.sum(jnp.exp(logits - peak), axis=1, keepdims=True))
    hot = label == iota(label.shape, 1).astype(F32)
    part_loss = jnp.sum(jnp.where(hot, live * (log_total - logits), 0.0), axis=0, keepdims=True)
    probs = jnp.exp(logits - log_total)
    d_logits = ((probs - hot.astype(F32)) * live / lc_ref[0]).astype(BF)
    @pl.when(step == 0)
    def _():
        dbias_ref[...] = jnp.zeros_like(dbias_ref)
        loss_ref[...] = jnp.zeros_like(loss_ref)

    loss_ref[...] += part_loss
    dbias_ref[...] += jnp.sum(d_logits.astype(F32), axis=0, keepdims=True)
    d_hidden = mm(d_logits, head_ref[...], D11)
    d_pre, d_gain, d_shift = backward_block(d_hidden, unit, inv, y, norm_ref[layer, 0:1, :])
    add_weight_sums(dw_ref, dnorm_ref, d_pre, hid_ref[...], agg, d_gain, d_shift, step)
    feat = hid_ref.shape[1]
    dw_ref[:, 2 * feat : 2 * feat + classes] += mm(top, d_logits, D00)
    into_places(dw_ref, perm_ref)
    ds_ref[...] = mm(d_pre, self_ref[...], D10)
    da_ref[...] = (mm(d_pre, neigh_ref[...], D10) / count).astype(BF)


def top_layer(layer, label_count, a_bnd, shared, part, hidden, counts, w_self, w_neigh, norms, labels, live, head, bias, perm):
    node_total, feat = hidden.shape
    bnd_total = a_bnd.shape[1]
    hid = w_self.shape[0]
    depth = norms.shape[0]
    classes = head.shape[1]
    row = pl.BlockSpec((1, FWD_NODES), lambda i: (0, i))
    return pl.pallas_call(
        functools.partial(top_kernel, layer=layer),
        grid=(node_total // FWD_NODES,),
        in_specs=[pl.BlockSpec(memory_space=pltpu.SMEM)]
        + forward_specs(node_total, bnd_total, feat, hid, depth, 0)
        + [row, row, whole((hid, classes)), whole((1, classes)), whole((hid, hid))],
        out_specs=[
            rows_spec(feat),
            rows_spec(feat),
            whole((hid, 2 * hid + 128)),
            whole((2, hid)),
            whole((1, classes)),
            whole((1, classes)),
        ],
        out_shape=[
            jax.ShapeDtypeStruct((node_total, feat), F32),
            jax.ShapeDtypeStruct((node_total, feat), BF),
            jax.ShapeDtypeStruct((hid, 2 * hid + 128), F32),
            jax.ShapeDtypeStruct((2, hid), F32),
            jax.ShapeDtypeStruct((1, classes), F32),
            jax.ShapeDtypeStruct((1, classes), F32),
        ],
        compiler_params=params(),
        cost_estimate=pl.CostEstimate(
            flops=2 * node_total * (bnd_total + 3072) * 256,
            bytes_accessed=node_total * (bnd_total + 4096),
            transcendentals=0,
        ),
        name="top_step",
    )(label_count, a_bnd, *shared, part, hidden, counts, w_self, w_neigh, norms, labels, live, head, bias, perm)


def lower_kernel(
    early_ref, late_ref, dshared_ref, brow_ref, pre_ref, hid_ref, agg_ref, cnt_ref, norm_ref, perm_ref, self_ref, neigh_ref,
    *outs, layer
):
    step = pl.program_id(0)
    nodes = early_ref.shape[0]
    hot = row_hot(brow_ref[layer + 1 : layer + 2, :], step * nodes, nodes)
    shared = dshared_ref[...]
    shared_top = shared.astype(BF)
    shared_rest = (shared - shared_top.astype(F32)).astype(BF)
    d_hidden = jnp.where(step < pl.num_programs(0) // 2, early_ref[...], late_ref[...])
    d_hidden = d_hidden + mm(hot, shared_top, D10) + mm(hot, shared_rest, D10)
    unit, inv = normalise(pre_ref[...])
    gain = norm_ref[layer, 0:1, :]
    y = unit * gain + norm_ref[layer, 1:2, :]
    d_pre, d_gain, d_shift = backward_block(d_hidden, unit, inv, y, gain)
    dw_ref, dnorm_ref = outs[0], outs[1]
    add_weight_sums(dw_ref, dnorm_ref, d_pre, hid_ref[...], agg_ref[...], d_gain, d_shift, step)
    into_places(dw_ref, perm_ref)
    if len(outs) > 2:
        (count,) = columns([cnt_ref[layer : layer + 1, :]], hid_ref.shape[1])
        outs[2][...] = mm(d_pre, self_ref[...], D10)
        outs[3][...] = (mm(d_pre, neigh_ref[...], D10) / count).astype(BF)


def layer_backward(layer, d_early, d_late, d_shared, boundary, pre, hidden, agg, counts, norms, perm, w_self, w_neigh):
    hid = d_early.shape[1]
    node_total, feat = hidden.shape
    half = node_total // FWD_NODES // 2
    depth, own = boundary.shape
    out_specs = [whole((hid, 2 * feat)), whole((2, hid))]
    out_shape = [jax.ShapeDtypeStruct((hid, 2 * feat), F32), jax.ShapeDtypeStruct((2, hid), F32)]
    if layer:
        out_specs += [rows_spec(feat), rows_spec(feat)]
        out_shape += [
            jax.ShapeDtypeStruct((node_total, feat), F32),
            jax.ShapeDtypeStruct((node_total, feat), BF),
        ]
    return pl.pallas_call(
        functools.partial(lower_kernel, layer=layer),
        grid=(node_total // FWD_NODES,),
        in_specs=[
            pl.BlockSpec((FWD_NODES, hid), lambda i: (jnp.minimum(i, half - 1), 0)),
            pl.BlockSpec((FWD_NODES, hid), lambda i: (jnp.maximum(i - half, 0), 0)),
            whole((own, hid)),
            whole((depth, own)),
            rows_spec(hid),
            rows_spec(feat),
            rows_spec(feat),
            pl.BlockSpec((depth, FWD_NODES), lambda i: (0, i)),
            whole((depth, 2, hid)),
            whole((hid, hid)),
            whole((hid, feat)),
            whole((hid, feat)),
        ],
        out_specs=out_specs,
        out_shape=out_shape,
        compiler_params=params(),
        cost_estimate=pl.CostEstimate(
            flops=2 * node_total * 2048 * 256, bytes_accessed=node_total * 6144, transcendentals=0
        ),
        name="lower_step",
    )(d_early, d_late, d_shared, boundary, pre, hidden, agg, counts, norms, perm, w_self, w_neigh)


def spread_kernel(a_ref, d_ref, *refs, add):
    total = mm(a_ref[...].astype(BF), d_ref[...], D00)
    if add:
        total = total + refs[0][...]
    refs[-1][...] = total.astype(refs[-1].dtype)


def spread(a, d_rows, extra, kind, first, steps):
    node_total = a.shape[0]
    feat = d_rows.shape[1]
    specs = [pl.BlockSpec((node_total, BWD_COLS), lambda i: (0, i + first)), whole((node_total, feat))]
    specs += [pl.BlockSpec((BWD_COLS, feat), lambda i: (i + first, 0))] * len(extra)
    return pl.pallas_call(
        functools.partial(spread_kernel, add=len(extra) > 0),
        grid=(steps,),
        in_specs=specs,
        out_specs=pl.BlockSpec((BWD_COLS, feat), lambda i: (i, 0)),
        out_shape=jax.ShapeDtypeStruct((steps * BWD_COLS, feat), kind),
        compiler_params=params(),
        cost_estimate=pl.CostEstimate(
            flops=2 * node_total * steps * BWD_COLS * 256,
            bytes_accessed=node_total * steps * BWD_COLS,
            transcendentals=0,
        ),
        name="spread_near" if extra else "spread_far",
    )(a, d_rows, *extra)


def lane_pad(value):
    wide = -(-value.shape[1] // 128) * 128
    return jnp.pad(value, ((0, 0), (0, wide - value.shape[1])))


def factored_step(weight, gradient, row_new, col_new, row_mean):
    estimate = row_new[..., None, :] * col_new[..., :, None] / row_mean[..., None, None]
    return weight - LEARN_RATE * gradient * lax.rsqrt(estimate)


def vector_step(param, gradient, state):
    state_new = 0.5 * state + 0.5 * (gradient * gradient + SQUARE_EPS)
    return (param - VECTOR_RATE * gradient * lax.rsqrt(state_new), state_new)


def on_device(
    features,
    labels,
    train_mask,
    boundary,
    neighbours,
    counts,
    first_weight,
    rest_weight,
    head_weight,
    norm_params,
    head_bias,
    first_row,
    first_col,
    rest_row,
    rest_col,
    head_row,
    head_col,
    norm_state,
    bias_state,
    *,
    total,
):
    me = lax.axis_index("dom").astype(I32)
    me_ref = me[None]
    depth = norm_params.shape[0]
    own = boundary.shape[1]
    node_total, f_in = features.shape
    hid = norm_params.shape[2]
    classes = head_bias.shape[0]
    cols_own = hid // total if hid >= total else 1

    first_t = first_weight.T
    rest_t = jnp.swapaxes(rest_weight, 1, 2)
    ids = jnp.swapaxes(neighbours, 1, 2)

    col = jnp.arange(hid, dtype=I32)
    position = place((col // cols_own) ^ me, total) * cols_own + col % cols_own
    perm = (position[:, None] == jnp.arange(hid, dtype=I32)[None, :]).astype(BF)

    hidden = lane_pad(features.astype(BF))
    f_wide = hidden.shape[1]
    mine = jnp.concatenate(
        [lane_pad(first_t[:, :f_in]), lane_pad(first_t[:, f_in:])]
        + [rest_t[k] for k in range(depth - 1)]
        + [lane_pad(head_weight)],
        axis=1,
    ).astype(BF)
    tiles = mine.shape[1] // 128
    mine = jnp.swapaxes(mine.reshape(cols_own, tiles, 128), 0, 1).reshape(tiles * cols_own, 128)
    labelled = jnp.sum(train_mask)
    labelled = jnp.where(jnp.arange(128) == 0, labelled // 64, jnp.where(jnp.arange(128) == 1, labelled % 64, 0))
    pad_rows = -(own + tiles * cols_own + 1) % 16
    labelled = jnp.pad(labelled.astype(BF)[None], ((0, pad_rows), (0, 0)))
    first_rows = jnp.concatenate([hidden[boundary[0]], mine, labelled], axis=0)

    tables = [None] * depth
    parts = [None] * depth

    def beside(layer, table):
        def near(wait):
            a_loc = build(after(me_ref, wait), ids, counts, layer, total, own, False)
            tables[layer] = (a_loc, None)
            return a_loc

        def far(wait):
            a_loc = tables[layer][0]
            tables[layer] = (a_loc, build(after(me_ref, wait), ids, counts, layer, total, own, True))
            return tables[layer][1]

        def sums(wait):
            parts[layer] = local_sum(tables[layer][0], after(table, wait))
            return parts[layer]

        return [near, far, sums]

    got = gather_rows(first_rows, total, beside(0, hidden))
    got = [g.reshape(total // 2, -1, 128) for g in got]
    shared = [g[:, :own].reshape(-1, 128) for g in got]
    both = jnp.concatenate([g[:, own:] for g in got], axis=0)
    packed = both[:, : tiles * cols_own].reshape(total, tiles, cols_own, 128)
    packed = jnp.swapaxes(packed, 1, 2).reshape(hid, tiles * 128)
    packed = mm(perm, packed, D10).astype(BF)
    marks = both[:, tiles * cols_own].astype(F32)
    label_count = (64.0 * jnp.sum(marks[:, 0]) + jnp.sum(marks[:, 1])).reshape(1)
    weights = []
    at = 0
    for layer in range(depth):
        wide = hid if layer else f_wide
        weights.append((packed[:, at : at + wide], packed[:, at + wide : at + 2 * wide]))
        at += 2 * wide
    head = packed[:, at : at + classes]

    saved = []
    for layer in range(depth):
        if layer:
            shared = gather_rows(published, total, beside(layer, hidden))
        a_loc, a_bnd = tables[layer]
        w_self, w_neigh = weights[layer]
        if layer < depth - 1:
            new, agg, pre, published = layer_forward(
                layer, a_bnd, shared, parts[layer], hidden, counts, w_self, w_neigh, norm_params, boundary
            )
            saved.append((a_loc, a_bnd, hidden, agg, pre))
            hidden = new
    ds, da, dw, dnorm, dbias, loss = top_layer(
        depth - 1, label_count, a_bnd, shared, parts[-1], hidden, counts, w_self, w_neigh, norm_params,
        labels[None], train_mask[None], head, head_bias[None], perm,
    )
    d_weights = [None] * depth
    d_norms = [None] * depth
    d_weights[-1], d_norms[-1] = dw, dnorm
    near_steps = node_total // BWD_COLS
    far_steps = a_bnd.shape[1] // BWD_COLS
    for layer in reversed(range(depth - 1)):
        d_far = spread(a_bnd, da, (), BF, far_steps // 2, far_steps // 2)
        arrived = hop(d_far, 1, total)
        d_keep = spread(a_bnd, after(da, d_far), (), BF, 0, far_steps // 2)
        rows = add_up([d_keep, arrived])
        d_near = []
        rounds = bit_groups(total)[::-1][1:]
        for i, (low, size) in enumerate(rounds):
            step = rows.shape[0] // size
            sums = exchange_sum([rows[d * step : (d + 1) * step] for d in range(size)], low, total)
            if i < 2:
                d_near.append(spread(a_loc, after(da, rows), (ds,), F32, i * near_steps // 2, near_steps // 2))
                sums[0] = after(sums[0], d_near[-1])
            rows = add_up(sums)
        d_shared = rows.astype(F32)
        a_loc, a_bnd, hidden, agg, pre = saved[layer]
        w_self, w_neigh = weights[layer]
        outs = layer_backward(
            layer, *d_near, d_shared, boundary, pre, hidden, agg, counts, norm_params, perm, w_self, w_neigh
        )
        d_weights[layer], d_norms[layer] = outs[0], outs[1]
        if layer:
            ds, da = outs[2:]

    g_top = scatter_rows(d_weights[-1], total)
    g_head = g_top[:, 2 * hid : 2 * hid + classes]
    g_rest = jnp.stack([scatter_rows(d_weights[k], total) for k in range(1, depth - 1)] + [g_top[:, : 2 * hid]])
    g_wide = scatter_rows(d_weights[0], total)
    g_first = jnp.concatenate([g_wide[:, :f_in], g_wide[:, f_wide : f_wide + f_in]], axis=1)

    sq_first = g_first * g_first + SQUARE_EPS
    sq_rest = g_rest * g_rest + SQUARE_EPS
    sq_head = g_head * g_head + SQUARE_EPS
    head_row_new = 0.5 * head_row + 0.5 * jnp.mean(sq_head, axis=1)
    pieces = [
        jnp.stack(d_norms).reshape(-1),
        dbias.reshape(-1),
        jnp.sum(sq_first, axis=0),
        jnp.sum(sq_rest, axis=1).reshape(-1),
        jnp.sum(sq_head, axis=0),
        jnp.sum(head_row_new, keepdims=True),
        jnp.sum(loss, keepdims=True).reshape(1),
    ]
    sums = sum_all(jnp.concatenate(pieces), total)
    parts = []
    at = 0
    for piece in pieces:
        parts.append(sums[at : at + piece.shape[0]])
        at += piece.shape[0]
    g_norms = parts[0].reshape(norm_params.shape)
    g_bias = parts[1]
    first_sums = parts[2]
    rest_sums = parts[3].reshape(rest_row.shape)
    head_sums = parts[4]
    head_row_mean = parts[5][0] / hid
    loss_sum = parts[6][0]

    first_row_new = 0.5 * first_row + 0.5 * first_sums / hid
    first_col_new = 0.5 * first_col + 0.5 * jnp.mean(sq_first, axis=1)
    rest_row_new = 0.5 * rest_row + 0.5 * rest_sums / hid
    rest_col_new = 0.5 * rest_col + 0.5 * jnp.mean(sq_rest, axis=2)
    head_col_new = 0.5 * head_col + 0.5 * head_sums / hid
    first_new = factored_step(first_t, g_first, first_row_new, first_col_new, jnp.mean(first_row_new))
    rest_new = factored_step(rest_t, g_rest, rest_row_new, rest_col_new, jnp.mean(rest_row_new, axis=1))
    head_new = head_weight - LEARN_RATE * g_head * lax.rsqrt(
        head_row_new[:, None] * head_col_new[None, :] / head_row_mean
    )
    norm_new, norm_state_new = vector_step(norm_params, g_norms, norm_state)
    bias_new, bias_state_new = vector_step(head_bias, g_bias, bias_state)
    first_new = first_new.T
    rest_new = jnp.swapaxes(rest_new, 1, 2)
    return (
        loss_sum,
        label_count[0],
        first_new,
        rest_new,
        head_new,
        norm_new,
        bias_new,
        g_first.T,
        jnp.swapaxes(g_rest, 1, 2),
        g_head,
        g_norms,
        g_bias,
        first_row_new,
        first_col_new,
        rest_row_new,
        rest_col_new,
        head_row_new,
        head_col_new,
        norm_state_new,
        bias_state_new,
        first_new.astype(BF),
        rest_new.astype(BF),
        head_new.astype(BF),
        norm_new.astype(BF),
    )


def solution(mesh):
    placed = (
        P("dom", None),
        P("dom"),
        P("dom"),
        P(None, "dom"),
        P(None, "dom", None),
        P(None, "dom"),
        P(None, "dom"),
        P(None, None, "dom"),
        P("dom", None),
        P(),
        P(),
        P(),
        P("dom"),
        P(),
        P(None, "dom"),
        P("dom"),
        P(),
        P(),
        P(),
    )
    return jax.shard_map(
        functools.partial(on_device, total=mesh.shape["dom"]),
        mesh=mesh,
        in_specs=placed,
        out_specs=(
            P(),
            P(),
            P(None, "dom"),
            P(None, None, "dom"),
            P("dom", None),
            P(),
            P(),
            P(None, "dom"),
            P(None, None, "dom"),
            P("dom", None),
            P(),
            P(),
            P(),
            P("dom"),
            P(),
            P(None, "dom"),
            P("dom"),
            P(),
            P(),
            P(),
            P(None, "dom"),
            P(None, None, "dom"),
            P("dom", None),
            P(),
        ),
        check_vma=False,
    )
```

```python
import functools

import jax
import jax.numpy as jnp
from jax import lax
from jax.experimental import pallas as pl
from jax.experimental.pallas import tpu as pltpu
from jax.sharding import PartitionSpec as P

LEARN_RATE = 0.03
VECTOR_RATE = 0.25
SQUARE_EPS = 1e-30
NORM_EPS = 1e-05

BF = jnp.bfloat16
F32 = jnp.float32
F8 = jnp.float8_e4m3fn
I32 = jnp.int32

D00 = (((0,), (0,)), ((), ()))
D11 = (((1,), (1,)), ((), ()))
D10 = (((1,), (0,)), ((), ()))

LO = 256
BUILD_NODES = 512
GROUP_NODES = 16
FWD_NODES = 512
BWD_COLS = 1024
VMEM_LIMIT = 28 << 20


def mm(left, right, dims):
    return lax.dot_general(left, right, dims, preferred_element_type=F32)


def iota(shape, dim):
    return lax.broadcasted_iota(I32, shape, dim)


def params():
    return pltpu.CompilerParams(vmem_limit_bytes=VMEM_LIMIT)


def in_hbm(value):
    return pltpu.with_memory_space_constraint(value, pltpu.HBM)


def whole(shape):
    return pl.BlockSpec(shape, lambda i: (0,) * len(shape))


def hop(value, mask, total):
    return lax.ppermute(value, "dom", [(i, i ^ mask) for i in range(total)])


def bit_groups(total):
    bits = total.bit_length() - 1
    groups = [(0, 2)]
    at = 1
    while at < bits:
        wide = min(2, bits - at)
        groups.append((at, 1 << wide))
        at += wide
    return groups[::-1]


def place(relative, total):
    out, scale = 0, 1
    for low, size in bit_groups(total):
        out = out + ((relative >> low) & (size - 1)) * scale
        scale *= size
    return out


def after(value, *others):
    return lax.optimization_barrier((value, *others))[0]


def after_all(parts, work):
    return parts if work is None else [after(parts[0], work)] + parts[1:]


def gather_rows(rows, total, works):
    groups = bit_groups(total)
    works = [None] * (len(groups) - len(works)) + list(works)
    for i, (low, size) in enumerate(groups):
        got = [hop(rows, d << low, total) for d in range(1, size)]
        done = works[i](rows) if works[i] else rows
        if i == len(groups) - 1:
            return rows, got[0]
        rows = after(jnp.concatenate([rows] + got, axis=0), done)


def cut(rows, size):
    step = rows.shape[0] // size
    return [rows[d * step : (d + 1) * step] for d in range(size)]


def swap(parts, low, total):
    return [parts[0]] + [hop(part, d << low, total) for d, part in enumerate(parts) if d]


def add_up(parts):
    kind = parts[0].dtype
    parts = [part.astype(F32) for part in parts]
    while len(parts) > 1:
        parts = [parts[i] + parts[i + 1] for i in range(0, len(parts), 2)]
    return parts[0].astype(kind)


def one_hots(ids, base_ref, low_ref):
    slots, nodes = ids.shape
    high = (ids >> 8).astype(F32).astype(BF)
    low = (ids & 255).astype(F32).astype(BF)
    width = slots * GROUP_NODES
    widen = (iota((slots, width), 0) == iota((slots, width), 1) // GROUP_NODES).astype(F32).astype(BF)
    same = iota((nodes, width), 0) % GROUP_NODES == iota((nodes, width), 1) % GROUP_NODES
    base_ref[...] = jnp.where(same, mm(high, widen, D00), -1.0).astype(BF)
    low_ref[...] = jnp.where(same, mm(low, widen, D00), 0.0)


def count_rows(start, groups, blocks, base_ref, low_ref, outs, kinds):
    width = base_ref.shape[1]
    low_iota = iota((LO, width), 0).astype(F32).astype(BF)
    one = jnp.ones((), BF)
    zero = jnp.zeros((), BF)
    sums = []
    for g in range(groups):
        rows = pl.ds(start + g * GROUP_NODES, GROUP_NODES)
        base = base_ref[rows, :]
        low_row = jnp.sum(low_ref[rows, :], axis=0, keepdims=True).astype(BF)
        right = jnp.where(low_row == low_iota, one, zero)
        left = jnp.concatenate([jnp.where(base == jnp.asarray(h, BF), one, zero) for h in range(blocks)], axis=0)
        sums.append(mm(left, right, D11))
    for h in range(blocks):
        rows = jnp.concatenate([part[h * GROUP_NODES : (h + 1) * GROUP_NODES] for part in sums], axis=0)
        for out, kind in zip(outs, kinds):
            out[pl.ds(start, groups * GROUP_NODES), h * LO : (h + 1) * LO] = rows.astype(kind)


def live_ids(ids_ref, cnt_ref, layer):
    slots, nodes = ids_ref.shape[1:]
    return jnp.where(iota((slots, nodes), 0) < cnt_ref[layer : layer + 1, :], ids_ref[0], -1)


def all_rows(nodes, blocks, base_ref, low_ref, outs, kinds):
    step = 2 * GROUP_NODES
    if blocks <= 32:
        for start in range(0, nodes, step):
            count_rows(start, 2, blocks, base_ref, low_ref, outs, kinds)
    else:

        def body(i, carry):
            count_rows(pl.multiple_of(i * step, step), 2, blocks, base_ref, low_ref, outs, kinds)
            return carry

        lax.fori_loop(0, nodes // step, body, 0)


def far_kernel(me_ref, ids_ref, cnt_ref, out_ref, base_ref, low_ref, *, layer, total, own, node_total):
    ids = live_ids(ids_ref, cnt_ref, layer)
    table = ids - node_total
    moved = place((table // own) ^ me_ref[0], total) * own + table % own
    one_hots(jnp.where(table < 0, -1, moved), base_ref, low_ref)
    all_rows(ids.shape[1], out_ref.shape[1] // LO, base_ref, low_ref, [out_ref], [F8])


def build_specs(slots, depth, nodes, layer):
    return [
        pl.BlockSpec((1, slots, nodes), lambda i: (layer, 0, i)),
        pl.BlockSpec((depth, nodes), lambda i: (0, i)),
    ]


def build_far(me, ids, counts, layer, total, own):
    depth, slots, node_total = ids.shape
    cols = total * own
    nodes = BUILD_NODES if cols <= 8192 else 128
    width = slots * GROUP_NODES
    return pl.pallas_call(
        functools.partial(far_kernel, layer=layer, total=total, own=own, node_total=node_total),
        grid=(node_total // nodes,),
        in_specs=[pl.BlockSpec(memory_space=pltpu.SMEM)] + build_specs(slots, depth, nodes, layer),
        out_specs=pl.BlockSpec((nodes, cols), lambda i: (i, 0)),
        out_shape=pltpu.HBM((node_total, cols), F8),
        scratch_shapes=[pltpu.VMEM((nodes, width), BF), pltpu.VMEM((nodes, width), F32)],
        compiler_params=params(),
        cost_estimate=pl.CostEstimate(
            flops=2 * node_total * cols * 256, bytes_accessed=node_total * cols, transcendentals=0
        ),
        name="build_far",
    )(me, ids, counts)


def near_kernel(ids_ref, cnt_ref, table_ref, part_ref, *refs, layer):
    *a_ref, base_ref, low_ref, rows_ref = refs
    one_hots(live_ids(ids_ref, cnt_ref, layer), base_ref, low_ref)
    nodes, cols = rows_ref.shape
    all_rows(nodes, cols // LO, base_ref, low_ref, [rows_ref, *a_ref], [BF, F8])
    part_ref[...] = mm(rows_ref[...], table_ref[...], D10)


def near_step(ids, counts, table, layer):
    depth, slots, node_total = ids.shape
    feat = table.shape[1]
    nodes = BUILD_NODES
    width = slots * GROUP_NODES
    return pl.pallas_call(
        functools.partial(near_kernel, layer=layer),
        grid=(node_total // nodes,),
        in_specs=build_specs(slots, depth, nodes, layer) + [whole((node_total, feat))],
        out_specs=[
            pl.BlockSpec((nodes, feat), lambda i: (i, 0)),
            pl.BlockSpec((nodes, node_total), lambda i: (i, 0)),
        ][: 1 + (layer > 0)],
        out_shape=[
            jax.ShapeDtypeStruct((node_total, feat), F32),
            pltpu.HBM((node_total, node_total), F8),
        ][: 1 + (layer > 0)],
        scratch_shapes=[
            pltpu.VMEM((nodes, width), BF),
            pltpu.VMEM((nodes, width), F32),
            pltpu.VMEM((nodes, node_total), BF),
        ],
        compiler_params=params(),
        cost_estimate=pl.CostEstimate(
            flops=4 * node_total * node_total * 256, bytes_accessed=node_total * node_total, transcendentals=0
        ),
        name="near_step",
    )(ids, counts, table)


def columns(rows, width):
    nodes = rows[0].shape[1]
    pick = iota((16, nodes), 0)
    stacked = jnp.zeros((16, nodes), F32)
    for r, row in enumerate(rows):
        stacked = jnp.where(pick == r, row.astype(F32), stacked)
    stacked = stacked.astype(BF)
    outs = []
    for r in range(len(rows)):
        take = (iota((16, width), 0) == r).astype(F32).astype(BF)
        outs.append(mm(stacked, take, D00))
    return outs


def normalise(pre):
    centre = pre - jnp.mean(pre, axis=1, keepdims=True)
    inv = lax.rsqrt(jnp.mean(centre * centre, axis=1, keepdims=True) + NORM_EPS)
    return centre * inv, inv


def row_hot(brow, start, nodes):
    return (iota((nodes, brow.shape[1]), 0) + start == brow).astype(F32).astype(BF)


def boundary_sums(a_ref, near_ref, far_ref, sum_ref):
    step = pl.program_id(0)

    @pl.when(step == 0)
    def _():
        sum_ref[...] = jnp.zeros_like(sum_ref)

    before = sum_ref[...]
    half = near_ref.shape[0]
    total = mm(a_ref[:, :half].astype(BF), near_ref[...], D10)
    sum_ref[...] = total + mm(a_ref[:, half:].astype(BF), far_ref[...], D10)
    return before


def forward_block(summed, part_ref, hid_ref, cnt_ref, self_ref, neigh_ref, norm_ref, layer):
    (count,) = columns([cnt_ref[layer : layer + 1, :]], hid_ref.shape[1])
    agg = ((part_ref[...] + summed) / count).astype(BF)
    pre = mm(hid_ref[...], self_ref[...], D11) + mm(agg, neigh_ref[...], D11)
    unit, inv = normalise(pre)
    y = unit * norm_ref[layer, 0:1, :] + norm_ref[layer, 1:2, :]
    return agg, pre, unit, inv, y, count


def layer_kernel(
    a_ref, near_ref, far_ref, part_ref, hid_ref, cnt_ref, self_ref, neigh_ref, norm_ref, brow_ref,
    next_ref, agg_ref, pre_ref, pub_ref, acc_ref, sum_ref, *, layer
):
    step = pl.program_id(0)
    summed = boundary_sums(a_ref, near_ref, far_ref, sum_ref)
    agg, pre, _, _, y, _ = forward_block(summed, part_ref, hid_ref, cnt_ref, self_ref, neigh_ref, norm_ref, layer)
    nodes = hid_ref.shape[0]
    agg_ref[...] = agg
    pre_ref[...] = pre
    new = (y * jax.nn.sigmoid(y)).astype(BF)
    next_ref[...] = new
    hot = row_hot(brow_ref[layer + 1 : layer + 2, :], (step - 1) * nodes, nodes)

    @pl.when(step == 0)
    def _():
        acc_ref[...] = jnp.zeros_like(acc_ref)

    acc_ref[...] += mm(hot, new, D00)

    @pl.when(step == pl.num_programs(0) - 1)
    def _():
        pub_ref[...] = acc_ref[...].astype(BF)


def weight_columns(layer, hid, first_wide):
    return 0 if layer == 0 else 2 * first_wide + 2 * hid * (layer - 1)


def weight_specs(hid, feat, layer):
    at = weight_columns(layer, hid, hid // 2) // feat
    return [pl.BlockSpec((hid, feat), lambda i: (0, at)), pl.BlockSpec((hid, feat), lambda i: (0, at + 1))]


def last_spec(shape, pick):
    return pl.BlockSpec(shape, lambda i: pick(jnp.maximum(i - 1, 0)))


def forward_specs(layer, node_total, bnd_total, feat, hid, depth):
    steps = node_total // FWD_NODES
    return [
        pl.BlockSpec((FWD_NODES, bnd_total), lambda i: (jnp.minimum(i, steps - 1), 0)),
        whole((bnd_total // 2, feat)),
        whole((bnd_total // 2, feat)),
        last_spec((FWD_NODES, feat), lambda i: (i, 0)),
        last_spec((FWD_NODES, feat), lambda i: (i, 0)),
        last_spec((depth, FWD_NODES), lambda i: (0, i)),
        *weight_specs(hid, feat, layer),
        whole((depth, 2, hid)),
    ]


def rows_spec(width):
    return pl.BlockSpec((FWD_NODES, width), lambda i: (i, 0))


def layer_forward(layer, a_bnd, shared, part, hidden, counts, weights, norms, boundary):
    node_total, feat = hidden.shape
    bnd_total = a_bnd.shape[1]
    hid = weights.shape[0]
    depth, own = boundary.shape
    row = lambda width: last_spec((FWD_NODES, width), lambda i: (i, 0))
    return pl.pallas_call(
        functools.partial(layer_kernel, layer=layer),
        grid=(node_total // FWD_NODES + 1,),
        in_specs=forward_specs(layer, node_total, bnd_total, feat, hid, depth) + [whole((depth, own))],
        out_specs=[row(hid), row(feat), row(hid), whole((own, hid))],
        out_shape=[
            jax.ShapeDtypeStruct((node_total, hid), BF),
            jax.ShapeDtypeStruct((node_total, feat), BF),
            jax.ShapeDtypeStruct((node_total, hid), F32),
            jax.ShapeDtypeStruct((own, hid), BF),
        ],
        scratch_shapes=[pltpu.VMEM((own, hid), F32), pltpu.VMEM((FWD_NODES, feat), F32)],
        compiler_params=params(),
        cost_estimate=pl.CostEstimate(
            flops=2 * node_total * (bnd_total + 1024) * 256,
            bytes_accessed=node_total * (bnd_total + 4096),
            transcendentals=0,
        ),
        name="layer_step",
    )(in_hbm(a_bnd), *shared, part, hidden, counts, weights, weights, norms, boundary)


def backward_block(d_hidden, unit, inv, y, gain):
    sig = jax.nn.sigmoid(y)
    d_out = d_hidden * sig * (1.0 + y * (1.0 - sig))
    d_gain = jnp.sum(d_out * unit, axis=0, keepdims=True)
    d_shift = jnp.sum(d_out, axis=0, keepdims=True)
    d_unit = d_out * gain
    d_pre = inv * (
        d_unit
        - jnp.mean(d_unit, axis=1, keepdims=True)
        - unit * jnp.mean(d_unit * unit, axis=1, keepdims=True)
    )
    return d_pre.astype(BF), d_gain, d_shift


def add_weight_sums(dw_ref, dnorm_ref, d_pre, hidden, agg, d_gain, d_shift, step):
    @pl.when(step == 0)
    def _():
        dw_ref[...] = jnp.zeros_like(dw_ref)
        dnorm_ref[...] = jnp.zeros_like(dnorm_ref)

    feat = hidden.shape[1]
    dw_ref[:, 0:feat] += mm(d_pre, hidden, D00)
    dw_ref[:, feat : 2 * feat] += mm(d_pre, agg, D00)
    dnorm_ref[0:1, :] += d_gain
    dnorm_ref[1:2, :] += d_shift


def into_places(dw_ref, perm_ref):
    @pl.when(pl.program_id(0) == pl.num_programs(0) - 1)
    def _():
        perm = perm_ref[...]
        rest = dw_ref[...]
        moved = jnp.zeros_like(rest)
        for _ in range(3):
            term = rest.astype(BF)
            moved = moved + mm(perm, term, D00)
            rest = rest - term.astype(F32)
        dw_ref[...] = moved


def top_kernel(
    lc_ref, a_ref, near_ref, far_ref, part_ref, hid_ref, cnt_ref, self_ref, neigh_ref, norm_ref,
    lab_ref, mask_ref, head_ref, bias_ref, perm_ref,
    ds_ref, da_ref, dw_ref, dnorm_ref, dbias_ref, loss_ref, sum_ref, *, layer
):
    step = pl.program_id(0)
    summed = boundary_sums(a_ref, near_ref, far_ref, sum_ref)
    agg, _, unit, inv, y, count = forward_block(
        summed, part_ref, hid_ref, cnt_ref, self_ref, neigh_ref, norm_ref, layer
    )
    classes = bias_ref.shape[1]
    head = head_ref[:, :classes]
    top = (y * jax.nn.sigmoid(y)).astype(BF)
    logits = mm(top, head, D10) + bias_ref[...]
    label, live = columns([lab_ref[...], jnp.where(step == 0, 0, mask_ref[...])], classes)
    peak = jnp.max(logits, axis=1, keepdims=True)
    log_total = peak + jnp.log(jnp.sum(jnp.exp(logits - peak), axis=1, keepdims=True))
    hot = label == iota(label.shape, 1).astype(F32)
    part_loss = jnp.sum(jnp.where(hot, live * (log_total - logits), 0.0), axis=0, keepdims=True)
    probs = jnp.exp(logits - log_total)
    d_logits = ((probs - hot.astype(F32)) * live / lc_ref[0]).astype(BF)

    @pl.when(step == 0)
    def _():
        dbias_ref[...] = jnp.zeros_like(dbias_ref)
        loss_ref[...] = jnp.zeros_like(loss_ref)

    loss_ref[...] += part_loss
    dbias_ref[...] += jnp.sum(d_logits.astype(F32), axis=0, keepdims=True)
    d_hidden = mm(d_logits, head, D11)
    d_pre, d_gain, d_shift = backward_block(d_hidden, unit, inv, y, norm_ref[layer, 0:1, :])
    add_weight_sums(dw_ref, dnorm_ref, d_pre, hid_ref[...], agg, d_gain, d_shift, step)
    feat = hid_ref.shape[1]
    dw_ref[:, 2 * feat : 2 * feat + classes] += mm(top, d_logits, D00)
    into_places(dw_ref, perm_ref)
    ds_ref[...] = mm(d_pre, self_ref[...], D10)
    da_ref[...] = (mm(d_pre, neigh_ref[...], D10) / count).astype(BF)


def top_layer(layer, label_count, a_bnd, shared, part, hidden, counts, weights, norms, labels, live, bias, perm):
    node_total, feat = hidden.shape
    bnd_total = a_bnd.shape[1]
    hid = weights.shape[0]
    depth = norms.shape[0]
    classes = bias.shape[1]
    head_at = weight_columns(depth, hid, hid // 2) // 128
    row = last_spec((1, FWD_NODES), lambda i: (0, i))
    rows = last_spec((FWD_NODES, feat), lambda i: (i, 0))
    return pl.pallas_call(
        functools.partial(top_kernel, layer=layer),
        grid=(node_total // FWD_NODES + 1,),
        in_specs=[pl.BlockSpec(memory_space=pltpu.SMEM)]
        + forward_specs(layer, node_total, bnd_total, feat, hid, depth)
        + [row, row, pl.BlockSpec((hid, 128), lambda i: (0, head_at)), whole((1, classes)), whole((hid, hid))],
        out_specs=[
            rows,
            rows,
            whole((hid, 2 * hid + 128)),
            whole((2, hid)),
            whole((1, classes)),
            whole((1, classes)),
        ],
        out_shape=[
            jax.ShapeDtypeStruct((node_total, feat), F32),
            jax.ShapeDtypeStruct((node_total, feat), BF),
            jax.ShapeDtypeStruct((hid, 2 * hid + 128), F32),
            jax.ShapeDtypeStruct((2, hid), F32),
            jax.ShapeDtypeStruct((1, classes), F32),
            jax.ShapeDtypeStruct((1, classes), F32),
        ],
        scratch_shapes=[pltpu.VMEM((FWD_NODES, feat), F32)],
        compiler_params=params(),
        cost_estimate=pl.CostEstimate(
            flops=2 * node_total * (bnd_total + 3072) * 256,
            bytes_accessed=node_total * (bnd_total + 4096),
            transcendentals=0,
        ),
        name="top_step",
    )(label_count, in_hbm(a_bnd), *shared, part, hidden, counts, weights, weights, norms, labels, live, weights, bias, perm)


def lower_kernel(
    early_ref, late_ref, dshared_ref, brow_ref, pre_ref, hid_ref, agg_ref, cnt_ref, norm_ref, perm_ref, self_ref, neigh_ref,
    *outs, layer
):
    step = pl.program_id(0)
    nodes = early_ref.shape[0]
    hot = row_hot(brow_ref[layer + 1 : layer + 2, :], step * nodes, nodes)
    shared = dshared_ref[...]
    shared_top = shared.astype(BF)
    shared_rest = (shared - shared_top.astype(F32)).astype(BF)
    d_hidden = jnp.where(step < pl.num_programs(0) // 2, early_ref[...], late_ref[...])
    d_hidden = d_hidden + mm(hot, shared_top, D10) + mm(hot, shared_rest, D10)
    unit, inv = normalise(pre_ref[...])
    gain = norm_ref[layer, 0:1, :]
    y = unit * gain + norm_ref[layer, 1:2, :]
    d_pre, d_gain, d_shift = backward_block(d_hidden, unit, inv, y, gain)
    dw_ref, dnorm_ref = outs[0], outs[1]
    add_weight_sums(dw_ref, dnorm_ref, d_pre, hid_ref[...], agg_ref[...], d_gain, d_shift, step)
    into_places(dw_ref, perm_ref)
    if len(outs) > 2:
        (count,) = columns([cnt_ref[layer : layer + 1, :]], hid_ref.shape[1])
        outs[2][...] = mm(d_pre, self_ref[...], D10)
        outs[3][...] = (mm(d_pre, neigh_ref[...], D10) / count).astype(BF)


def layer_backward(layer, d_early, d_late, d_shared, boundary, pre, hidden, agg, counts, norms, perm, weights):
    hid = d_early.shape[1]
    node_total, feat = hidden.shape
    half = node_total // FWD_NODES // 2
    depth, own = boundary.shape
    out_specs = [whole((hid, 2 * feat)), whole((2, hid))]
    out_shape = [jax.ShapeDtypeStruct((hid, 2 * feat), F32), jax.ShapeDtypeStruct((2, hid), F32)]
    if layer:
        out_specs += [rows_spec(feat), rows_spec(feat)]
        out_shape += [
            jax.ShapeDtypeStruct((node_total, feat), F32),
            jax.ShapeDtypeStruct((node_total, feat), BF),
        ]
    return pl.pallas_call(
        functools.partial(lower_kernel, layer=layer),
        grid=(node_total // FWD_NODES,),
        in_specs=[
            pl.BlockSpec((FWD_NODES, hid), lambda i: (jnp.minimum(i, half - 1), 0)),
            pl.BlockSpec((FWD_NODES, hid), lambda i: (jnp.maximum(i - half, 0), 0)),
            whole((own, hid)),
            whole((depth, own)),
            rows_spec(hid),
            rows_spec(feat),
            rows_spec(feat),
            pl.BlockSpec((depth, FWD_NODES), lambda i: (0, i)),
            whole((depth, 2, hid)),
            whole((hid, hid)),
            *weight_specs(hid, feat, layer),
        ],
        out_specs=out_specs,
        out_shape=out_shape,
        compiler_params=params(),
        cost_estimate=pl.CostEstimate(
            flops=2 * node_total * 2048 * 256, bytes_accessed=node_total * 6144, transcendentals=0
        ),
        name="lower_step",
    )(d_early, d_late, d_shared, boundary, pre, hidden, agg, counts, norms, perm, weights, weights)


def spread_kernel(a_ref, d_ref, *refs, add):
    total = mm(a_ref[...].astype(BF), d_ref[...], D00)
    if add:
        total = total + refs[0][...]
    refs[-1][...] = total.astype(refs[-1].dtype)


def spread(a, d_rows, extra, kind, first, steps):
    node_total = a.shape[0]
    feat = d_rows.shape[1]
    specs = [pl.BlockSpec((node_total, BWD_COLS), lambda i: (0, i + first)), whole((node_total, feat))]
    specs += [pl.BlockSpec((BWD_COLS, feat), lambda i: (i + first, 0))] * len(extra)
    return pl.pallas_call(
        functools.partial(spread_kernel, add=len(extra) > 0),
        grid=(steps,),
        in_specs=specs,
        out_specs=pl.BlockSpec((BWD_COLS, feat), lambda i: (i, 0)),
        out_shape=jax.ShapeDtypeStruct((steps * BWD_COLS, feat), kind),
        compiler_params=params(),
        cost_estimate=pl.CostEstimate(
            flops=2 * node_total * steps * BWD_COLS * 256,
            bytes_accessed=node_total * steps * BWD_COLS,
            transcendentals=0,
        ),
        name="spread_near" if extra else "spread_far",
    )(in_hbm(a), d_rows, *extra)


def lane_pad(value):
    wide = -(-value.shape[1] // 128) * 128
    return jnp.pad(value, ((0, 0), (0, wide - value.shape[1])))


def factored_step(weight, gradient, row_new, col_new, row_mean):
    estimate = row_new[..., None, :] * col_new[..., :, None] / row_mean[..., None, None]
    return weight - LEARN_RATE * gradient * lax.rsqrt(estimate)


def vector_step(param, gradient, state):
    state_new = 0.5 * state + 0.5 * (gradient * gradient + SQUARE_EPS)
    return (param - VECTOR_RATE * gradient * lax.rsqrt(state_new), state_new)


def on_device(
    features,
    labels,
    train_mask,
    boundary,
    neighbours,
    counts,
    first_weight,
    rest_weight,
    head_weight,
    norm_params,
    head_bias,
    first_row,
    first_col,
    rest_row,
    rest_col,
    head_row,
    head_col,
    norm_state,
    bias_state,
    *,
    total,
):
    me = lax.axis_index("dom").astype(I32)
    me_ref = me[None]
    depth = norm_params.shape[0]
    own = boundary.shape[1]
    node_total, f_in = features.shape
    hid = norm_params.shape[2]
    classes = head_bias.shape[0]
    cols_own = hid // total if hid >= total else 1

    first_t = first_weight.T
    rest_t = jnp.swapaxes(rest_weight, 1, 2)
    ids = jnp.swapaxes(neighbours, 1, 2)

    col = jnp.arange(hid, dtype=I32)
    position = place((col // cols_own) ^ me, total) * cols_own + col % cols_own
    perm = (position[:, None] == jnp.arange(hid, dtype=I32)[None, :]).astype(BF)

    hidden = lane_pad(features.astype(BF))
    f_wide = hidden.shape[1]
    mine = jnp.concatenate(
        [lane_pad(first_t[:, :f_in]), lane_pad(first_t[:, f_in:])]
        + [rest_t[k] for k in range(depth - 1)]
        + [lane_pad(head_weight)],
        axis=1,
    ).astype(BF)
    tiles = mine.shape[1] // 128
    mine = jnp.swapaxes(mine.reshape(cols_own, tiles, 128), 0, 1).reshape(tiles * cols_own, 128)
    labelled = jnp.sum(train_mask)
    labelled = jnp.where(jnp.arange(128) == 0, labelled // 64, jnp.where(jnp.arange(128) == 1, labelled % 64, 0))
    pad_rows = -(own + tiles * cols_own + 1) % 16
    labelled = jnp.pad(labelled.astype(BF)[None], ((0, pad_rows), (0, 0)))
    first_rows = jnp.concatenate([hidden[boundary[0]], mine, labelled], axis=0)

    tables = [[None, None] for _ in range(depth)]
    parts = [None] * depth

    def beside(layer, table):
        def far(wait):
            tables[layer][1] = build_far(after(me_ref, wait), ids, counts, layer, total, own)
            return tables[layer][1]

        def near(wait):
            parts[layer], *matrix = near_step(ids, counts, after(table, wait), layer)
            tables[layer][0] = matrix[0] if matrix else None
            return parts[layer]

        return [far, near, None]

    got = gather_rows(first_rows, total, beside(0, hidden))
    got = [g.reshape(total // 2, -1, 128) for g in got]
    shared = [g[:, :own].reshape(-1, 128) for g in got]
    both = jnp.concatenate([g[:, own:] for g in got], axis=0)
    packed = both[:, : tiles * cols_own].reshape(total, tiles, cols_own, 128)
    packed = jnp.swapaxes(packed, 1, 2).reshape(hid, tiles * 128)
    packed = mm(perm, packed, D10).astype(BF)
    marks = both[:, tiles * cols_own].astype(F32)
    label_count = (64.0 * jnp.sum(marks[:, 0]) + jnp.sum(marks[:, 1])).reshape(1)
    weights, label_count, perm = lax.optimization_barrier((packed, label_count, perm))

    saved = []
    for layer in range(depth):
        if layer:
            shared = gather_rows(published, total, beside(layer, hidden))
        a_loc, a_bnd = tables[layer]
        if layer < depth - 1:
            new, agg, pre, published = layer_forward(
                layer, a_bnd, shared, parts[layer], hidden, counts, weights, norm_params, boundary
            )
            saved.append((a_loc, a_bnd, hidden, agg, pre))
            hidden = new
    ds, da, dw, dnorm, dbias, loss = top_layer(
        depth - 1, label_count, a_bnd, shared, parts[-1], hidden, counts, weights, norm_params,
        labels[None], train_mask[None], head_bias[None], perm,
    )
    d_norms = [None] * depth
    d_norms[-1] = dnorm
    grads = [None] * depth
    near_steps = node_total // BWD_COLS
    far_steps = a_bnd.shape[1] // BWD_COLS
    rounds = bit_groups(total)[::-1]
    for layer in reversed(range(depth - 1)):
        d_near = []
        for i in range(len(rounds) + 1):
            here = da
            if i < len(rounds):
                dw = swap(cut(dw, rounds[i][1]), rounds[i][0], total)
                here = after(here, dw[0])
            if i == 1:
                arrived = hop(sent, 1, total)
                here = after(here, sent)
            elif i > 1:
                low, size = rounds[i - 1]
                far = swap(cut(far, size), low, total)
                here = after(here, far[0])
            work = None
            if i == 0:
                work = sent = spread(a_bnd, here, (), BF, far_steps // 2, far_steps // 2)
            elif i == 1:
                work = spread(a_bnd, here, (), BF, 0, far_steps // 2)
            elif i < 4:
                work = spread(a_loc, here, (ds,), F32, (i - 2) * near_steps // 2, near_steps // 2)
                d_near.append(work)
            if i < len(rounds):
                dw = add_up(after_all(dw, work))
            if i == 1:
                far = add_up([work, arrived])
            elif i > 1:
                far = add_up(after_all(far, work))
        grads[layer + 1] = dw
        d_shared = far.astype(F32)
        a_loc, a_bnd, hidden, agg, pre = saved[layer]
        outs = layer_backward(
            layer, *d_near, d_shared, boundary, pre, hidden, agg, counts, norm_params, perm, weights
        )
        dw, d_norms[layer] = outs[0], outs[1]
        if layer:
            ds, da = outs[2:]

    g_head = grads[-1][:, 2 * hid : 2 * hid + classes]
    g_rest = jnp.stack([g[:, : 2 * hid] for g in grads[1:]])
    sq_rest = g_rest * g_rest + SQUARE_EPS
    sq_head = g_head * g_head + SQUARE_EPS
    head_row_new = 0.5 * head_row + 0.5 * jnp.mean(sq_head, axis=1)

    pieces = [
        jnp.stack(d_norms).reshape(-1),
        dbias.reshape(-1),
        jnp.sum(sq_rest, axis=1).reshape(-1),
        jnp.sum(sq_head, axis=0),
        jnp.sum(head_row_new, keepdims=True),
        jnp.sum(loss, keepdims=True).reshape(1),
    ]
    wide = dw.shape[1]
    count = sum(piece.shape[0] for piece in pieces)
    sums = jnp.pad(jnp.concatenate(pieces), (0, -count % (8 * wide))).reshape(-1, wide)
    extra = sums.shape[0]
    last = len(rounds) - 1
    for i, (low, size) in enumerate(rounds):
        keep = cut(dw, size)
        if i == last:
            keep = [jnp.concatenate([keep[p ^ d] for p in range(size)], axis=0) for d in range(size)]
        got = swap([jnp.concatenate([part, sums], axis=0) for part in keep], low, total)
        both = add_up(got)
        sums = both[-extra:]
        dw = both[:-extra]
    blocks = [jnp.sum(block * block + SQUARE_EPS, axis=0) for block in cut(dw, rounds[last][1])]
    first_sums = add_up(blocks)
    for low, size in rounds[:last]:
        mask = 1
        while mask < size:
            first_sums = first_sums + hop(first_sums, mask << low, total)
            mask *= 2
    g_wide = dw[:cols_own]
    g_first = jnp.concatenate([g_wide[:, :f_in], g_wide[:, f_wide : f_wide + f_in]], axis=1)
    first_sums = jnp.concatenate([first_sums[:f_in], first_sums[f_wide : f_wide + f_in]])
    sq_first = g_first * g_first + SQUARE_EPS

    sums = sums.reshape(-1)
    parts = []
    at = 0
    for piece in pieces:
        parts.append(sums[at : at + piece.shape[0]])
        at += piece.shape[0]
    g_norms = parts[0].reshape(norm_params.shape)
    g_bias = parts[1]
    rest_sums = parts[2].reshape(rest_row.shape)
    head_sums = parts[3]
    head_row_mean = parts[4][0] / hid
    loss_sum = parts[5][0]

    first_row_new = 0.5 * first_row + 0.5 * first_sums / hid
    first_col_new = 0.5 * first_col + 0.5 * jnp.mean(sq_first, axis=1)
    rest_row_new = 0.5 * rest_row + 0.5 * rest_sums / hid
    rest_col_new = 0.5 * rest_col + 0.5 * jnp.mean(sq_rest, axis=2)
    head_col_new = 0.5 * head_col + 0.5 * head_sums / hid
    first_new = factored_step(first_t, g_first, first_row_new, first_col_new, jnp.mean(first_row_new))
    rest_new = factored_step(rest_t, g_rest, rest_row_new, rest_col_new, jnp.mean(rest_row_new, axis=1))
    head_new = head_weight - LEARN_RATE * g_head * lax.rsqrt(
        head_row_new[:, None] * head_col_new[None, :] / head_row_mean
    )
    norm_new, norm_state_new = vector_step(norm_params, g_norms, norm_state)
    bias_new, bias_state_new = vector_step(head_bias, g_bias, bias_state)
    first_new = first_new.T
    rest_new = jnp.swapaxes(rest_new, 1, 2)
    return (
        loss_sum,
        label_count[0],
        first_new,
        rest_new,
        head_new,
        norm_new,
        bias_new,
        g_first.T,
        jnp.swapaxes(g_rest, 1, 2),
        g_head,
        g_norms,
        g_bias,
        first_row_new,
        first_col_new,
        rest_row_new,
        rest_col_new,
        head_row_new,
        head_col_new,
        norm_state_new,
        bias_state_new,
        first_new.astype(BF),
        rest_new.astype(BF),
        head_new.astype(BF),
        norm_new.astype(BF),
    )


def solution(mesh):
    placed = (
        P("dom", None),
        P("dom"),
        P("dom"),
        P(None, "dom"),
        P(None, "dom", None),
        P(None, "dom"),
        P(None, "dom"),
        P(None, None, "dom"),
        P("dom", None),
        P(),
        P(),
        P(),
        P("dom"),
        P(),
        P(None, "dom"),
        P("dom"),
        P(),
        P(),
        P(),
    )
    return jax.shard_map(
        functools.partial(on_device, total=mesh.shape["dom"]),
        mesh=mesh,
        in_specs=placed,
        out_specs=(
            P(),
            P(),
            P(None, "dom"),
            P(None, None, "dom"),
            P("dom", None),
            P(),
            P(),
            P(None, "dom"),
            P(None, None, "dom"),
            P("dom", None),
            P(),
            P(),
            P(),
            P("dom"),
            P(),
            P(None, "dom"),
            P("dom"),
            P(),
            P(),
            P(),
            P(None, "dom"),
            P(None, None, "dom"),
            P("dom", None),
            P(),
        ),
        check_vma=False,
    )
```

```python
import functools

import jax
import jax.numpy as jnp
from jax import lax
from jax.experimental import pallas as pl
from jax.experimental.pallas import tpu as pltpu
from jax.sharding import PartitionSpec as P

LEARN_RATE = 0.03
VECTOR_RATE = 0.25
SQUARE_EPS = 1e-30
NORM_EPS = 1e-05

BF = jnp.bfloat16
F32 = jnp.float32
F8 = jnp.float8_e4m3fn
I32 = jnp.int32

D00 = (((0,), (0,)), ((), ()))
D11 = (((1,), (1,)), ((), ()))
D10 = (((1,), (0,)), ((), ()))

LO = 256
BUILD_NODES = 512
GROUP_NODES = 16
FWD_NODES = 512
BWD_COLS = 1024
VMEM_LIMIT = 28 << 20


def mm(left, right, dims):
    return lax.dot_general(left, right, dims, preferred_element_type=F32)


def iota(shape, dim):
    return lax.broadcasted_iota(I32, shape, dim)


def params():
    return pltpu.CompilerParams(vmem_limit_bytes=VMEM_LIMIT)


def in_hbm(value):
    return pltpu.with_memory_space_constraint(value, pltpu.HBM)


def whole(shape):
    return pl.BlockSpec(shape, lambda i: (0,) * len(shape))


def hop(value, mask, total):
    return lax.ppermute(value, "dom", [(i, i ^ mask) for i in range(total)])


def bit_groups(total):
    bits = total.bit_length() - 1
    groups = [(0, 2)]
    at = 1
    while at < bits:
        wide = min(2, bits - at)
        groups.append((at, 1 << wide))
        at += wide
    return groups[::-1]


def place(relative, total):
    out, scale = 0, 1
    for low, size in bit_groups(total):
        out = out + ((relative >> low) & (size - 1)) * scale
        scale *= size
    return out


def after(value, *others):
    return lax.optimization_barrier((value, *others))[0]


def after_all(parts, work):
    return parts if work is None else [after(parts[0], work)] + parts[1:]


def gather_rows(rows, total, works):
    groups = bit_groups(total)
    works = [None] * (len(groups) - len(works)) + list(works)
    for i, (low, size) in enumerate(groups):
        got = [hop(rows, d << low, total) for d in range(1, size)]
        done = works[i](rows) if works[i] else rows
        if i == len(groups) - 1:
            return rows, got[0]
        rows = after(jnp.concatenate([rows] + got, axis=0), done)


def cut(rows, size):
    step = rows.shape[0] // size
    return [rows[d * step : (d + 1) * step] for d in range(size)]


def swap(parts, low, total):
    return [parts[0]] + [hop(part, d << low, total) for d, part in enumerate(parts) if d]


def add_up(parts):
    kind = parts[0].dtype
    parts = [part.astype(F32) for part in parts]
    while len(parts) > 1:
        parts = [parts[i] + parts[i + 1] for i in range(0, len(parts), 2)]
    return parts[0].astype(kind)


def first_kernel(feat_ref, brow_ref, first_ref, rest_ref, head_ref, mask_ref, hid_ref, out_ref, rows_ref):
    f_in, nodes = feat_ref.shape
    own = brow_ref.shape[1]
    cols, classes = head_ref.shape
    turned = feat_ref[...].astype(BF)
    eye = (iota((f_in, 128), 0) == iota((f_in, 128), 1)).astype(F32).astype(BF)
    hid_ref[...] = mm(turned, eye, D00).astype(BF)
    hot = (iota((nodes, own), 0) == brow_ref[0:1, :]).astype(F32).astype(BF)
    rows_ref[...] = jnp.zeros_like(rows_ref)
    rows_ref[0:own, :] = mm(mm(turned, hot, D10).astype(BF), eye, D00)
    at = own
    rows_ref[at : at + cols, 0:f_in] = first_ref[:, 0:f_in]
    rows_ref[at + cols : at + 2 * cols, 0:f_in] = first_ref[:, f_in : 2 * f_in]
    at += 2 * cols
    for k in range(rest_ref.shape[0]):
        for c in range(0, rest_ref.shape[2], 128):
            rows_ref[at : at + cols, :] = rest_ref[k, :, c : c + 128]
            at += cols
    rows_ref[at : at + cols, 0:classes] = head_ref[...]
    at += cols
    count = jnp.sum(mask_ref[...].astype(F32), axis=1, keepdims=True)
    high = jnp.floor(count * (1.0 / 64.0))
    lane = iota((1, 128), 1)
    rows_ref[at : at + 1, :] = jnp.where(lane == 0, high, jnp.where(lane == 1, count - 64.0 * high, 0.0))
    out_ref[...] = rows_ref[...].astype(BF)


def first_message(feat_t, boundary, first_t, rest_t, head_weight, live):
    own = boundary.shape[1]
    cols = head_weight.shape[0]
    tiles = 3 + rest_t.shape[0] * rest_t.shape[2] // 128
    rows = -(-(own + tiles * cols + 1) // 16) * 16
    return pl.pallas_call(
        first_kernel,
        out_shape=[jax.ShapeDtypeStruct((feat_t.shape[1], 128), BF), jax.ShapeDtypeStruct((rows, 128), BF)],
        scratch_shapes=[pltpu.VMEM((rows, 128), F32)],
        compiler_params=params(),
        name="first_message",
    )(feat_t, boundary, first_t, rest_t, head_weight, live), tiles


def one_hots(ids, base_ref, low_ref):
    slots, nodes = ids.shape
    high = (ids >> 8).astype(F32).astype(BF)
    low = (ids & 255).astype(F32).astype(BF)
    width = slots * GROUP_NODES
    widen = (iota((slots, width), 0) == iota((slots, width), 1) // GROUP_NODES).astype(F32).astype(BF)
    same = iota((nodes, width), 0) % GROUP_NODES == iota((nodes, width), 1) % GROUP_NODES
    base_ref[...] = jnp.where(same, mm(high, widen, D00), -1.0).astype(BF)
    low_ref[...] = jnp.where(same, mm(low, widen, D00), 0.0)


def count_rows(start, groups, blocks, base_ref, low_ref, outs, kinds):
    width = base_ref.shape[1]
    low_iota = iota((LO, width), 0).astype(F32).astype(BF)
    one = jnp.ones((), BF)
    zero = jnp.zeros((), BF)
    sums = []
    for g in range(groups):
        rows = pl.ds(start + g * GROUP_NODES, GROUP_NODES)
        base = base_ref[rows, :]
        low_row = jnp.sum(low_ref[rows, :], axis=0, keepdims=True).astype(BF)
        right = jnp.where(low_row == low_iota, one, zero)
        left = jnp.concatenate([jnp.where(base == jnp.asarray(h, BF), one, zero) for h in range(blocks)], axis=0)
        sums.append(mm(left, right, D11))
    for h in range(blocks):
        rows = jnp.concatenate([part[h * GROUP_NODES : (h + 1) * GROUP_NODES] for part in sums], axis=0)
        for out, kind in zip(outs, kinds):
            out[pl.ds(start, groups * GROUP_NODES), h * LO : (h + 1) * LO] = rows.astype(kind)


def live_ids(ids_ref, cnt_ref, layer):
    slots, nodes = ids_ref.shape[1:]
    return jnp.where(iota((slots, nodes), 0) < cnt_ref[layer : layer + 1, :], ids_ref[0], -1)


def all_rows(nodes, blocks, base_ref, low_ref, outs, kinds):
    step = 2 * GROUP_NODES
    if blocks <= 32:
        for start in range(0, nodes, step):
            count_rows(start, 2, blocks, base_ref, low_ref, outs, kinds)
    else:

        def body(i, carry):
            count_rows(pl.multiple_of(i * step, step), 2, blocks, base_ref, low_ref, outs, kinds)
            return carry

        lax.fori_loop(0, nodes // step, body, 0)


def far_kernel(me_ref, ids_ref, cnt_ref, out_ref, base_ref, low_ref, *, layer, total, own, node_total):
    ids = live_ids(ids_ref, cnt_ref, layer)
    table = ids - node_total
    moved = place((table // own) ^ me_ref[0], total) * own + table % own
    one_hots(jnp.where(table < 0, -1, moved), base_ref, low_ref)
    all_rows(ids.shape[1], out_ref.shape[1] // LO, base_ref, low_ref, [out_ref], [F8])


def build_specs(slots, depth, nodes, layer):
    return [
        pl.BlockSpec((1, slots, nodes), lambda i: (layer, 0, i)),
        pl.BlockSpec((depth, nodes), lambda i: (0, i)),
    ]


def build_far(me, ids, counts, layer, total, own):
    depth, slots, node_total = ids.shape
    cols = total * own
    nodes = BUILD_NODES if cols <= 8192 else 128
    width = slots * GROUP_NODES
    return pl.pallas_call(
        functools.partial(far_kernel, layer=layer, total=total, own=own, node_total=node_total),
        grid=(node_total // nodes,),
        in_specs=[pl.BlockSpec(memory_space=pltpu.SMEM)] + build_specs(slots, depth, nodes, layer),
        out_specs=pl.BlockSpec((nodes, cols), lambda i: (i, 0)),
        out_shape=pltpu.HBM((node_total, cols), F8),
        scratch_shapes=[pltpu.VMEM((nodes, width), BF), pltpu.VMEM((nodes, width), F32)],
        compiler_params=params(),
        cost_estimate=pl.CostEstimate(
            flops=2 * node_total * cols * 256, bytes_accessed=node_total * cols, transcendentals=0
        ),
        name="build_far",
    )(me, ids, counts)


def near_kernel(ids_ref, cnt_ref, table_ref, part_ref, *refs, layer):
    *a_ref, base_ref, low_ref, rows_ref = refs
    one_hots(live_ids(ids_ref, cnt_ref, layer), base_ref, low_ref)
    nodes, cols = rows_ref.shape
    all_rows(nodes, cols // LO, base_ref, low_ref, [rows_ref, *a_ref], [BF, F8])
    part_ref[...] = mm(rows_ref[...], table_ref[...], D10)


def near_step(ids, counts, table, layer):
    depth, slots, node_total = ids.shape
    feat = table.shape[1]
    nodes = BUILD_NODES
    width = slots * GROUP_NODES
    return pl.pallas_call(
        functools.partial(near_kernel, layer=layer),
        grid=(node_total // nodes,),
        in_specs=build_specs(slots, depth, nodes, layer) + [whole((node_total, feat))],
        out_specs=[
            pl.BlockSpec((nodes, feat), lambda i: (i, 0)),
            pl.BlockSpec((nodes, node_total), lambda i: (i, 0)),
        ][: 1 + (layer > 0)],
        out_shape=[
            jax.ShapeDtypeStruct((node_total, feat), F32),
            pltpu.HBM((node_total, node_total), F8),
        ][: 1 + (layer > 0)],
        scratch_shapes=[
            pltpu.VMEM((nodes, width), BF),
            pltpu.VMEM((nodes, width), F32),
            pltpu.VMEM((nodes, node_total), BF),
        ],
        compiler_params=params(),
        cost_estimate=pl.CostEstimate(
            flops=4 * node_total * node_total * 256, bytes_accessed=node_total * node_total, transcendentals=0
        ),
        name="near_step",
    )(ids, counts, table)


def columns(rows, width):
    nodes = rows[0].shape[1]
    pick = iota((16, nodes), 0)
    stacked = jnp.zeros((16, nodes), F32)
    for r, row in enumerate(rows):
        stacked = jnp.where(pick == r, row.astype(F32), stacked)
    stacked = stacked.astype(BF)
    outs = []
    for r in range(len(rows)):
        take = (iota((16, width), 0) == r).astype(F32).astype(BF)
        outs.append(mm(stacked, take, D00))
    return outs


def count_inverse(cnt_ref, layer, width):
    (count,) = columns([cnt_ref[layer : layer + 1, :]], 128)
    return jnp.concatenate([1.0 / count] * (width // 128), axis=1)


def normalise(pre):
    centre = pre - jnp.mean(pre, axis=1, keepdims=True)
    inv = lax.rsqrt(jnp.mean(centre * centre, axis=1, keepdims=True) + NORM_EPS)
    return centre * inv, inv


def row_hot(brow, start, nodes):
    return (iota((nodes, brow.shape[1]), 0) + start == brow).astype(F32).astype(BF)


def boundary_sums(a_ref, near_ref, far_ref, sum_ref):
    step = pl.program_id(0)

    @pl.when(step == 0)
    def _():
        sum_ref[...] = jnp.zeros_like(sum_ref)

    before = sum_ref[...]
    half = near_ref.shape[0]
    total = mm(a_ref[:, :half].astype(BF), near_ref[...], D10)
    sum_ref[...] = total + mm(a_ref[:, half:].astype(BF), far_ref[...], D10)
    return before


def forward_block(summed, part_ref, hid_ref, cnt_ref, self_ref, neigh_ref, norm_ref, layer):
    share = count_inverse(cnt_ref, layer, hid_ref.shape[1])
    agg = ((part_ref[...] + summed) * share).astype(BF)
    pre = mm(hid_ref[...], self_ref[...], D11) + mm(agg, neigh_ref[...], D11)
    unit, inv = normalise(pre)
    y = unit * norm_ref[layer, 0:1, :] + norm_ref[layer, 1:2, :]
    return agg, pre, unit, inv, y, share


def layer_kernel(
    a_ref, near_ref, far_ref, part_ref, hid_ref, cnt_ref, self_ref, neigh_ref, norm_ref, brow_ref,
    next_ref, agg_ref, pre_ref, pub_ref, acc_ref, sum_ref, *, layer
):
    step = pl.program_id(0)
    summed = boundary_sums(a_ref, near_ref, far_ref, sum_ref)
    agg, pre, _, _, y, _ = forward_block(summed, part_ref, hid_ref, cnt_ref, self_ref, neigh_ref, norm_ref, layer)
    nodes = hid_ref.shape[0]
    agg_ref[...] = agg
    pre_ref[...] = pre
    new = (y * jax.nn.sigmoid(y)).astype(BF)
    next_ref[...] = new
    hot = row_hot(brow_ref[layer + 1 : layer + 2, :], (step - 1) * nodes, nodes)

    @pl.when(step == 0)
    def _():
        acc_ref[...] = jnp.zeros_like(acc_ref)

    acc_ref[...] += mm(hot, new, D00)

    @pl.when(step == pl.num_programs(0) - 1)
    def _():
        pub_ref[...] = acc_ref[...].astype(BF)


def weight_columns(layer, hid, first_wide):
    return 0 if layer == 0 else 2 * first_wide + 2 * hid * (layer - 1)


def weight_specs(hid, feat, layer):
    at = weight_columns(layer, hid, hid // 2) // feat
    return [pl.BlockSpec((hid, feat), lambda i: (0, at)), pl.BlockSpec((hid, feat), lambda i: (0, at + 1))]


def last_spec(shape, pick):
    return pl.BlockSpec(shape, lambda i: pick(jnp.maximum(i - 1, 0)))


def forward_specs(layer, node_total, bnd_total, feat, hid, depth):
    steps = node_total // FWD_NODES
    return [
        pl.BlockSpec((FWD_NODES, bnd_total), lambda i: (jnp.minimum(i, steps - 1), 0)),
        whole((bnd_total // 2, feat)),
        whole((bnd_total // 2, feat)),
        last_spec((FWD_NODES, feat), lambda i: (i, 0)),
        last_spec((FWD_NODES, feat), lambda i: (i, 0)),
        last_spec((depth, FWD_NODES), lambda i: (0, i)),
        *weight_specs(hid, feat, layer),
        whole((depth, 2, hid)),
    ]


def rows_spec(width):
    return pl.BlockSpec((FWD_NODES, width), lambda i: (i, 0))


def layer_forward(layer, a_bnd, shared, part, hidden, counts, weights, norms, boundary):
    node_total, feat = hidden.shape
    bnd_total = a_bnd.shape[1]
    hid = weights.shape[0]
    depth, own = boundary.shape
    row = lambda width: last_spec((FWD_NODES, width), lambda i: (i, 0))
    return pl.pallas_call(
        functools.partial(layer_kernel, layer=layer),
        grid=(node_total // FWD_NODES + 1,),
        in_specs=forward_specs(layer, node_total, bnd_total, feat, hid, depth) + [whole((depth, own))],
        out_specs=[row(hid), row(feat), row(hid), whole((own, hid))],
        out_shape=[
            jax.ShapeDtypeStruct((node_total, hid), BF),
            jax.ShapeDtypeStruct((node_total, feat), BF),
            jax.ShapeDtypeStruct((node_total, hid), F32),
            jax.ShapeDtypeStruct((own, hid), BF),
        ],
        scratch_shapes=[pltpu.VMEM((own, hid), F32), pltpu.VMEM((FWD_NODES, feat), F32)],
        compiler_params=params(),
        cost_estimate=pl.CostEstimate(
            flops=2 * node_total * (bnd_total + 1024) * 256,
            bytes_accessed=node_total * (bnd_total + 4096),
            transcendentals=0,
        ),
        name="layer_step",
    )(in_hbm(a_bnd), *shared, part, hidden, counts, weights, weights, norms, boundary)


def backward_block(d_hidden, unit, inv, y, gain):
    sig = jax.nn.sigmoid(y)
    d_out = d_hidden * sig * (1.0 + y * (1.0 - sig))
    d_gain = jnp.sum(d_out * unit, axis=0, keepdims=True)
    d_shift = jnp.sum(d_out, axis=0, keepdims=True)
    d_unit = d_out * gain
    d_pre = inv * (
        d_unit
        - jnp.mean(d_unit, axis=1, keepdims=True)
        - unit * jnp.mean(d_unit * unit, axis=1, keepdims=True)
    )
    return d_pre.astype(BF), d_gain, d_shift


def add_weight_sums(dw_ref, dnorm_ref, d_pre, hidden, agg, d_gain, d_shift, step):
    @pl.when(step == 0)
    def _():
        dw_ref[...] = jnp.zeros_like(dw_ref)
        dnorm_ref[...] = jnp.zeros_like(dnorm_ref)

    feat = hidden.shape[1]
    dw_ref[:, 0:feat] += mm(d_pre, hidden, D00)
    dw_ref[:, feat : 2 * feat] += mm(d_pre, agg, D00)
    dnorm_ref[0:1, :] += d_gain
    dnorm_ref[1:2, :] += d_shift


def into_places(dw_ref, perm_ref):
    @pl.when(pl.program_id(0) == pl.num_programs(0) - 1)
    def _():
        perm = perm_ref[...]
        rest = dw_ref[...]
        moved = jnp.zeros_like(rest)
        for _ in range(3):
            term = rest.astype(BF)
            moved = moved + mm(perm, term, D00)
            rest = rest - term.astype(F32)
        dw_ref[...] = moved


def top_kernel(
    lc_ref, a_ref, near_ref, far_ref, part_ref, hid_ref, cnt_ref, self_ref, neigh_ref, norm_ref,
    lab_ref, mask_ref, head_ref, bias_ref, perm_ref,
    ds_ref, da_ref, dw_ref, dnorm_ref, dbias_ref, loss_ref, sum_ref, *, layer
):
    step = pl.program_id(0)
    summed = boundary_sums(a_ref, near_ref, far_ref, sum_ref)
    agg, _, unit, inv, y, share = forward_block(
        summed, part_ref, hid_ref, cnt_ref, self_ref, neigh_ref, norm_ref, layer
    )
    classes = bias_ref.shape[1]
    head = head_ref[:, :classes]
    top = (y * jax.nn.sigmoid(y)).astype(BF)
    logits = mm(top, head, D10) + bias_ref[...]
    label, live = columns([lab_ref[...], jnp.where(step == 0, 0, mask_ref[...])], classes)
    peak = jnp.max(logits, axis=1, keepdims=True)
    log_total = peak + jnp.log(jnp.sum(jnp.exp(logits - peak), axis=1, keepdims=True))
    hot = label == iota(label.shape, 1).astype(F32)
    part_loss = jnp.sum(jnp.where(hot, live * (log_total - logits), 0.0), axis=0, keepdims=True)
    probs = jnp.exp(logits - log_total)
    d_logits = ((probs - hot.astype(F32)) * live / lc_ref[0]).astype(BF)

    @pl.when(step == 0)
    def _():
        dbias_ref[...] = jnp.zeros_like(dbias_ref)
        loss_ref[...] = jnp.zeros_like(loss_ref)

    loss_ref[...] += part_loss
    dbias_ref[...] += jnp.sum(d_logits.astype(F32), axis=0, keepdims=True)
    d_hidden = mm(d_logits, head, D11)
    d_pre, d_gain, d_shift = backward_block(d_hidden, unit, inv, y, norm_ref[layer, 0:1, :])
    add_weight_sums(dw_ref, dnorm_ref, d_pre, hid_ref[...], agg, d_gain, d_shift, step)
    feat = hid_ref.shape[1]
    dw_ref[:, 2 * feat : 2 * feat + classes] += mm(top, d_logits, D00)
    into_places(dw_ref, perm_ref)
    ds_ref[...] = mm(d_pre, self_ref[...], D10)
    da_ref[...] = (mm(d_pre, neigh_ref[...], D10) * share).astype(BF)


def top_layer(layer, label_count, a_bnd, shared, part, hidden, counts, weights, norms, labels, live, bias, perm):
    node_total, feat = hidden.shape
    bnd_total = a_bnd.shape[1]
    hid = weights.shape[0]
    depth = norms.shape[0]
    classes = bias.shape[1]
    head_at = weight_columns(depth, hid, hid // 2) // 128
    row = last_spec((1, FWD_NODES), lambda i: (0, i))
    rows = last_spec((FWD_NODES, feat), lambda i: (i, 0))
    return pl.pallas_call(
        functools.partial(top_kernel, layer=layer),
        grid=(node_total // FWD_NODES + 1,),
        in_specs=[pl.BlockSpec(memory_space=pltpu.SMEM)]
        + forward_specs(layer, node_total, bnd_total, feat, hid, depth)
        + [row, row, pl.BlockSpec((hid, 128), lambda i: (0, head_at)), whole((1, classes)), whole((hid, hid))],
        out_specs=[
            rows,
            rows,
            whole((hid, 3 * hid)),
            whole((2, hid)),
            whole((1, classes)),
            whole((1, classes)),
        ],
        out_shape=[
            jax.ShapeDtypeStruct((node_total, feat), F32),
            jax.ShapeDtypeStruct((node_total, feat), BF),
            jax.ShapeDtypeStruct((hid, 3 * hid), F32),
            jax.ShapeDtypeStruct((2, hid), F32),
            jax.ShapeDtypeStruct((1, classes), F32),
            jax.ShapeDtypeStruct((1, classes), F32),
        ],
        scratch_shapes=[pltpu.VMEM((FWD_NODES, feat), F32)],
        compiler_params=params(),
        cost_estimate=pl.CostEstimate(
            flops=2 * node_total * (bnd_total + 3072) * 256,
            bytes_accessed=node_total * (bnd_total + 4096),
            transcendentals=0,
        ),
        name="top_step",
    )(label_count, in_hbm(a_bnd), *shared, part, hidden, counts, weights, weights, norms, labels, live, weights, bias, perm)


def lower_kernel(
    near_ref, dshared_ref, brow_ref, pre_ref, hid_ref, agg_ref, cnt_ref, norm_ref, perm_ref, self_ref, neigh_ref,
    *outs, layer
):
    step = pl.program_id(0)
    nodes = near_ref.shape[0]
    hot = row_hot(brow_ref[layer + 1 : layer + 2, :], step * nodes, nodes)
    shared = dshared_ref[...]
    shared_top = shared.astype(BF)
    shared_rest = (shared - shared_top.astype(F32)).astype(BF)
    d_hidden = near_ref[...] + mm(hot, shared_top, D10) + mm(hot, shared_rest, D10)
    unit, inv = normalise(pre_ref[...])
    gain = norm_ref[layer, 0:1, :]
    y = unit * gain + norm_ref[layer, 1:2, :]
    d_pre, d_gain, d_shift = backward_block(d_hidden, unit, inv, y, gain)
    dw_ref, dnorm_ref = outs[0], outs[1]
    add_weight_sums(dw_ref, dnorm_ref, d_pre, hid_ref[...], agg_ref[...], d_gain, d_shift, step)
    into_places(dw_ref, perm_ref)
    if len(outs) > 2:
        share = count_inverse(cnt_ref, layer, hid_ref.shape[1])
        outs[2][...] = mm(d_pre, self_ref[...], D10)
        outs[3][...] = (mm(d_pre, neigh_ref[...], D10) * share).astype(BF)


def layer_backward(layer, d_near, d_shared, boundary, pre, hidden, agg, counts, norms, perm, weights):
    hid = d_near.shape[1]
    node_total, feat = hidden.shape
    depth, own = boundary.shape
    out_specs = [whole((hid, 2 * feat)), whole((2, hid))]
    out_shape = [jax.ShapeDtypeStruct((hid, 2 * feat), F32), jax.ShapeDtypeStruct((2, hid), F32)]
    if layer:
        out_specs += [rows_spec(feat), rows_spec(feat)]
        out_shape += [
            jax.ShapeDtypeStruct((node_total, feat), F32),
            jax.ShapeDtypeStruct((node_total, feat), BF),
        ]
    return pl.pallas_call(
        functools.partial(lower_kernel, layer=layer),
        grid=(node_total // FWD_NODES,),
        in_specs=[
            rows_spec(hid),
            whole((own, hid)),
            whole((depth, own)),
            rows_spec(hid),
            rows_spec(feat),
            rows_spec(feat),
            pl.BlockSpec((depth, FWD_NODES), lambda i: (0, i)),
            whole((depth, 2, hid)),
            whole((hid, hid)),
            *weight_specs(hid, feat, layer),
        ],
        out_specs=out_specs,
        out_shape=out_shape,
        compiler_params=params(),
        cost_estimate=pl.CostEstimate(
            flops=2 * node_total * 2048 * 256, bytes_accessed=node_total * 6144, transcendentals=0
        ),
        name="lower_step",
    )(d_near, d_shared, boundary, pre, hidden, agg, counts, norms, perm, weights, weights)


def spread_kernel(a_ref, d_ref, *refs, add):
    total = mm(a_ref[...].astype(BF), d_ref[...], D00)
    if add:
        total = total + refs[0][...]
    refs[-1][...] = total.astype(refs[-1].dtype)


def spread(a, d_rows, extra, kind, first, steps):
    node_total = a.shape[0]
    feat = d_rows.shape[1]
    specs = [pl.BlockSpec((node_total, BWD_COLS), lambda i: (0, i + first)), whole((node_total, feat))]
    specs += [pl.BlockSpec((BWD_COLS, feat), lambda i: (i + first, 0))] * len(extra)
    return pl.pallas_call(
        functools.partial(spread_kernel, add=len(extra) > 0),
        grid=(steps,),
        in_specs=specs,
        out_specs=pl.BlockSpec((BWD_COLS, feat), lambda i: (i, 0)),
        out_shape=jax.ShapeDtypeStruct((steps * BWD_COLS, feat), kind),
        compiler_params=params(),
        cost_estimate=pl.CostEstimate(
            flops=2 * node_total * steps * BWD_COLS * 256,
            bytes_accessed=node_total * steps * BWD_COLS,
            transcendentals=0,
        ),
        name="spread_near" if extra else "spread_far",
    )(in_hbm(a), d_rows, *extra)


def factored_step(weight, gradient, row_new, col_new, row_mean):
    estimate = row_new[..., None, :] * col_new[..., :, None] / row_mean[..., None, None]
    return weight - LEARN_RATE * gradient * lax.rsqrt(estimate)


def vector_step(param, gradient, state):
    state_new = 0.5 * state + 0.5 * (gradient * gradient + SQUARE_EPS)
    return (param - VECTOR_RATE * gradient * lax.rsqrt(state_new), state_new)


def on_device(
    features,
    labels,
    train_mask,
    boundary,
    neighbours,
    counts,
    first_weight,
    rest_weight,
    head_weight,
    norm_params,
    head_bias,
    first_row,
    first_col,
    rest_row,
    rest_col,
    head_row,
    head_col,
    norm_state,
    bias_state,
    *,
    total,
):
    me = lax.axis_index("dom").astype(I32)
    me_ref = me[None]
    depth = norm_params.shape[0]
    own = boundary.shape[1]
    node_total, f_in = features.shape
    hid = norm_params.shape[2]
    classes = head_bias.shape[0]
    cols_own = hid // total if hid >= total else 1

    first_t = first_weight.T
    rest_t = jnp.swapaxes(rest_weight, 1, 2)
    ids = jnp.swapaxes(neighbours, 1, 2)

    col = jnp.arange(hid, dtype=I32)
    position = place((col // cols_own) ^ me, total) * cols_own + col % cols_own
    perm = (position[:, None] == jnp.arange(hid, dtype=I32)[None, :]).astype(BF)

    (hidden, first_rows), tiles = first_message(
        features.T, boundary, first_t, rest_t, head_weight, train_mask[None]
    )
    f_wide = hidden.shape[1]

    tables = [[None, None] for _ in range(depth)]
    parts = [None] * depth

    def beside(layer, table):
        def far(wait):
            tables[layer][1] = build_far(after(me_ref, wait), ids, counts, layer, total, own)
            return tables[layer][1]

        def near(wait):
            parts[layer], *matrix = near_step(ids, counts, after(table, wait), layer)
            tables[layer][0] = matrix[0] if matrix else None
            return parts[layer]

        return [far, near, None]

    got = gather_rows(first_rows, total, beside(0, hidden))
    got = [g.reshape(total // 2, -1, 128) for g in got]
    shared = [g[:, :own].reshape(-1, 128) for g in got]
    both = jnp.concatenate([g[:, own:] for g in got], axis=0)
    packed = both[:, : tiles * cols_own].reshape(total, tiles, cols_own, 128)
    packed = jnp.swapaxes(packed, 1, 2).reshape(hid, tiles * 128)
    packed = mm(perm, packed, D10).astype(BF)
    marks = both[:, tiles * cols_own].astype(F32)
    label_count = (64.0 * jnp.sum(marks[:, 0]) + jnp.sum(marks[:, 1])).reshape(1)
    weights, label_count, perm = lax.optimization_barrier((packed, label_count, perm))

    saved = []
    for layer in range(depth):
        if layer:
            shared = gather_rows(published, total, beside(layer, hidden))
        a_loc, a_bnd = tables[layer]
        if layer < depth - 1:
            new, agg, pre, published = layer_forward(
                layer, a_bnd, shared, parts[layer], hidden, counts, weights, norm_params, boundary
            )
            saved.append((a_loc, a_bnd, hidden, agg, pre))
            hidden = new
    ds, da, dw, dnorm, dbias, loss = top_layer(
        depth - 1, label_count, a_bnd, shared, parts[-1], hidden, counts, weights, norm_params,
        labels[None], train_mask[None], head_bias[None], perm,
    )
    d_norms = [None] * depth
    d_norms[-1] = dnorm
    grads = [None] * depth
    near_steps = node_total // BWD_COLS
    far_steps = a_bnd.shape[1] // BWD_COLS
    rounds = bit_groups(total)[::-1]
    for layer in reversed(range(depth - 1)):
        low, size = rounds[0]
        dw = swap(cut(dw, size), low, total)
        sent = spread(a_bnd, after(da, dw[0]), (), BF, far_steps // 2, far_steps // 2)
        dw = add_up(after_all(dw, sent))
        arrived = hop(sent, 1, total)
        kept = spread(a_bnd, after(da, sent), (), BF, 0, far_steps // 2)
        far = kept.astype(F32) + arrived.astype(F32)
        near = None
        for low, size in rounds[1:]:
            far, dw = cut(far, size), cut(dw, size)
            edge, width = far[0].shape
            tall = dw[0].shape[0]
            stacks = [
                jnp.concatenate([far[d]] + [dw[d][:, c : c + width] for c in range(0, dw[d].shape[1], width)], axis=0)
                for d in range(size)
            ]
            stacks = swap([stacks[0]] + [stack.astype(BF) for stack in stacks[1:]], low, total)
            if near is None:
                near = spread(a_loc, after(da, stacks[0]), (ds,), F32, 0, near_steps)
                stacks[0] = after(stacks[0], near)
            stack = add_up(stacks)
            far = stack[:edge]
            dw = jnp.concatenate([stack[r : r + tall] for r in range(edge, stack.shape[0], tall)], axis=1)
        grads[layer + 1] = dw
        a_loc, a_bnd, hidden, agg, pre = saved[layer]
        outs = layer_backward(
            layer, near, far, boundary, pre, hidden, agg, counts, norm_params, perm, weights
        )
        dw, d_norms[layer] = outs[0], outs[1]
        if layer:
            ds, da = outs[2:]

    g_head = grads[-1][:, 2 * hid : 2 * hid + classes]
    g_rest = jnp.stack([g[:, : 2 * hid] for g in grads[1:]])
    sq_rest = g_rest * g_rest + SQUARE_EPS
    sq_head = g_head * g_head + SQUARE_EPS
    head_row_new = 0.5 * head_row + 0.5 * jnp.mean(sq_head, axis=1)

    pieces = [
        jnp.stack(d_norms).reshape(-1),
        dbias.reshape(-1),
        jnp.sum(sq_rest, axis=1).reshape(-1),
        jnp.sum(sq_head, axis=0),
        jnp.sum(head_row_new, keepdims=True),
        jnp.sum(loss, keepdims=True).reshape(1),
    ]
    wide = dw.shape[1]
    count = sum(piece.shape[0] for piece in pieces)
    sums = jnp.pad(jnp.concatenate(pieces), (0, -count % (8 * wide))).reshape(-1, wide)
    extra = sums.shape[0]
    last = len(rounds) - 1
    for i, (low, size) in enumerate(rounds):
        keep = cut(dw, size)
        if i == last:
            keep = [jnp.concatenate([keep[p ^ d] for p in range(size)], axis=0) for d in range(size)]
        got = swap([jnp.concatenate([part, sums], axis=0) for part in keep], low, total)
        both = add_up(got)
        sums = both[-extra:]
        dw = both[:-extra]
    blocks = [jnp.sum(block * block + SQUARE_EPS, axis=0) for block in cut(dw, rounds[last][1])]
    first_sums = add_up(blocks)
    for low, size in rounds[:last]:
        mask = 1
        while mask < size:
            first_sums = first_sums + hop(first_sums, mask << low, total)
            mask *= 2
    g_wide = dw[:cols_own]
    g_first = jnp.concatenate([g_wide[:, :f_in], g_wide[:, f_wide : f_wide + f_in]], axis=1)
    first_sums = jnp.concatenate([first_sums[:f_in], first_sums[f_wide : f_wide + f_in]])
    sq_first = g_first * g_first + SQUARE_EPS

    sums = sums.reshape(-1)
    parts = []
    at = 0
    for piece in pieces:
        parts.append(sums[at : at + piece.shape[0]])
        at += piece.shape[0]
    g_norms = parts[0].reshape(norm_params.shape)
    g_bias = parts[1]
    rest_sums = parts[2].reshape(rest_row.shape)
    head_sums = parts[3]
    head_row_mean = parts[4][0] / hid
    loss_sum = parts[5][0]

    first_row_new = 0.5 * first_row + 0.5 * first_sums / hid
    first_col_new = 0.5 * first_col + 0.5 * jnp.mean(sq_first, axis=1)
    rest_row_new = 0.5 * rest_row + 0.5 * rest_sums / hid
    rest_col_new = 0.5 * rest_col + 0.5 * jnp.mean(sq_rest, axis=2)
    head_col_new = 0.5 * head_col + 0.5 * head_sums / hid
    first_new = factored_step(first_t, g_first, first_row_new, first_col_new, jnp.mean(first_row_new))
    rest_new = factored_step(rest_t, g_rest, rest_row_new, rest_col_new, jnp.mean(rest_row_new, axis=1))
    head_new = head_weight - LEARN_RATE * g_head * lax.rsqrt(
        head_row_new[:, None] * head_col_new[None, :] / head_row_mean
    )
    norm_new, norm_state_new = vector_step(norm_params, g_norms, norm_state)
    bias_new, bias_state_new = vector_step(head_bias, g_bias, bias_state)
    first_new = first_new.T
    rest_new = jnp.swapaxes(rest_new, 1, 2)
    return (
        loss_sum,
        label_count[0],
        first_new,
        rest_new,
        head_new,
        norm_new,
        bias_new,
        g_first.T,
        jnp.swapaxes(g_rest, 1, 2),
        g_head,
        g_norms,
        g_bias,
        first_row_new,
        first_col_new,
        rest_row_new,
        rest_col_new,
        head_row_new,
        head_col_new,
        norm_state_new,
        bias_state_new,
        first_new.astype(BF),
        rest_new.astype(BF),
        head_new.astype(BF),
        norm_new.astype(BF),
    )


def solution(mesh):
    placed = (
        P("dom", None),
        P("dom"),
        P("dom"),
        P(None, "dom"),
        P(None, "dom", None),
        P(None, "dom"),
        P(None, "dom"),
        P(None, None, "dom"),
        P("dom", None),
        P(),
        P(),
        P(),
        P("dom"),
        P(),
        P(None, "dom"),
        P("dom"),
        P(),
        P(),
        P(),
    )
    return jax.shard_map(
        functools.partial(on_device, total=mesh.shape["dom"]),
        mesh=mesh,
        in_specs=placed,
        out_specs=(
            P(),
            P(),
            P(None, "dom"),
            P(None, None, "dom"),
            P("dom", None),
            P(),
            P(),
            P(None, "dom"),
            P(None, None, "dom"),
            P("dom", None),
            P(),
            P(),
            P(),
            P("dom"),
            P(),
            P(None, "dom"),
            P("dom"),
            P(),
            P(),
            P(),
            P(None, "dom"),
            P(None, None, "dom"),
            P("dom", None),
            P(),
        ),
        check_vma=False,
    )
```

```python
import functools

import jax
import jax.numpy as jnp
from jax import lax
from jax.experimental import pallas as pl
from jax.experimental.pallas import tpu as pltpu
from jax.sharding import PartitionSpec as P

LEARN_RATE = 0.03
VECTOR_RATE = 0.25
SQUARE_EPS = 1e-30
NORM_EPS = 1e-05

BF = jnp.bfloat16
F32 = jnp.float32
F8 = jnp.float8_e4m3fn
I32 = jnp.int32

D00 = (((0,), (0,)), ((), ()))
D11 = (((1,), (1,)), ((), ()))
D10 = (((1,), (0,)), ((), ()))

LO = 256
NEAR_NODES = 512
FAR_NODES = 1024
GROUP_NODES = 16
FWD_NODES = 512
LOWER_NODES = 1024
BWD_COLS = 1024
VMEM_LIMIT = 28 << 20


def mm(left, right, dims):
    return lax.dot_general(left, right, dims, preferred_element_type=F32)


def iota(shape, dim):
    return lax.broadcasted_iota(I32, shape, dim)


def params():
    return pltpu.CompilerParams(vmem_limit_bytes=VMEM_LIMIT)


def in_hbm(value):
    return pltpu.with_memory_space_constraint(value, pltpu.HBM)


def whole(shape):
    return pl.BlockSpec(shape, lambda i: (0,) * len(shape))


def hop(value, mask, total):
    return lax.ppermute(value, "dom", [(i, i ^ mask) for i in range(total)])


def bit_groups(total):
    bits = total.bit_length() - 1
    groups = [(0, 2)]
    at = 1
    while at < bits:
        wide = min(2, bits - at)
        groups.append((at, 1 << wide))
        at += wide
    return groups[::-1]


def place(relative, total):
    out, scale = 0, 1
    for low, size in bit_groups(total):
        out = out + ((relative >> low) & (size - 1)) * scale
        scale *= size
    return out


def after(value, *others):
    return lax.optimization_barrier((value, *others))[0]


def after_all(parts, work):
    return parts if work is None else [after(parts[0], work)] + parts[1:]


def gather_rows(rows, total, works):
    groups = bit_groups(total)
    works = [None] * (len(groups) - len(works)) + list(works)
    for i, (low, size) in enumerate(groups):
        got = [hop(rows, d << low, total) for d in range(1, size)]
        done = works[i](rows) if works[i] else rows
        if i == len(groups) - 1:
            return rows, got[0]
        rows = after(jnp.concatenate([rows] + got, axis=0), done)


def cut(rows, size):
    step = rows.shape[0] // size
    return [rows[d * step : (d + 1) * step] for d in range(size)]


def swap(parts, low, total):
    return [parts[0]] + [hop(part, d << low, total) for d, part in enumerate(parts) if d]


def add_up(parts):
    kind = parts[0].dtype
    parts = [part.astype(F32) for part in parts]
    while len(parts) > 1:
        parts = [parts[i] + parts[i + 1] for i in range(0, len(parts), 2)]
    return parts[0].astype(kind)


def first_kernel(feat_ref, brow_ref, first_ref, rest_ref, head_ref, mask_ref, hid_ref, out_ref, rows_ref):
    f_in, nodes = feat_ref.shape
    own = brow_ref.shape[1]
    cols, classes = head_ref.shape
    turned = feat_ref[...].astype(BF)
    eye = (iota((f_in, 128), 0) == iota((f_in, 128), 1)).astype(F32).astype(BF)
    hid_ref[...] = mm(turned, eye, D00).astype(BF)
    hot = (iota((nodes, own), 0) == brow_ref[0:1, :]).astype(F32).astype(BF)
    rows_ref[...] = jnp.zeros_like(rows_ref)
    rows_ref[0:own, :] = mm(mm(turned, hot, D10).astype(BF), eye, D00)
    at = own
    rows_ref[at : at + cols, 0:f_in] = first_ref[:, 0:f_in]
    rows_ref[at + cols : at + 2 * cols, 0:f_in] = first_ref[:, f_in : 2 * f_in]
    at += 2 * cols
    for k in range(rest_ref.shape[0]):
        for c in range(0, rest_ref.shape[2], 128):
            rows_ref[at : at + cols, :] = rest_ref[k, :, c : c + 128]
            at += cols
    rows_ref[at : at + cols, 0:classes] = head_ref[...]
    at += cols
    count = jnp.sum(mask_ref[...].astype(F32), axis=1, keepdims=True)
    high = jnp.floor(count * (1.0 / 64.0))
    lane = iota((1, 128), 1)
    rows_ref[at : at + 1, :] = jnp.where(lane == 0, high, jnp.where(lane == 1, count - 64.0 * high, 0.0))
    out_ref[...] = rows_ref[...].astype(BF)


def first_message(feat_t, boundary, first_t, rest_t, head_weight, live):
    own = boundary.shape[1]
    cols = head_weight.shape[0]
    tiles = 3 + rest_t.shape[0] * rest_t.shape[2] // 128
    rows = -(-(own + tiles * cols + 1) // 16) * 16
    return pl.pallas_call(
        first_kernel,
        out_shape=[jax.ShapeDtypeStruct((feat_t.shape[1], 128), BF), jax.ShapeDtypeStruct((rows, 128), BF)],
        scratch_shapes=[pltpu.VMEM((rows, 128), F32)],
        compiler_params=params(),
        name="first_message",
    )(*map(in_hbm, (feat_t, boundary, first_t, rest_t, head_weight, live))), tiles


def one_hots(ids, base_ref, low_ref):
    slots, nodes = ids.shape
    high = (ids >> 8).astype(F32).astype(BF)
    low = (ids & 255).astype(F32).astype(BF)
    width = slots * GROUP_NODES
    widen = (iota((slots, width), 0) == iota((slots, width), 1) // GROUP_NODES).astype(F32).astype(BF)
    same = iota((nodes, width), 0) % GROUP_NODES == iota((nodes, width), 1) % GROUP_NODES
    base_ref[...] = jnp.where(same, mm(high, widen, D00), -1.0).astype(BF)
    low_ref[...] = jnp.where(same, mm(low, widen, D00), 0.0)


def count_rows(start, groups, blocks, base_ref, low_ref, outs, kinds):
    width = base_ref.shape[1]
    low_iota = iota((LO, width), 0).astype(F32).astype(BF)
    one = jnp.ones((), BF)
    zero = jnp.zeros((), BF)
    sums = []
    for g in range(groups):
        rows = pl.ds(start + g * GROUP_NODES, GROUP_NODES)
        base = base_ref[rows, :]
        low_row = jnp.sum(low_ref[rows, :], axis=0, keepdims=True).astype(BF)
        right = jnp.where(low_row == low_iota, one, zero)
        left = jnp.concatenate([jnp.where(base == jnp.asarray(h, BF), one, zero) for h in range(blocks)], axis=0)
        sums.append(mm(left, right, D11))
    for h in range(blocks):
        rows = jnp.concatenate([part[h * GROUP_NODES : (h + 1) * GROUP_NODES] for part in sums], axis=0)
        for out, kind in zip(outs, kinds):
            out[pl.ds(start, groups * GROUP_NODES), h * LO : (h + 1) * LO] = rows.astype(kind)


def live_ids(ids_ref, cnt_ref, layer):
    slots, nodes = ids_ref.shape[1:]
    return jnp.where(iota((slots, nodes), 0) < cnt_ref[layer : layer + 1, :], ids_ref[0], -1)


def all_rows(nodes, blocks, base_ref, low_ref, outs, kinds):
    step = 2 * GROUP_NODES
    if blocks <= 32:
        for start in range(0, nodes, step):
            count_rows(start, 2, blocks, base_ref, low_ref, outs, kinds)
    else:

        def body(i, carry):
            count_rows(pl.multiple_of(i * step, step), 2, blocks, base_ref, low_ref, outs, kinds)
            return carry

        lax.fori_loop(0, nodes // step, body, 0)


def far_kernel(me_ref, ids_ref, cnt_ref, out_ref, base_ref, low_ref, *, layer, total, own, node_total):
    ids = live_ids(ids_ref, cnt_ref, layer)
    table = ids - node_total
    moved = place((table // own) ^ me_ref[0], total) * own + table % own
    one_hots(jnp.where(table < 0, -1, moved), base_ref, low_ref)
    all_rows(ids.shape[1], out_ref.shape[1] // LO, base_ref, low_ref, [out_ref], [F8])


def build_specs(slots, depth, nodes, layer):
    return [
        pl.BlockSpec((1, slots, nodes), lambda i: (layer, 0, i)),
        pl.BlockSpec((depth, nodes), lambda i: (0, i)),
    ]


def build_far(me, ids, counts, layer, total, own):
    depth, slots, node_total = ids.shape
    cols = total * own
    nodes = FAR_NODES if cols <= 8192 else 128
    width = slots * GROUP_NODES
    return pl.pallas_call(
        functools.partial(far_kernel, layer=layer, total=total, own=own, node_total=node_total),
        grid=(node_total // nodes,),
        in_specs=[pl.BlockSpec(memory_space=pltpu.SMEM)] + build_specs(slots, depth, nodes, layer),
        out_specs=pl.BlockSpec((nodes, cols), lambda i: (i, 0)),
        out_shape=pltpu.HBM((node_total, cols), F8),
        scratch_shapes=[pltpu.VMEM((nodes, width), BF), pltpu.VMEM((nodes, width), F32)],
        compiler_params=params(),
        cost_estimate=pl.CostEstimate(
            flops=2 * node_total * cols * 256, bytes_accessed=node_total * cols, transcendentals=0
        ),
        name="build_far",
    )(me, in_hbm(ids), in_hbm(counts))


def near_kernel(ids_ref, cnt_ref, table_ref, part_ref, *refs, layer):
    *a_ref, base_ref, low_ref, rows_ref = refs
    one_hots(live_ids(ids_ref, cnt_ref, layer), base_ref, low_ref)
    nodes, cols = rows_ref.shape
    all_rows(nodes, cols // LO, base_ref, low_ref, [rows_ref, *a_ref], [BF, F8])
    part_ref[...] = mm(rows_ref[...], table_ref[...], D10)


def near_step(ids, counts, table, layer):
    depth, slots, node_total = ids.shape
    feat = table.shape[1]
    nodes = NEAR_NODES
    width = slots * GROUP_NODES
    return pl.pallas_call(
        functools.partial(near_kernel, layer=layer),
        grid=(node_total // nodes,),
        in_specs=build_specs(slots, depth, nodes, layer) + [whole((node_total, feat))],
        out_specs=[
            pl.BlockSpec((nodes, feat), lambda i: (i, 0)),
            pl.BlockSpec((nodes, node_total), lambda i: (i, 0)),
        ][: 1 + (layer > 0)],
        out_shape=[
            jax.ShapeDtypeStruct((node_total, feat), F32),
            pltpu.HBM((node_total, node_total), F8),
        ][: 1 + (layer > 0)],
        scratch_shapes=[
            pltpu.VMEM((nodes, width), BF),
            pltpu.VMEM((nodes, width), F32),
            pltpu.VMEM((nodes, node_total), BF),
        ],
        compiler_params=params(),
        cost_estimate=pl.CostEstimate(
            flops=4 * node_total * node_total * 256, bytes_accessed=node_total * node_total, transcendentals=0
        ),
        name="near_step",
    )(in_hbm(ids), in_hbm(counts), table)


def columns(rows, width):
    nodes = rows[0].shape[1]
    pick = iota((16, nodes), 0)
    stacked = jnp.zeros((16, nodes), F32)
    for r, row in enumerate(rows):
        stacked = jnp.where(pick == r, row.astype(F32), stacked)
    stacked = stacked.astype(BF)
    outs = []
    for r in range(len(rows)):
        take = (iota((16, width), 0) == r).astype(F32).astype(BF)
        outs.append(mm(stacked, take, D00))
    return outs


def count_inverse(cnt_ref, layer, width):
    (count,) = columns([cnt_ref[layer : layer + 1, :]], 128)
    return jnp.concatenate([1.0 / count] * (width // 128), axis=1)


def normalise(pre):
    centre = pre - jnp.mean(pre, axis=1, keepdims=True)
    inv = lax.rsqrt(jnp.mean(centre * centre, axis=1, keepdims=True) + NORM_EPS)
    return centre * inv, inv


def row_hot(brow, start, nodes):
    return (iota((nodes, brow.shape[1]), 0) + start == brow).astype(F32).astype(BF)


def boundary_sums(a_ref, near_ref, far_ref, sum_ref):
    half = near_ref.shape[0]
    total = mm(a_ref[:, :half].astype(BF), near_ref[...], D10)
    sum_ref[...] = total + mm(a_ref[:, half:].astype(BF), far_ref[...], D10)


def in_turn(begin, sums, finish, end):
    step = pl.program_id(0)
    last = pl.num_programs(0) - 1

    @pl.when(step == 0)
    def _():
        begin()
        sums()

    @pl.when((step > 0) & (step < last))
    def _():
        finish()
        sums()

    @pl.when(step == last)
    def _():
        finish()
        end()


def forward_block(summed, part_ref, hid_ref, cnt_ref, self_ref, neigh_ref, norm_ref, layer):
    share = count_inverse(cnt_ref, layer, hid_ref.shape[1])
    agg = ((part_ref[...] + summed) * share).astype(BF)
    pre = mm(hid_ref[...], self_ref[...], D11) + mm(agg, neigh_ref[...], D11)
    unit, inv = normalise(pre)
    y = unit * norm_ref[layer, 0:1, :] + norm_ref[layer, 1:2, :]
    return agg, pre, unit, inv, y, share


def layer_kernel(
    a_ref, near_ref, far_ref, part_ref, hid_ref, cnt_ref, self_ref, neigh_ref, norm_ref, brow_ref,
    next_ref, agg_ref, pre_ref, pub_ref, acc_ref, sum_ref, *, layer
):
    def begin():
        acc_ref[...] = jnp.zeros_like(acc_ref)

    def sums():
        boundary_sums(a_ref, near_ref, far_ref, sum_ref)

    def finish():
        agg, pre, _, _, y, _ = forward_block(
            sum_ref[...], part_ref, hid_ref, cnt_ref, self_ref, neigh_ref, norm_ref, layer
        )
        nodes = hid_ref.shape[0]
        agg_ref[...] = agg
        pre_ref[...] = pre
        new = (y * jax.nn.sigmoid(y)).astype(BF)
        next_ref[...] = new
        hot = row_hot(brow_ref[layer + 1 : layer + 2, :], (pl.program_id(0) - 1) * nodes, nodes)
        acc_ref[...] += mm(hot, new, D00)

    def end():
        pub_ref[...] = acc_ref[...].astype(BF)

    in_turn(begin, sums, finish, end)


def weight_columns(layer, hid, first_wide):
    return 0 if layer == 0 else 2 * first_wide + 2 * hid * (layer - 1)


def weight_specs(hid, feat, layer):
    at = weight_columns(layer, hid, hid // 2) // feat
    return [pl.BlockSpec((hid, feat), lambda i: (0, at)), pl.BlockSpec((hid, feat), lambda i: (0, at + 1))]


def last_spec(shape, pick):
    return pl.BlockSpec(shape, lambda i: pick(jnp.maximum(i - 1, 0)))


def forward_specs(layer, node_total, bnd_total, feat, hid, depth):
    steps = node_total // FWD_NODES
    return [
        pl.BlockSpec((FWD_NODES, bnd_total), lambda i: (jnp.minimum(i, steps - 1), 0)),
        whole((bnd_total // 2, feat)),
        whole((bnd_total // 2, feat)),
        last_spec((FWD_NODES, feat), lambda i: (i, 0)),
        last_spec((FWD_NODES, feat), lambda i: (i, 0)),
        last_spec((depth, FWD_NODES), lambda i: (0, i)),
        *weight_specs(hid, feat, layer),
        whole((depth, 2, hid)),
    ]


def rows_spec(width):
    return pl.BlockSpec((FWD_NODES, width), lambda i: (i, 0))


def layer_forward(layer, a_bnd, shared, part, hidden, counts, weights, norms, boundary):
    node_total, feat = hidden.shape
    bnd_total = a_bnd.shape[1]
    hid = weights.shape[0]
    depth, own = boundary.shape
    row = lambda width: last_spec((FWD_NODES, width), lambda i: (i, 0))
    return pl.pallas_call(
        functools.partial(layer_kernel, layer=layer),
        grid=(node_total // FWD_NODES + 1,),
        in_specs=forward_specs(layer, node_total, bnd_total, feat, hid, depth) + [whole((depth, own))],
        out_specs=[row(hid), row(feat), row(hid), whole((own, hid))],
        out_shape=[
            jax.ShapeDtypeStruct((node_total, hid), BF),
            jax.ShapeDtypeStruct((node_total, feat), BF),
            jax.ShapeDtypeStruct((node_total, hid), F32),
            jax.ShapeDtypeStruct((own, hid), BF),
        ],
        scratch_shapes=[pltpu.VMEM((own, hid), F32), pltpu.VMEM((FWD_NODES, feat), F32)],
        compiler_params=params(),
        cost_estimate=pl.CostEstimate(
            flops=2 * node_total * (bnd_total + 1024) * 256,
            bytes_accessed=node_total * (bnd_total + 4096),
            transcendentals=0,
        ),
        name="layer_step",
    )(in_hbm(a_bnd), *shared, part, hidden, counts, weights, weights, norms, boundary)


def backward_block(d_hidden, unit, inv, y, gain):
    sig = jax.nn.sigmoid(y)
    d_out = d_hidden * sig * (1.0 + y * (1.0 - sig))
    d_gain = jnp.sum(d_out * unit, axis=0, keepdims=True)
    d_shift = jnp.sum(d_out, axis=0, keepdims=True)
    d_unit = d_out * gain
    d_pre = inv * (
        d_unit
        - jnp.mean(d_unit, axis=1, keepdims=True)
        - unit * jnp.mean(d_unit * unit, axis=1, keepdims=True)
    )
    return d_pre.astype(BF), d_gain, d_shift


def add_weight_sums(dw_ref, dnorm_ref, d_pre, hidden, agg, d_gain, d_shift):
    feat = hidden.shape[1]
    hid = d_pre.shape[1]
    dw_ref[0:hid, 0:feat] += mm(d_pre, hidden, D00)
    dw_ref[0:hid, feat : 2 * feat] += mm(d_pre, agg, D00)
    dnorm_ref[0:1, :] += d_gain
    dnorm_ref[1:2, :] += d_shift


def into_places(dw_ref, perm_ref):
    perm = perm_ref[...]
    rows = slice(0, perm.shape[0])
    rest = dw_ref[rows, :]
    moved = jnp.zeros_like(rest)
    for _ in range(3):
        term = rest.astype(BF)
        moved = moved + mm(perm, term, D00)
        rest = rest - term.astype(F32)
    dw_ref[rows, :] = moved


def top_kernel(
    a_ref, near_ref, far_ref, part_ref, hid_ref, cnt_ref, self_ref, neigh_ref, norm_ref,
    lab_ref, mask_ref, marks_ref, head_ref, bias_ref, perm_ref,
    ds_ref, da_ref, dw_ref, dnorm_ref, dbias_ref, loss_ref, label_ref, sum_ref, *, layer
):
    feat = hid_ref.shape[1]
    classes = bias_ref.shape[1]

    def begin():
        for ref in (dw_ref, dnorm_ref, dbias_ref, loss_ref):
            ref[...] = jnp.zeros_like(ref)
        marks = jnp.sum(marks_ref[...], axis=0, keepdims=True)
        label_ref[...] = 64.0 * marks[:, 0:1] + marks[:, 1:2]

    def sums():
        boundary_sums(a_ref, near_ref, far_ref, sum_ref)

    def finish():
        agg, _, unit, inv, y, share = forward_block(
            sum_ref[...], part_ref, hid_ref, cnt_ref, self_ref, neigh_ref, norm_ref, layer
        )
        head = head_ref[:, :classes]
        top = (y * jax.nn.sigmoid(y)).astype(BF)
        logits = mm(top, head, D10) + bias_ref[...]
        label, live = columns([lab_ref[...], mask_ref[...]], classes)
        peak = jnp.max(logits, axis=1, keepdims=True)
        log_total = peak + jnp.log(jnp.sum(jnp.exp(logits - peak), axis=1, keepdims=True))
        hot = label == iota(label.shape, 1).astype(F32)
        loss_ref[...] += jnp.sum(jnp.where(hot, live * (log_total - logits), 0.0), axis=0, keepdims=True)
        probs = jnp.exp(logits - log_total)
        d_logits = ((probs - hot.astype(F32)) * live / label_ref[...]).astype(BF)
        dbias_ref[...] += jnp.sum(d_logits.astype(F32), axis=0, keepdims=True)
        d_hidden = mm(d_logits, head, D11)
        d_pre, d_gain, d_shift = backward_block(d_hidden, unit, inv, y, norm_ref[layer, 0:1, :])
        add_weight_sums(dw_ref, dnorm_ref, d_pre, hid_ref[...], agg, d_gain, d_shift)
        dw_ref[:, 2 * feat : 2 * feat + classes] += mm(top, d_logits, D00)
        ds_ref[...] = mm(d_pre, self_ref[...], D10)
        da_ref[...] = (mm(d_pre, neigh_ref[...], D10) * share).astype(BF)

    in_turn(begin, sums, finish, lambda: into_places(dw_ref, perm_ref))


def top_layer(layer, marks, a_bnd, shared, part, hidden, counts, weights, norms, labels, live, bias, perm):
    node_total, feat = hidden.shape
    bnd_total = a_bnd.shape[1]
    hid = weights.shape[0]
    depth = norms.shape[0]
    classes = bias.shape[1]
    head_at = weight_columns(depth, hid, hid // 2) // 128
    row = last_spec((1, FWD_NODES), lambda i: (0, i))
    rows = last_spec((FWD_NODES, feat), lambda i: (i, 0))
    return pl.pallas_call(
        functools.partial(top_kernel, layer=layer),
        grid=(node_total // FWD_NODES + 1,),
        in_specs=forward_specs(layer, node_total, bnd_total, feat, hid, depth)
        + [row, row, whole(marks.shape), pl.BlockSpec((hid, 128), lambda i: (0, head_at)), whole((1, classes)), whole((hid, hid))],
        out_specs=[
            rows,
            rows,
            whole((hid, 3 * hid)),
            whole((2, hid)),
            whole((1, classes)),
            whole((1, classes)),
            whole((1, 1)),
        ],
        out_shape=[
            jax.ShapeDtypeStruct((node_total, feat), F32),
            jax.ShapeDtypeStruct((node_total, feat), BF),
            jax.ShapeDtypeStruct((hid, 3 * hid), F32),
            jax.ShapeDtypeStruct((2, hid), F32),
            jax.ShapeDtypeStruct((1, classes), F32),
            jax.ShapeDtypeStruct((1, classes), F32),
            jax.ShapeDtypeStruct((1, 1), F32),
        ],
        scratch_shapes=[pltpu.VMEM((FWD_NODES, feat), F32)],
        compiler_params=params(),
        cost_estimate=pl.CostEstimate(
            flops=2 * node_total * (bnd_total + 3072) * 256,
            bytes_accessed=node_total * (bnd_total + 4096),
            transcendentals=0,
        ),
        name="top_step",
    )(in_hbm(a_bnd), *shared, part, hidden, counts, weights, weights, norms, labels, live, marks, weights, bias, perm)


def lower_kernel(
    near_ref, dshared_ref, brow_ref, pre_ref, hid_ref, agg_ref, cnt_ref, norm_ref, perm_ref, self_ref, neigh_ref,
    *refs, layer
):
    step = pl.program_id(0)
    nodes = near_ref.shape[0]
    hid = near_ref.shape[1]
    if layer:
        dw_ref, dnorm_ref, ds_ref, da_ref = refs
    else:
        sums_ref, dw_ref, dnorm_ref = refs

    @pl.when(step == 0)
    def _():
        dw_ref[...] = jnp.zeros_like(dw_ref)
        dnorm_ref[...] = jnp.zeros_like(dnorm_ref)

    hot = row_hot(brow_ref[layer + 1 : layer + 2, :], step * nodes, nodes)
    shared = dshared_ref[...]
    shared_top = shared.astype(BF)
    shared_rest = (shared - shared_top.astype(F32)).astype(BF)
    d_hidden = near_ref[...] + mm(hot, shared_top, D10) + mm(hot, shared_rest, D10)
    unit, inv = normalise(pre_ref[...])
    gain = norm_ref[layer, 0:1, :]
    y = unit * gain + norm_ref[layer, 1:2, :]
    d_pre, d_gain, d_shift = backward_block(d_hidden, unit, inv, y, gain)
    add_weight_sums(dw_ref, dnorm_ref, d_pre, hid_ref[...], agg_ref[...], d_gain, d_shift)
    if layer:
        share = count_inverse(cnt_ref, layer, hid_ref.shape[1])
        ds_ref[...] = mm(d_pre, self_ref[...], D10)
        da_ref[...] = (mm(d_pre, neigh_ref[...], D10) * share).astype(BF)

    @pl.when(step == pl.num_programs(0) - 1)
    def _():
        into_places(dw_ref, perm_ref)
        if not layer:
            dw_ref[hid : hid + 2, :] = dnorm_ref[...]
            dw_ref[hid + 2 :, :] = sums_ref[...]


def layer_backward(layer, d_near, d_shared, boundary, pre, hidden, agg, counts, norms, perm, weights, sums=()):
    hid = d_near.shape[1]
    node_total, feat = hidden.shape
    depth, own = boundary.shape
    rows = lambda width: pl.BlockSpec((LOWER_NODES, width), lambda i: (i, 0))
    tall = hid if layer else hid + 2 + sums[0].shape[0]
    out_specs = [whole((tall, 2 * feat)), whole((2, hid))]
    out_shape = [jax.ShapeDtypeStruct((tall, 2 * feat), F32), jax.ShapeDtypeStruct((2, hid), F32)]
    if layer:
        out_specs += [rows(feat), rows(feat)]
        out_shape += [
            jax.ShapeDtypeStruct((node_total, feat), F32),
            jax.ShapeDtypeStruct((node_total, feat), BF),
        ]
    return pl.pallas_call(
        functools.partial(lower_kernel, layer=layer),
        grid=(node_total // LOWER_NODES,),
        in_specs=[
            rows(hid),
            whole((own, hid)),
            whole((depth, own)),
            rows(hid),
            rows(feat),
            rows(feat),
            pl.BlockSpec((depth, LOWER_NODES), lambda i: (0, i)),
            whole((depth, 2, hid)),
            whole((hid, hid)),
            *weight_specs(hid, feat, layer),
            *[whole(array.shape) for array in sums],
        ],
        out_specs=out_specs,
        out_shape=out_shape,
        compiler_params=params(),
        cost_estimate=pl.CostEstimate(
            flops=2 * node_total * 2048 * 256, bytes_accessed=node_total * 6144, transcendentals=0
        ),
        name="lower_step",
    )(d_near, d_shared, boundary, pre, hidden, agg, counts, norms, perm, weights, weights, *sums)


def spread_kernel(a_ref, d_ref, *refs, add):
    total = mm(a_ref[...].astype(BF), d_ref[...], D00)
    if add:
        total = total + refs[0][...]
    refs[-1][...] = total.astype(refs[-1].dtype)


def spread(a, d_rows, extra, kind, first, steps):
    node_total = a.shape[0]
    feat = d_rows.shape[1]
    specs = [pl.BlockSpec((node_total, BWD_COLS), lambda i: (0, i + first)), whole((node_total, feat))]
    specs += [pl.BlockSpec((BWD_COLS, feat), lambda i: (i + first, 0))] * len(extra)
    return pl.pallas_call(
        functools.partial(spread_kernel, add=len(extra) > 0),
        grid=(steps,),
        in_specs=specs,
        out_specs=pl.BlockSpec((BWD_COLS, feat), lambda i: (i, 0)),
        out_shape=jax.ShapeDtypeStruct((steps * BWD_COLS, feat), kind),
        compiler_params=params(),
        cost_estimate=pl.CostEstimate(
            flops=2 * node_total * steps * BWD_COLS * 256,
            bytes_accessed=node_total * steps * BWD_COLS,
            transcendentals=0,
        ),
        name="spread_near" if extra else "spread_far",
    )(in_hbm(a), d_rows, *extra)


def factored_step(weight, gradient, row_new, col_new, row_mean):
    estimate = row_new[..., None, :] * col_new[..., :, None] / row_mean[..., None, None]
    return weight - LEARN_RATE * gradient * lax.rsqrt(estimate)


def vector_step(param, gradient, state):
    state_new = 0.5 * state + 0.5 * (gradient * gradient + SQUARE_EPS)
    return (param - VECTOR_RATE * gradient * lax.rsqrt(state_new), state_new)


def on_device(
    features,
    labels,
    train_mask,
    boundary,
    neighbours,
    counts,
    first_weight,
    rest_weight,
    head_weight,
    norm_params,
    head_bias,
    first_row,
    first_col,
    rest_row,
    rest_col,
    head_row,
    head_col,
    norm_state,
    bias_state,
    *,
    total,
):
    me = lax.axis_index("dom").astype(I32)
    me_ref = me[None]
    depth = norm_params.shape[0]
    own = boundary.shape[1]
    node_total, f_in = features.shape
    hid = norm_params.shape[2]
    classes = head_bias.shape[0]
    cols_own = hid // total if hid >= total else 1

    first_t = first_weight.T
    rest_t = jnp.swapaxes(rest_weight, 1, 2)
    ids = jnp.swapaxes(neighbours, 1, 2)

    col = jnp.arange(hid, dtype=I32)
    position = place((col // cols_own) ^ me, total) * cols_own + col % cols_own
    perm = (position[:, None] == jnp.arange(hid, dtype=I32)[None, :]).astype(BF)

    (hidden, first_rows), tiles = first_message(
        features.T, boundary, first_t, rest_t, head_weight, train_mask[None]
    )
    f_wide = hidden.shape[1]

    tables = [[None, None] for _ in range(depth)]
    parts = [None] * depth

    def beside(layer, table):
        def far(wait):
            tables[layer][1] = build_far(after(me_ref, wait), ids, counts, layer, total, own)
            return tables[layer][1]

        def near(wait):
            parts[layer], *matrix = near_step(ids, counts, after(table, wait), layer)
            tables[layer][0] = matrix[0] if matrix else None
            return parts[layer]

        return [far, near, None]

    got = gather_rows(first_rows, total, beside(0, hidden))
    got = [g.reshape(total // 2, -1, 128) for g in got]
    shared = [g[:, :own].reshape(-1, 128) for g in got]
    both = jnp.concatenate([g[:, own:] for g in got], axis=0)
    packed = both[:, : tiles * cols_own].reshape(total, tiles, cols_own, 128)
    packed = jnp.swapaxes(packed, 1, 2).reshape(hid, tiles * 128)
    packed = mm(perm, packed, D10).astype(BF)
    marks = both[:, tiles * cols_own].astype(F32)
    weights, marks, perm = lax.optimization_barrier((packed, marks, perm))

    saved = []
    for layer in range(depth):
        if layer:
            shared = gather_rows(published, total, beside(layer, hidden))
        a_loc, a_bnd = tables[layer]
        if layer < depth - 1:
            new, agg, pre, published = layer_forward(
                layer, a_bnd, shared, parts[layer], hidden, counts, weights, norm_params, boundary
            )
            saved.append((a_loc, a_bnd, hidden, agg, pre))
            hidden = new
    ds, da, dw, dnorm, dbias, loss, label_count = top_layer(
        depth - 1, marks, a_bnd, shared, parts[-1], hidden, counts, weights, norm_params,
        labels[None], train_mask[None], head_bias[None], perm,
    )
    d_norms = [None] * depth
    d_norms[-1] = dnorm
    grads = [None] * depth
    near_steps = node_total // BWD_COLS
    far_steps = a_bnd.shape[1] // BWD_COLS
    rounds = bit_groups(total)[::-1]
    for layer in reversed(range(depth - 1)):
        low, size = rounds[0]
        dw = swap(cut(dw, size), low, total)
        sent = spread(a_bnd, after(da, dw[0]), (), BF, far_steps // 2, far_steps // 2)
        dw = add_up(after_all(dw, sent))
        arrived = hop(sent, 1, total)
        kept = spread(a_bnd, after(da, sent), (), BF, 0, far_steps // 2)
        far = kept.astype(F32) + arrived.astype(F32)
        near = None
        for low, size in rounds[1:]:
            far, dw = cut(far, size), cut(dw, size)
            edge, width = far[0].shape
            tall = dw[0].shape[0]
            stacks = [
                jnp.concatenate([far[d]] + [dw[d][:, c : c + width] for c in range(0, dw[d].shape[1], width)], axis=0)
                for d in range(size)
            ]
            stacks = swap([stacks[0]] + [stack.astype(BF) for stack in stacks[1:]], low, total)
            if near is None:
                near = spread(a_loc, after(da, stacks[0]), (ds,), F32, 0, near_steps)
                stacks[0] = after(stacks[0], near)
            stack = add_up(stacks)
            far = stack[:edge]
            dw = jnp.concatenate([stack[r : r + tall] for r in range(edge, stack.shape[0], tall)], axis=1)
        grads[layer + 1] = dw
        a_loc, a_bnd, hidden, agg, pre = saved[layer]
        sums = ()
        if not layer:
            wide = 2 * f_wide
            g_head = grads[-1][:, 2 * hid : 2 * hid + classes]
            g_rest = [g[:, : 2 * hid] for g in grads[1:]]
            sq_rest = [g * g + SQUARE_EPS for g in g_rest]
            sq_head = g_head * g_head + SQUARE_EPS
            head_row_new = 0.5 * head_row + 0.5 * jnp.mean(sq_head, axis=1)
            ends = jnp.concatenate(
                [jnp.sum(head_row_new, keepdims=True).reshape(1, 1), jnp.sum(loss, keepdims=True).reshape(1, 1)], axis=1
            )
            row = jnp.concatenate([dbias, jnp.sum(sq_head, axis=0, keepdims=True), ends], axis=1)
            row = jnp.pad(row, ((0, 0), (0, wide - row.shape[1])))
            squares = [jnp.sum(sq, axis=0, keepdims=True) for sq in sq_rest]
            squares = [sq[:, c : c + wide] for sq in squares for c in range(0, 2 * hid, wide)]
            rows = jnp.concatenate(d_norms[1:] + squares + [row], axis=0)
            sums = (jnp.pad(rows, ((0, -(rows.shape[0] + 2) % 16), (0, 0))),)
        outs = layer_backward(
            layer, near, far, boundary, pre, hidden, agg, counts, norm_params, perm, weights, sums
        )
        dw = outs[0]
        if layer:
            d_norms[layer] = outs[1]
            ds, da = outs[2:]

    extra = dw.shape[0] - hid
    last = len(rounds) - 1
    for i, (low, size) in enumerate(rounds):
        sums = dw[-extra:]
        keep = cut(dw[:-extra], size)
        if i == last:
            keep = [jnp.concatenate([keep[p ^ d] for p in range(size)], axis=0) for d in range(size)]
        dw = add_up(swap([jnp.concatenate([part, sums], axis=0) for part in keep], low, total))
    sums, dw = dw[-extra:], dw[:-extra]
    first_sums = add_up([jnp.sum(block * block + SQUARE_EPS, axis=0, keepdims=True) for block in cut(dw, rounds[last][1])])
    for i, (low, size) in enumerate(rounds[:last]):
        mask = 1
        while mask < size:
            first_sums = first_sums + hop(first_sums, mask << low, total)
            if not i:
                sums = after(sums, first_sums)
            mask *= 2
    g_wide = dw[:cols_own]
    g_first = jnp.concatenate([g_wide[:, :f_in], g_wide[:, f_wide : f_wide + f_in]], axis=1)
    first_sums = jnp.concatenate([first_sums[0, :f_in], first_sums[0, f_wide : f_wide + f_in]])
    sq_first = g_first * g_first + SQUARE_EPS
    g_rest = jnp.stack(g_rest)
    sq_rest = jnp.stack(sq_rest)

    g_norms = sums[: 2 * depth].reshape(norm_params.shape)
    at = 2 * depth
    tall = (depth - 1) * 2 * hid // wide
    rest_sums = sums[at : at + tall].reshape(rest_row.shape)
    row = sums[at + tall]
    g_bias = row[:classes]
    head_sums = row[classes : 2 * classes]
    head_row_mean = row[2 * classes] / hid
    loss_sum = row[2 * classes + 1]

    first_row_new = 0.5 * first_row + 0.5 * first_sums / hid
    first_col_new = 0.5 * first_col + 0.5 * jnp.mean(sq_first, axis=1)
    rest_row_new = 0.5 * rest_row + 0.5 * rest_sums / hid
    rest_col_new = 0.5 * rest_col + 0.5 * jnp.mean(sq_rest, axis=2)
    head_col_new = 0.5 * head_col + 0.5 * head_sums / hid
    first_new = factored_step(first_t, g_first, first_row_new, first_col_new, jnp.mean(first_row_new))
    rest_new = factored_step(rest_t, g_rest, rest_row_new, rest_col_new, jnp.mean(rest_row_new, axis=1))
    head_new = head_weight - LEARN_RATE * g_head * lax.rsqrt(
        head_row_new[:, None] * head_col_new[None, :] / head_row_mean
    )
    norm_new, norm_state_new = vector_step(norm_params, g_norms, norm_state)
    bias_new, bias_state_new = vector_step(head_bias, g_bias, bias_state)
    first_new = first_new.T
    rest_new = jnp.swapaxes(rest_new, 1, 2)
    return (
        loss_sum,
        label_count[0, 0],
        first_new,
        rest_new,
        head_new,
        norm_new,
        bias_new,
        g_first.T,
        jnp.swapaxes(g_rest, 1, 2),
        g_head,
        g_norms,
        g_bias,
        first_row_new,
        first_col_new,
        rest_row_new,
        rest_col_new,
        head_row_new,
        head_col_new,
        norm_state_new,
        bias_state_new,
        first_new.astype(BF),
        rest_new.astype(BF),
        head_new.astype(BF),
        norm_new.astype(BF),
    )


def solution(mesh):
    placed = (
        P("dom", None),
        P("dom"),
        P("dom"),
        P(None, "dom"),
        P(None, "dom", None),
        P(None, "dom"),
        P(None, "dom"),
        P(None, None, "dom"),
        P("dom", None),
        P(),
        P(),
        P(),
        P("dom"),
        P(),
        P(None, "dom"),
        P("dom"),
        P(),
        P(),
        P(),
    )
    return jax.shard_map(
        functools.partial(on_device, total=mesh.shape["dom"]),
        mesh=mesh,
        in_specs=placed,
        out_specs=(
            P(),
            P(),
            P(None, "dom"),
            P(None, None, "dom"),
            P("dom", None),
            P(),
            P(),
            P(None, "dom"),
            P(None, None, "dom"),
            P("dom", None),
            P(),
            P(),
            P(),
            P("dom"),
            P(),
            P(None, "dom"),
            P("dom"),
            P(),
            P(),
            P(),
            P(None, "dom"),
            P(None, None, "dom"),
            P("dom", None),
            P(),
        ),
        check_vma=False,
    )
```

```python
import functools

import jax
import jax.numpy as jnp
from jax import lax
from jax.experimental import pallas as pl
from jax.experimental.pallas import tpu as pltpu
from jax.sharding import PartitionSpec as P

LEARN_RATE = 0.03
VECTOR_RATE = 0.25
SQUARE_EPS = 1e-30
NORM_EPS = 1e-05

BF = jnp.bfloat16
F32 = jnp.float32
F8 = jnp.float8_e4m3fn
I32 = jnp.int32

D00 = (((0,), (0,)), ((), ()))
D11 = (((1,), (1,)), ((), ()))
D10 = (((1,), (0,)), ((), ()))

LO = 256
NEAR_NODES = 512
FAR_NODES = 1024
GROUP_NODES = 16
FWD_NODES = 1024
LOWER_NODES = 1024
BWD_COLS = 1024
VMEM_LIMIT = 26 << 20


def mm(left, right, dims):
    return lax.dot_general(left, right, dims, preferred_element_type=F32)


def iota(shape, dim):
    return lax.broadcasted_iota(I32, shape, dim)


def params(bnd_total=0):
    return pltpu.CompilerParams(vmem_limit_bytes=VMEM_LIMIT if bnd_total <= 4096 else 60 << 20)


def in_hbm(value):
    return pltpu.with_memory_space_constraint(value, pltpu.HBM)


def whole(shape):
    return pl.BlockSpec(shape, lambda i: (0,) * len(shape))


def hop(value, mask, total):
    return lax.ppermute(value, "dom", [(i, i ^ mask) for i in range(total)])


def bit_groups(total):
    bits = total.bit_length() - 1
    groups = [(0, 2)]
    at = 1
    while at < bits:
        wide = min(2, bits - at)
        groups.append((at, 1 << wide))
        at += wide
    return groups[::-1]


def place(relative, total):
    out, scale = 0, 1
    for low, size in bit_groups(total):
        out = out + ((relative >> low) & (size - 1)) * scale
        scale *= size
    return out


def after(value, *others):
    return lax.optimization_barrier((value, *others))[0]


def after_all(parts, work):
    return parts if work is None else [after(parts[0], work)] + parts[1:]


def gather_rows(rows, total, works):
    groups = bit_groups(total)
    works = [None] * (len(groups) - len(works)) + list(works)
    for i, (low, size) in enumerate(groups):
        got = [hop(rows, d << low, total) for d in range(1, size)]
        done = works[i](rows) if works[i] else rows
        if i == len(groups) - 1:
            return rows, got[0]
        rows = after(jnp.concatenate([rows] + got, axis=0), done)


def cut(rows, size):
    step = rows.shape[0] // size
    return [rows[d * step : (d + 1) * step] for d in range(size)]


def swap(parts, low, total):
    return [parts[0]] + [hop(part, d << low, total) for d, part in enumerate(parts) if d]


def add_up(parts):
    kind = parts[0].dtype
    parts = [part.astype(F32) for part in parts]
    while len(parts) > 1:
        parts = [parts[i] + parts[i + 1] for i in range(0, len(parts), 2)]
    return parts[0].astype(kind)


def first_kernel(feat_ref, brow_ref, first_ref, rest_ref, head_ref, mask_ref, hid_ref, out_ref, rows_ref):
    f_in, nodes = feat_ref.shape
    own = brow_ref.shape[1]
    cols, classes = head_ref.shape
    turned = feat_ref[...].astype(BF)
    eye = (iota((f_in, 128), 0) == iota((f_in, 128), 1)).astype(F32).astype(BF)
    hid_ref[...] = mm(turned, eye, D00).astype(BF)
    hot = (iota((nodes, own), 0) == brow_ref[0:1, :]).astype(F32).astype(BF)
    rows_ref[...] = jnp.zeros_like(rows_ref)
    rows_ref[0:own, :] = mm(mm(turned, hot, D10).astype(BF), eye, D00)
    at = own
    rows_ref[at : at + cols, 0:f_in] = first_ref[:, 0:f_in]
    rows_ref[at + cols : at + 2 * cols, 0:f_in] = first_ref[:, f_in : 2 * f_in]
    at += 2 * cols
    for k in range(rest_ref.shape[0]):
        for c in range(0, rest_ref.shape[2], 128):
            rows_ref[at : at + cols, :] = rest_ref[k, :, c : c + 128]
            at += cols
    rows_ref[at : at + cols, 0:classes] = head_ref[...]
    at += cols
    count = jnp.sum(mask_ref[...].astype(F32), axis=1, keepdims=True)
    high = jnp.floor(count * (1.0 / 64.0))
    lane = iota((1, 128), 1)
    rows_ref[at : at + 1, :] = jnp.where(lane == 0, high, jnp.where(lane == 1, count - 64.0 * high, 0.0))
    out_ref[...] = rows_ref[...].astype(BF)


def first_message(feat_t, boundary, first_t, rest_t, head_weight, live):
    own = boundary.shape[1]
    cols = head_weight.shape[0]
    tiles = 3 + rest_t.shape[0] * rest_t.shape[2] // 128
    rows = -(-(own + tiles * cols + 1) // 16) * 16
    return pl.pallas_call(
        first_kernel,
        out_shape=[jax.ShapeDtypeStruct((feat_t.shape[1], 128), BF), jax.ShapeDtypeStruct((rows, 128), BF)],
        scratch_shapes=[pltpu.VMEM((rows, 128), F32)],
        compiler_params=params(),
        name="first_message",
    )(*map(in_hbm, (feat_t, boundary, first_t, rest_t, head_weight, live))), tiles


def one_hots(ids, base_ref, low_ref):
    slots, nodes = ids.shape
    high = (ids >> 8).astype(F32).astype(BF)
    low = (ids & 255).astype(F32).astype(BF)
    width = slots * GROUP_NODES
    widen = (iota((slots, width), 0) == iota((slots, width), 1) // GROUP_NODES).astype(F32).astype(BF)
    same = iota((nodes, width), 0) % GROUP_NODES == iota((nodes, width), 1) % GROUP_NODES
    base_ref[...] = jnp.where(same, mm(high, widen, D00), -1.0).astype(BF)
    low_ref[...] = jnp.where(same, mm(low, widen, D00), 0.0)


def count_rows(start, groups, blocks, base_ref, low_ref, outs, kinds):
    width = base_ref.shape[1]
    low_iota = iota((LO, width), 0).astype(F32).astype(BF)
    one = jnp.ones((), BF)
    zero = jnp.zeros((), BF)
    sums = []
    for g in range(groups):
        rows = pl.ds(start + g * GROUP_NODES, GROUP_NODES)
        base = base_ref[rows, :]
        low_row = jnp.sum(low_ref[rows, :], axis=0, keepdims=True).astype(BF)
        right = jnp.where(low_row == low_iota, one, zero)
        left = jnp.concatenate([jnp.where(base == jnp.asarray(h, BF), one, zero) for h in range(blocks)], axis=0)
        sums.append(mm(left, right, D11))
    for h in range(blocks):
        rows = jnp.concatenate([part[h * GROUP_NODES : (h + 1) * GROUP_NODES] for part in sums], axis=0)
        for out, kind in zip(outs, kinds):
            out[pl.ds(start, groups * GROUP_NODES), h * LO : (h + 1) * LO] = rows.astype(kind)


def live_ids(ids_ref, cnt_ref, layer):
    slots, nodes = ids_ref.shape[1:]
    return jnp.where(iota((slots, nodes), 0) < cnt_ref[layer : layer + 1, :], ids_ref[0], -1)


def all_rows(nodes, blocks, base_ref, low_ref, outs, kinds):
    step = 2 * GROUP_NODES
    if blocks <= 32:
        for start in range(0, nodes, step):
            count_rows(start, 2, blocks, base_ref, low_ref, outs, kinds)
    else:

        def body(i, carry):
            count_rows(pl.multiple_of(i * step, step), 2, blocks, base_ref, low_ref, outs, kinds)
            return carry

        lax.fori_loop(0, nodes // step, body, 0)


def far_kernel(me_ref, ids_ref, cnt_ref, out_ref, base_ref, low_ref, *, layer, total, own, node_total):
    ids = live_ids(ids_ref, cnt_ref, layer)
    table = ids - node_total
    moved = place((table // own) ^ me_ref[0], total) * own + table % own
    one_hots(jnp.where(table < 0, -1, moved), base_ref, low_ref)
    all_rows(ids.shape[1], out_ref.shape[1] // LO, base_ref, low_ref, [out_ref], [F8])


def build_specs(slots, depth, nodes, layer):
    return [
        pl.BlockSpec((1, slots, nodes), lambda i: (layer, 0, i)),
        pl.BlockSpec((depth, nodes), lambda i: (0, i)),
    ]


def build_far(me, ids, counts, layer, total, own):
    depth, slots, node_total = ids.shape
    cols = total * own
    nodes = FAR_NODES if cols <= 8192 else 128
    width = slots * GROUP_NODES
    return pl.pallas_call(
        functools.partial(far_kernel, layer=layer, total=total, own=own, node_total=node_total),
        grid=(node_total // nodes,),
        in_specs=[pl.BlockSpec(memory_space=pltpu.SMEM)] + build_specs(slots, depth, nodes, layer),
        out_specs=pl.BlockSpec((nodes, cols), lambda i: (i, 0)),
        out_shape=pltpu.HBM((node_total, cols), F8),
        scratch_shapes=[pltpu.VMEM((nodes, width), BF), pltpu.VMEM((nodes, width), F32)],
        compiler_params=params(),
        cost_estimate=pl.CostEstimate(
            flops=2 * node_total * cols * 256, bytes_accessed=node_total * cols, transcendentals=0
        ),
        name="build_far",
    )(me, in_hbm(ids), in_hbm(counts))


def near_kernel(ids_ref, cnt_ref, table_ref, part_ref, *refs, layer):
    *a_ref, base_ref, low_ref, rows_ref = refs
    one_hots(live_ids(ids_ref, cnt_ref, layer), base_ref, low_ref)
    nodes, cols = rows_ref.shape
    all_rows(nodes, cols // LO, base_ref, low_ref, [rows_ref, *a_ref], [BF, F8])
    part_ref[...] = mm(rows_ref[...], table_ref[...], D10)


def near_step(ids, counts, table, layer):
    depth, slots, node_total = ids.shape
    feat = table.shape[1]
    nodes = NEAR_NODES
    width = slots * GROUP_NODES
    return pl.pallas_call(
        functools.partial(near_kernel, layer=layer),
        grid=(node_total // nodes,),
        in_specs=build_specs(slots, depth, nodes, layer) + [whole((node_total, feat))],
        out_specs=[
            pl.BlockSpec((nodes, feat), lambda i: (i, 0)),
            pl.BlockSpec((nodes, node_total), lambda i: (i, 0)),
        ][: 1 + (layer > 0)],
        out_shape=[
            jax.ShapeDtypeStruct((node_total, feat), F32),
            pltpu.HBM((node_total, node_total), F8),
        ][: 1 + (layer > 0)],
        scratch_shapes=[
            pltpu.VMEM((nodes, width), BF),
            pltpu.VMEM((nodes, width), F32),
            pltpu.VMEM((nodes, node_total), BF),
        ],
        compiler_params=params(),
        cost_estimate=pl.CostEstimate(
            flops=4 * node_total * node_total * 256, bytes_accessed=node_total * node_total, transcendentals=0
        ),
        name="near_step",
    )(in_hbm(ids), in_hbm(counts), table)


def columns(rows, width):
    nodes = rows[0].shape[1]
    pick = iota((16, nodes), 0)
    stacked = jnp.zeros((16, nodes), F32)
    for r, row in enumerate(rows):
        stacked = jnp.where(pick == r, row.astype(F32), stacked)
    stacked = stacked.astype(BF)
    outs = []
    for r in range(len(rows)):
        take = (iota((16, width), 0) == r).astype(F32).astype(BF)
        outs.append(mm(stacked, take, D00))
    return outs


def count_inverse(counts, width):
    (count,) = columns([counts], 128)
    return jnp.concatenate([1.0 / count] * (width // 128), axis=1)


def normalise(pre):
    centre = pre - jnp.mean(pre, axis=1, keepdims=True)
    inv = lax.rsqrt(jnp.mean(centre * centre, axis=1, keepdims=True) + NORM_EPS)
    return centre * inv, inv


def row_hot(brow, start, nodes):
    return (iota((nodes, brow.shape[1]), 0) + start == brow).astype(F32).astype(BF)


def in_turn(a_hbm, near_ref, far_ref, sum_ref, slots_ref, sems, finish):
    rows = slots_ref.shape[1]
    total = a_hbm.shape[0] // rows
    half = near_ref.shape[0]

    def at(i):
        return pl.ds(pl.multiple_of(i * rows, rows), rows)

    def fetch(i):
        slot = i % 2
        return pltpu.make_async_copy(a_hbm.at[at(i), :], slots_ref.at[slot], sems.at[slot])

    def sums(i):
        held = slots_ref.at[i % 2]
        part = mm(held[:, :half].astype(BF), near_ref[...], D10)
        sum_ref[...] = part + mm(held[:, half:].astype(BF), far_ref[...], D10)

    fetch(0).start()
    fetch(1).start()
    fetch(0).wait()
    sums(0)

    def body(i, carry):
        @pl.when(i + 1 < total)
        def _():
            fetch(i + 1).start()

        fetch(i).wait()
        finish(at(i - 1), sum_ref[...])
        sums(i)
        return carry

    lax.fori_loop(1, total, body, 0)
    finish(at(total - 1), sum_ref[...])


def before_norm(hidden, agg, weights_ref, layer):
    w_self, w_neigh = layer_weights(weights_ref, hidden.shape[1], layer)
    return mm(hidden, w_self, D11) + mm(agg, w_neigh, D11)


def forward_block(rows, summed, part_ref, hid_ref, cnt_ref, weights_ref, norm_ref, layer):
    feat = hid_ref.shape[1]
    hid = weights_ref.shape[0]
    share = count_inverse(cnt_ref[layer : layer + 1, rows], feat)
    agg = ((part_ref[rows, :] + summed) * share).astype(BF)
    unit, inv = normalise(before_norm(hid_ref[rows, :], agg, weights_ref, layer))
    y = unit * norm_ref[layer, 0:1, :] + norm_ref[layer, 1:2, :]
    return agg, unit, inv, y, share


def layer_kernel(
    a_hbm, near_ref, far_ref, part_ref, hid_ref, cnt_ref, weights_ref, norm_ref, brow_ref,
    next_ref, agg_ref, pub_ref, acc_ref, sum_ref, slots_ref, sems, *, layer
):
    acc_ref[...] = jnp.zeros_like(acc_ref)

    def finish(rows, summed):
        agg, _, _, y, _ = forward_block(
            rows, summed, part_ref, hid_ref, cnt_ref, weights_ref, norm_ref, layer
        )
        agg_ref[rows, :] = agg
        new = (y * jax.nn.sigmoid(y)).astype(BF)
        next_ref[rows, :] = new
        hot = row_hot(brow_ref[layer + 1 : layer + 2, :], rows.start, rows.size)
        acc_ref[...] += mm(hot, new, D00)

    in_turn(a_hbm, near_ref, far_ref, sum_ref, slots_ref, sems, finish)
    pub_ref[...] = acc_ref[...].astype(BF)


def weight_columns(layer, hid, first_wide):
    return 0 if layer == 0 else 2 * first_wide + 2 * hid * (layer - 1)


def layer_weights(weights_ref, feat, layer):
    at = weight_columns(layer, weights_ref.shape[0], weights_ref.shape[0] // 2)
    return weights_ref[:, at : at + feat], weights_ref[:, at + feat : at + 2 * feat]


def block_rows(bnd_total):
    return FWD_NODES if bnd_total <= 4096 else 128


def turn_scratch(bnd_total, feat):
    rows = block_rows(bnd_total)
    return [
        pltpu.VMEM((rows, feat), F32),
        pltpu.VMEM((2, rows, bnd_total), F8),
        pltpu.SemaphoreType.DMA((2,)),
    ]


HBM_SPEC = pl.BlockSpec(memory_space=pl.ANY)
VMEM_SPEC = pl.BlockSpec(memory_space=pltpu.VMEM)


def layer_forward(layer, a_bnd, shared, part, hidden, counts, weights, norms, boundary):
    node_total, feat = hidden.shape
    bnd_total = a_bnd.shape[1]
    hid = weights.shape[0]
    own = boundary.shape[1]
    return pl.pallas_call(
        functools.partial(layer_kernel, layer=layer),
        in_specs=[HBM_SPEC] + [VMEM_SPEC] * 8,
        out_specs=[VMEM_SPEC] * 3,
        out_shape=[
            jax.ShapeDtypeStruct((node_total, hid), BF),
            jax.ShapeDtypeStruct((node_total, feat), BF),
            jax.ShapeDtypeStruct((own, hid), BF),
        ],
        scratch_shapes=[pltpu.VMEM((own, hid), F32)] + turn_scratch(bnd_total, feat),
        compiler_params=params(bnd_total),
        cost_estimate=pl.CostEstimate(
            flops=2 * node_total * (bnd_total + 1024) * 256,
            bytes_accessed=node_total * (bnd_total + 4096),
            transcendentals=0,
        ),
        name="layer_step",
    )(in_hbm(a_bnd), *shared, part, hidden, counts, weights, norms, boundary)


def backward_block(d_hidden, unit, inv, y, gain):
    sig = jax.nn.sigmoid(y)
    d_out = d_hidden * sig * (1.0 + y * (1.0 - sig))
    d_gain = jnp.sum(d_out * unit, axis=0, keepdims=True)
    d_shift = jnp.sum(d_out, axis=0, keepdims=True)
    d_unit = d_out * gain
    d_pre = inv * (
        d_unit
        - jnp.mean(d_unit, axis=1, keepdims=True)
        - unit * jnp.mean(d_unit * unit, axis=1, keepdims=True)
    )
    return d_pre.astype(BF), d_gain, d_shift


def add_weight_sums(dw_ref, dnorm_ref, d_pre, hidden, agg, d_gain, d_shift):
    feat = hidden.shape[1]
    hid = d_pre.shape[1]
    dw_ref[0:hid, 0:feat] += mm(d_pre, hidden, D00)
    dw_ref[0:hid, feat : 2 * feat] += mm(d_pre, agg, D00)
    dnorm_ref[0:1, :] += d_gain
    dnorm_ref[1:2, :] += d_shift


def into_places(dw_ref, perm_ref):
    perm = perm_ref[...]
    rows = slice(0, perm.shape[0])
    rest = dw_ref[rows, :]
    moved = jnp.zeros_like(rest)
    for _ in range(3):
        term = rest.astype(BF)
        moved = moved + mm(perm, term, D00)
        rest = rest - term.astype(F32)
    dw_ref[rows, :] = moved


def top_kernel(
    a_hbm, near_ref, far_ref, part_ref, hid_ref, cnt_ref, weights_ref, norm_ref,
    lab_ref, mask_ref, marks_ref, bias_ref, perm_ref,
    ds_ref, da_ref, dw_ref, dnorm_ref, dbias_ref, loss_ref, label_ref, sum_ref, slots_ref, sems, *, layer
):
    feat = hid_ref.shape[1]
    hid = weights_ref.shape[0]
    classes = bias_ref.shape[1]
    for ref in (dw_ref, dnorm_ref, dbias_ref, loss_ref):
        ref[...] = jnp.zeros_like(ref)
    marks = jnp.sum(marks_ref[...], axis=0, keepdims=True)
    label_ref[...] = 64.0 * marks[:, 0:1] + marks[:, 1:2]
    head_at = weight_columns(layer + 1, hid, hid // 2)

    def finish(rows, summed):
        agg, unit, inv, y, share = forward_block(
            rows, summed, part_ref, hid_ref, cnt_ref, weights_ref, norm_ref, layer
        )
        head = weights_ref[:, head_at : head_at + 128][:, :classes]
        top = (y * jax.nn.sigmoid(y)).astype(BF)
        logits = mm(top, head, D10) + bias_ref[...]
        label, live = columns([lab_ref[:, rows], mask_ref[:, rows]], classes)
        peak = jnp.max(logits, axis=1, keepdims=True)
        log_total = peak + jnp.log(jnp.sum(jnp.exp(logits - peak), axis=1, keepdims=True))
        hot = label == iota(label.shape, 1).astype(F32)
        loss_ref[...] += jnp.sum(jnp.where(hot, live * (log_total - logits), 0.0), axis=0, keepdims=True)
        probs = jnp.exp(logits - log_total)
        d_logits = ((probs - hot.astype(F32)) * live / label_ref[...]).astype(BF)
        dbias_ref[...] += jnp.sum(d_logits.astype(F32), axis=0, keepdims=True)
        d_hidden = mm(d_logits, head, D11)
        d_pre, d_gain, d_shift = backward_block(d_hidden, unit, inv, y, norm_ref[layer, 0:1, :])
        add_weight_sums(dw_ref, dnorm_ref, d_pre, hid_ref[rows, :], agg, d_gain, d_shift)
        dw_ref[:, 2 * feat : 2 * feat + classes] += mm(top, d_logits, D00)
        w_self, w_neigh = layer_weights(weights_ref, feat, layer)
        ds_ref[rows, :] = mm(d_pre, w_self, D10)
        da_ref[rows, :] = (mm(d_pre, w_neigh, D10) * share).astype(BF)

    in_turn(a_hbm, near_ref, far_ref, sum_ref, slots_ref, sems, finish)
    into_places(dw_ref, perm_ref)


def top_layer(layer, marks, a_bnd, shared, part, hidden, counts, weights, norms, labels, live, bias, perm):
    node_total, feat = hidden.shape
    bnd_total = a_bnd.shape[1]
    hid = weights.shape[0]
    classes = bias.shape[1]
    return pl.pallas_call(
        functools.partial(top_kernel, layer=layer),
        in_specs=[HBM_SPEC] + [VMEM_SPEC] * 12,
        out_specs=[VMEM_SPEC] * 7,
        out_shape=[
            jax.ShapeDtypeStruct((node_total, feat), F32),
            jax.ShapeDtypeStruct((node_total, feat), BF),
            jax.ShapeDtypeStruct((hid, 3 * hid), F32),
            jax.ShapeDtypeStruct((2, hid), F32),
            jax.ShapeDtypeStruct((1, classes), F32),
            jax.ShapeDtypeStruct((1, classes), F32),
            jax.ShapeDtypeStruct((1, 1), F32),
        ],
        scratch_shapes=turn_scratch(bnd_total, feat),
        compiler_params=params(bnd_total),
        cost_estimate=pl.CostEstimate(
            flops=2 * node_total * (bnd_total + 3072) * 256,
            bytes_accessed=node_total * (bnd_total + 4096),
            transcendentals=0,
        ),
        name="top_step",
    )(in_hbm(a_bnd), *shared, part, hidden, counts, weights, norms, labels, live, marks, bias, perm)


def lower_kernel(
    near_ref, dshared_ref, brow_ref, hid_ref, agg_ref, cnt_ref, norm_ref, perm_ref, weights_ref,
    *refs, layer
):
    node_total, hid = near_ref.shape
    feat = hid_ref.shape[1]
    if layer:
        dw_ref, dnorm_ref, ds_ref, da_ref = refs
    else:
        sums_ref, dw_ref, dnorm_ref = refs
    dw_ref[...] = jnp.zeros_like(dw_ref)
    dnorm_ref[...] = jnp.zeros_like(dnorm_ref)
    gain = norm_ref[layer, 0:1, :]
    shared = dshared_ref[...]
    shared_top = shared.astype(BF)
    shared_rest = (shared - shared_top.astype(F32)).astype(BF)

    def block(i, carry):
        rows = pl.ds(pl.multiple_of(i * LOWER_NODES, LOWER_NODES), LOWER_NODES)
        hot = row_hot(brow_ref[layer + 1 : layer + 2, :], rows.start, LOWER_NODES)
        d_hidden = near_ref[rows, :] + mm(hot, shared_top, D10) + mm(hot, shared_rest, D10)
        hidden = hid_ref[rows, :]
        agg = agg_ref[rows, :]
        unit, inv = normalise(before_norm(hidden, agg, weights_ref, layer))
        y = unit * gain + norm_ref[layer, 1:2, :]
        d_pre, d_gain, d_shift = backward_block(d_hidden, unit, inv, y, gain)
        add_weight_sums(dw_ref, dnorm_ref, d_pre, hidden, agg, d_gain, d_shift)
        if layer:
            share = count_inverse(cnt_ref[layer : layer + 1, rows], feat)
            w_self, w_neigh = layer_weights(weights_ref, feat, layer)
            ds_ref[rows, :] = mm(d_pre, w_self, D10)
            da_ref[rows, :] = (mm(d_pre, w_neigh, D10) * share).astype(BF)
        return carry

    lax.fori_loop(0, node_total // LOWER_NODES, block, 0, unroll=True)
    into_places(dw_ref, perm_ref)
    if not layer:
        dw_ref[hid : hid + 2, :] = dnorm_ref[...]
        dw_ref[hid + 2 :, :] = sums_ref[...]


def layer_backward(layer, d_near, d_shared, boundary, hidden, agg, counts, norms, perm, weights, sums=()):
    hid = d_near.shape[1]
    node_total, feat = hidden.shape
    tall = hid if layer else hid + 2 + sums[0].shape[0]
    out_shape = [jax.ShapeDtypeStruct((tall, 2 * feat), F32), jax.ShapeDtypeStruct((2, hid), F32)]
    if layer:
        out_shape += [
            jax.ShapeDtypeStruct((node_total, feat), F32),
            jax.ShapeDtypeStruct((node_total, feat), BF),
        ]
    return pl.pallas_call(
        functools.partial(lower_kernel, layer=layer),
        in_specs=[VMEM_SPEC] * (9 + len(sums)),
        out_specs=[VMEM_SPEC] * len(out_shape),
        out_shape=out_shape,
        compiler_params=params(),
        cost_estimate=pl.CostEstimate(
            flops=2 * node_total * 2048 * 256, bytes_accessed=node_total * 6144, transcendentals=0
        ),
        name="lower_step",
    )(d_near, d_shared, boundary, hidden, agg, counts, norms, perm, weights, *sums)


def spread_kernel(a_ref, d_ref, *refs, add):
    total = mm(a_ref[...].astype(BF), d_ref[...], D00)
    if add:
        total = total + refs[0][...]
    refs[-1][...] = total.astype(refs[-1].dtype)


def spread(a, d_rows, extra, kind, first, steps):
    node_total = a.shape[0]
    feat = d_rows.shape[1]
    specs = [pl.BlockSpec((node_total, BWD_COLS), lambda i: (0, i + first)), whole((node_total, feat))]
    specs += [pl.BlockSpec((BWD_COLS, feat), lambda i: (i + first, 0))] * len(extra)
    return pl.pallas_call(
        functools.partial(spread_kernel, add=len(extra) > 0),
        grid=(steps,),
        in_specs=specs,
        out_specs=pl.BlockSpec((BWD_COLS, feat), lambda i: (i, 0)),
        out_shape=jax.ShapeDtypeStruct((steps * BWD_COLS, feat), kind),
        compiler_params=params(),
        cost_estimate=pl.CostEstimate(
            flops=2 * node_total * steps * BWD_COLS * 256,
            bytes_accessed=node_total * steps * BWD_COLS,
            transcendentals=0,
        ),
        name="spread_near" if extra else "spread_far",
    )(in_hbm(a), d_rows, *extra)


def factored_step(weight, gradient, row_new, col_new, row_mean):
    estimate = row_new[..., None, :] * col_new[..., :, None] / row_mean[..., None, None]
    return weight - LEARN_RATE * gradient * lax.rsqrt(estimate)


def vector_step(param, gradient, state):
    state_new = 0.5 * state + 0.5 * (gradient * gradient + SQUARE_EPS)
    return (param - VECTOR_RATE * gradient * lax.rsqrt(state_new), state_new)


def on_device(
    features,
    labels,
    train_mask,
    boundary,
    neighbours,
    counts,
    first_weight,
    rest_weight,
    head_weight,
    norm_params,
    head_bias,
    first_row,
    first_col,
    rest_row,
    rest_col,
    head_row,
    head_col,
    norm_state,
    bias_state,
    *,
    total,
):
    me = lax.axis_index("dom").astype(I32)
    me_ref = me[None]
    depth = norm_params.shape[0]
    own = boundary.shape[1]
    node_total, f_in = features.shape
    hid = norm_params.shape[2]
    classes = head_bias.shape[0]
    cols_own = hid // total if hid >= total else 1

    first_t = first_weight.T
    rest_t = jnp.swapaxes(rest_weight, 1, 2)
    ids = jnp.swapaxes(neighbours, 1, 2)

    col = jnp.arange(hid, dtype=I32)
    position = place((col // cols_own) ^ me, total) * cols_own + col % cols_own
    perm = (position[:, None] == jnp.arange(hid, dtype=I32)[None, :]).astype(BF)

    (hidden, first_rows), tiles = first_message(
        features.T, boundary, first_t, rest_t, head_weight, train_mask[None]
    )
    f_wide = hidden.shape[1]

    tables = [[None, None] for _ in range(depth)]
    parts = [None] * depth

    def beside(layer, table):
        def far(wait):
            tables[layer][1] = build_far(after(me_ref, wait), ids, counts, layer, total, own)
            return tables[layer][1]

        def near(wait):
            parts[layer], *matrix = near_step(ids, counts, after(table, wait), layer)
            tables[layer][0] = matrix[0] if matrix else None
            return parts[layer]

        return [far, near, None]

    got = gather_rows(first_rows, total, beside(0, hidden))
    got = [g.reshape(total // 2, -1, 128) for g in got]
    shared = [g[:, :own].reshape(-1, 128) for g in got]
    both = jnp.concatenate([g[:, own:] for g in got], axis=0)
    packed = both[:, : tiles * cols_own].reshape(total, tiles, cols_own, 128)
    packed = jnp.swapaxes(packed, 1, 2).reshape(hid, tiles * 128)
    packed = mm(perm, packed, D10).astype(BF)
    marks = both[:, tiles * cols_own].astype(F32)
    weights, marks, perm = lax.optimization_barrier((packed, marks, perm))

    saved = []
    for layer in range(depth):
        if layer:
            shared = gather_rows(published, total, beside(layer, hidden))
        a_loc, a_bnd = tables[layer]
        if layer < depth - 1:
            new, agg, published = layer_forward(
                layer, a_bnd, shared, parts[layer], hidden, counts, weights, norm_params, boundary
            )
            saved.append((a_loc, a_bnd, hidden, agg))
            hidden = new
    ds, da, dw, dnorm, dbias, loss, label_count = top_layer(
        depth - 1, marks, a_bnd, shared, parts[-1], hidden, counts, weights, norm_params,
        labels[None], train_mask[None], head_bias[None], perm,
    )
    d_norms = [None] * depth
    d_norms[-1] = dnorm
    grads = [None] * depth
    near_steps = node_total // BWD_COLS
    far_steps = a_bnd.shape[1] // BWD_COLS
    rounds = bit_groups(total)[::-1]
    for layer in reversed(range(depth - 1)):
        low, size = rounds[0]
        dw = swap(cut(dw, size), low, total)
        sent = spread(a_bnd, after(da, dw[0]), (), BF, far_steps // 2, far_steps // 2)
        dw = add_up(after_all(dw, sent))
        arrived = hop(sent, 1, total)
        kept = spread(a_bnd, after(da, sent), (), BF, 0, far_steps // 2)
        far = kept.astype(F32) + arrived.astype(F32)
        near = None
        for low, size in rounds[1:]:
            far, dw = cut(far, size), cut(dw, size)
            edge, width = far[0].shape
            tall = dw[0].shape[0]
            stacks = [
                jnp.concatenate([far[d]] + [dw[d][:, c : c + width] for c in range(0, dw[d].shape[1], width)], axis=0)
                for d in range(size)
            ]
            stacks = swap([stacks[0]] + [stack.astype(BF) for stack in stacks[1:]], low, total)
            if near is None:
                near = spread(a_loc, after(da, stacks[0]), (ds,), F32, 0, near_steps)
                stacks[0] = after(stacks[0], near)
            stack = add_up(stacks)
            far = stack[:edge]
            dw = jnp.concatenate([stack[r : r + tall] for r in range(edge, stack.shape[0], tall)], axis=1)
        grads[layer + 1] = dw
        a_loc, a_bnd, hidden, agg = saved[layer]
        sums = ()
        if not layer:
            wide = 2 * f_wide
            g_head = grads[-1][:, 2 * hid : 2 * hid + classes]
            g_rest = [g[:, : 2 * hid] for g in grads[1:]]
            sq_rest = [g * g + SQUARE_EPS for g in g_rest]
            sq_head = g_head * g_head + SQUARE_EPS
            head_row_new = 0.5 * head_row + 0.5 * jnp.mean(sq_head, axis=1)
            ends = jnp.concatenate(
                [jnp.sum(head_row_new, keepdims=True).reshape(1, 1), jnp.sum(loss, keepdims=True).reshape(1, 1)], axis=1
            )
            row = jnp.concatenate([dbias, jnp.sum(sq_head, axis=0, keepdims=True), ends], axis=1)
            row = jnp.pad(row, ((0, 0), (0, wide - row.shape[1])))
            squares = [jnp.sum(sq, axis=0, keepdims=True) for sq in sq_rest]
            squares = [sq[:, c : c + wide] for sq in squares for c in range(0, 2 * hid, wide)]
            rows = jnp.concatenate(d_norms[1:] + squares + [row], axis=0)
            sums = (jnp.pad(rows, ((0, -(rows.shape[0] + 2) % 16), (0, 0))),)
        outs = layer_backward(
            layer, near, far, boundary, hidden, agg, counts, norm_params, perm, weights, sums
        )
        dw = outs[0]
        if layer:
            d_norms[layer] = outs[1]
            ds, da = outs[2:]

    extra = dw.shape[0] - hid
    last = len(rounds) - 1
    for i, (low, size) in enumerate(rounds):
        sums = dw[-extra:]
        keep = cut(dw[:-extra], size)
        if i == last:
            keep = [jnp.concatenate([keep[p ^ d] for p in range(size)], axis=0) for d in range(size)]
        dw = add_up(swap([jnp.concatenate([part, sums], axis=0) for part in keep], low, total))
    sums, dw = dw[-extra:], dw[:-extra]
    first_sums = add_up([jnp.sum(block * block + SQUARE_EPS, axis=0, keepdims=True) for block in cut(dw, rounds[last][1])])
    for i, (low, size) in enumerate(rounds[:last]):
        mask = 1
        while mask < size:
            first_sums = first_sums + hop(first_sums, mask << low, total)
            if not i:
                sums = after(sums, first_sums)
            mask *= 2
    g_wide = dw[:cols_own]
    g_first = jnp.concatenate([g_wide[:, :f_in], g_wide[:, f_wide : f_wide + f_in]], axis=1)
    first_sums = jnp.concatenate([first_sums[0, :f_in], first_sums[0, f_wide : f_wide + f_in]])
    sq_first = g_first * g_first + SQUARE_EPS
    g_rest = jnp.stack(g_rest)
    sq_rest = jnp.stack(sq_rest)

    g_norms = sums[: 2 * depth].reshape(norm_params.shape)
    at = 2 * depth
    tall = (depth - 1) * 2 * hid // wide
    rest_sums = sums[at : at + tall].reshape(rest_row.shape)
    row = sums[at + tall]
    g_bias = row[:classes]
    head_sums = row[classes : 2 * classes]
    head_row_mean = row[2 * classes] / hid
    loss_sum = row[2 * classes + 1]

    first_row_new = 0.5 * first_row + 0.5 * first_sums / hid
    first_col_new = 0.5 * first_col + 0.5 * jnp.mean(sq_first, axis=1)
    rest_row_new = 0.5 * rest_row + 0.5 * rest_sums / hid
    rest_col_new = 0.5 * rest_col + 0.5 * jnp.mean(sq_rest, axis=2)
    head_col_new = 0.5 * head_col + 0.5 * head_sums / hid
    first_new = factored_step(first_t, g_first, first_row_new, first_col_new, jnp.mean(first_row_new))
    rest_new = factored_step(rest_t, g_rest, rest_row_new, rest_col_new, jnp.mean(rest_row_new, axis=1))
    head_new = head_weight - LEARN_RATE * g_head * lax.rsqrt(
        head_row_new[:, None] * head_col_new[None, :] / head_row_mean
    )
    norm_new, norm_state_new = vector_step(norm_params, g_norms, norm_state)
    bias_new, bias_state_new = vector_step(head_bias, g_bias, bias_state)
    first_new = first_new.T
    rest_new = jnp.swapaxes(rest_new, 1, 2)
    return (
        loss_sum,
        label_count[0, 0],
        first_new,
        rest_new,
        head_new,
        norm_new,
        bias_new,
        g_first.T,
        jnp.swapaxes(g_rest, 1, 2),
        g_head,
        g_norms,
        g_bias,
        first_row_new,
        first_col_new,
        rest_row_new,
        rest_col_new,
        head_row_new,
        head_col_new,
        norm_state_new,
        bias_state_new,
        first_new.astype(BF),
        rest_new.astype(BF),
        head_new.astype(BF),
        norm_new.astype(BF),
    )


def solution(mesh):
    placed = (
        P("dom", None),
        P("dom"),
        P("dom"),
        P(None, "dom"),
        P(None, "dom", None),
        P(None, "dom"),
        P(None, "dom"),
        P(None, None, "dom"),
        P("dom", None),
        P(),
        P(),
        P(),
        P("dom"),
        P(),
        P(None, "dom"),
        P("dom"),
        P(),
        P(),
        P(),
    )
    return jax.shard_map(
        functools.partial(on_device, total=mesh.shape["dom"]),
        mesh=mesh,
        in_specs=placed,
        out_specs=(
            P(),
            P(),
            P(None, "dom"),
            P(None, None, "dom"),
            P("dom", None),
            P(),
            P(),
            P(None, "dom"),
            P(None, None, "dom"),
            P("dom", None),
            P(),
            P(),
            P(),
            P("dom"),
            P(),
            P(None, "dom"),
            P("dom"),
            P(),
            P(),
            P(),
            P(None, "dom"),
            P(None, None, "dom"),
            P("dom", None),
            P(),
        ),
        check_vma=False,
    )
```

```python
import functools

import jax
import jax.numpy as jnp
from jax import lax
from jax.experimental import pallas as pl
from jax.experimental.pallas import tpu as pltpu
from jax.sharding import PartitionSpec as P

LEARN_RATE = 0.03
VECTOR_RATE = 0.25
SQUARE_EPS = 1e-30
NORM_EPS = 1e-05

BF = jnp.bfloat16
F32 = jnp.float32
F8 = jnp.float8_e4m3fn
I32 = jnp.int32

D00 = (((0,), (0,)), ((), ()))
D11 = (((1,), (1,)), ((), ()))
D10 = (((1,), (0,)), ((), ()))

LO = 256
NEAR_NODES = 512
FAR_NODES = 1024
GROUP_NODES = 16
FWD_NODES = 1024
LOWER_NODES = 1024
BWD_COLS = 1024
VMEM_LIMIT = 26 << 20


def mm(left, right, dims):
    return lax.dot_general(left, right, dims, preferred_element_type=F32)


def iota(shape, dim):
    return lax.broadcasted_iota(I32, shape, dim)


def params(bnd_total=0):
    return pltpu.CompilerParams(vmem_limit_bytes=VMEM_LIMIT if bnd_total <= 4096 else 60 << 20)


def in_hbm(value):
    return pltpu.with_memory_space_constraint(value, pltpu.HBM)


def whole(shape):
    return pl.BlockSpec(shape, lambda i: (0,) * len(shape))


def hop(value, mask, total):
    return lax.ppermute(value, "dom", [(i, i ^ mask) for i in range(total)])


def bit_groups(total):
    bits = total.bit_length() - 1
    groups = [(0, 2)]
    at = 1
    while at < bits:
        wide = min(2, bits - at)
        groups.append((at, 1 << wide))
        at += wide
    return groups[::-1]


def place(relative, total):
    out, scale = 0, 1
    for low, size in bit_groups(total):
        out = out + ((relative >> low) & (size - 1)) * scale
        scale *= size
    return out


def after(value, *others):
    return lax.optimization_barrier((value, *others))[0]


def after_all(parts, work):
    return parts if work is None else [after(parts[0], work)] + parts[1:]


def gather_rows(rows, total, works):
    groups = bit_groups(total)
    works = [None] * (len(groups) - len(works)) + list(works)
    for i, (low, size) in enumerate(groups):
        got = [hop(rows, d << low, total) for d in range(1, size)]
        done = works[i](rows) if works[i] else rows
        if i == len(groups) - 1:
            return rows, got[0]
        rows = after(jnp.concatenate([rows] + got, axis=0), done)


def cut(rows, size):
    step = rows.shape[0] // size
    return [rows[d * step : (d + 1) * step] for d in range(size)]


def swap(parts, low, total):
    return [parts[0]] + [hop(part, d << low, total) for d, part in enumerate(parts) if d]


def add_up(parts):
    kind = parts[0].dtype
    parts = [part.astype(F32) for part in parts]
    while len(parts) > 1:
        parts = [parts[i] + parts[i + 1] for i in range(0, len(parts), 2)]
    return parts[0].astype(kind)


def first_kernel(feat_ref, brow_ref, first_ref, rest_ref, head_ref, mask_ref, hid_ref, out_ref, rows_ref):
    f_in, nodes = feat_ref.shape
    own = brow_ref.shape[1]
    cols, classes = head_ref.shape
    turned = feat_ref[...].astype(BF)
    eye = (iota((f_in, 128), 0) == iota((f_in, 128), 1)).astype(F32).astype(BF)
    hid_ref[...] = mm(turned, eye, D00).astype(BF)
    hot = (iota((nodes, own), 0) == brow_ref[0:1, :]).astype(F32).astype(BF)
    rows_ref[...] = jnp.zeros_like(rows_ref)
    rows_ref[0:own, :] = mm(mm(turned, hot, D10).astype(BF), eye, D00)
    at = own
    rows_ref[at : at + cols, 0:f_in] = first_ref[:, 0:f_in]
    rows_ref[at + cols : at + 2 * cols, 0:f_in] = first_ref[:, f_in : 2 * f_in]
    at += 2 * cols
    for k in range(rest_ref.shape[0]):
        for c in range(0, rest_ref.shape[2], 128):
            rows_ref[at : at + cols, :] = rest_ref[k, :, c : c + 128]
            at += cols
    rows_ref[at : at + cols, 0:classes] = head_ref[...]
    at += cols
    count = jnp.sum(mask_ref[...].astype(F32), axis=1, keepdims=True)
    high = jnp.floor(count * (1.0 / 64.0))
    lane = iota((1, 128), 1)
    rows_ref[at : at + 1, :] = jnp.where(lane == 0, high, jnp.where(lane == 1, count - 64.0 * high, 0.0))
    out_ref[...] = rows_ref[...].astype(BF)


def first_message(feat_t, boundary, first_t, rest_t, head_weight, live):
    own = boundary.shape[1]
    cols = head_weight.shape[0]
    tiles = 3 + rest_t.shape[0] * rest_t.shape[2] // 128
    rows = -(-(own + tiles * cols + 1) // 16) * 16
    return pl.pallas_call(
        first_kernel,
        out_shape=[jax.ShapeDtypeStruct((feat_t.shape[1], 128), BF), jax.ShapeDtypeStruct((rows, 128), BF)],
        scratch_shapes=[pltpu.VMEM((rows, 128), F32)],
        compiler_params=params(),
        name="first_message",
    )(*map(in_hbm, (feat_t, boundary, first_t, rest_t, head_weight, live))), tiles


def one_hots(ids, base_ref, low_ref):
    slots, nodes = ids.shape
    high = (ids >> 8).astype(F32).astype(BF)
    low = (ids & 255).astype(F32).astype(BF)
    width = slots * GROUP_NODES
    shift = GROUP_NODES.bit_length() - 1
    widen = (iota((slots, width), 0) == iota((slots, width), 1) >> shift).astype(F32).astype(BF)
    same = iota((1, GROUP_NODES, width), 1) == iota((1, GROUP_NODES, width), 2) & (GROUP_NODES - 1)
    grouped = (nodes // GROUP_NODES, GROUP_NODES, width)
    base = jnp.where(same, mm(high, widen, D00).reshape(grouped), -1.0)
    base_ref[...] = base.reshape(nodes, width).astype(BF)
    low_ref[...] = jnp.where(same, mm(low, widen, D00).reshape(grouped), 0.0).reshape(nodes, width)


def count_rows(start, groups, blocks, base_ref, low_ref, outs, kinds):
    width = base_ref.shape[1]
    low_iota = iota((LO, width), 0).astype(F32).astype(BF)
    one = jnp.ones((), BF)
    zero = jnp.zeros((), BF)
    sums = []
    for g in range(groups):
        rows = pl.ds(start + g * GROUP_NODES, GROUP_NODES)
        base = base_ref[rows, :]
        low_row = jnp.sum(low_ref[rows, :], axis=0, keepdims=True).astype(BF)
        right = jnp.where(low_row == low_iota, one, zero)
        left = jnp.concatenate([jnp.where(base == jnp.asarray(h, BF), one, zero) for h in range(blocks)], axis=0)
        if len(kinds) == 1 and kinds[0] == BF:
            left, right = left.astype(F8), right.astype(F8)
        sums.append(mm(left, right, D11))
    for h in range(blocks):
        rows = jnp.concatenate([part[h * GROUP_NODES : (h + 1) * GROUP_NODES] for part in sums], axis=0)
        for out, kind in zip(outs, kinds):
            out[pl.ds(start, groups * GROUP_NODES), h * LO : (h + 1) * LO] = rows.astype(kind)


def live_ids(ids_ref, cnt_ref, layer):
    slots, nodes = ids_ref.shape[1:]
    return jnp.where(iota((slots, nodes), 0) < cnt_ref[layer : layer + 1, :], ids_ref[0], -1)


def all_rows(nodes, blocks, base_ref, low_ref, outs, kinds):
    step = 2 * GROUP_NODES
    if blocks <= 32:
        for start in range(0, nodes, step):
            count_rows(start, 2, blocks, base_ref, low_ref, outs, kinds)
    else:

        def body(i, carry):
            count_rows(pl.multiple_of(i * step, step), 2, blocks, base_ref, low_ref, outs, kinds)
            return carry

        lax.fori_loop(0, nodes // step, body, 0)


def far_kernel(me_ref, ids_ref, cnt_ref, out_ref, base_ref, low_ref, *, layer, total, own, node_total):
    ids = live_ids(ids_ref, cnt_ref, layer)
    table = ids - node_total
    moved = place((table >> own.bit_length() - 1) ^ me_ref[0], total) * own + (table & own - 1)
    one_hots(jnp.where(table < 0, -1, moved), base_ref, low_ref)
    all_rows(ids.shape[1], out_ref.shape[1] // LO, base_ref, low_ref, [out_ref], [F8])


def build_specs(slots, depth, nodes, layer):
    return [
        pl.BlockSpec((1, slots, nodes), lambda i: (layer, 0, i)),
        pl.BlockSpec((depth, nodes), lambda i: (0, i)),
    ]


def build_far(me, ids, counts, layer, total, own):
    depth, slots, node_total = ids.shape
    cols = total * own
    nodes = FAR_NODES if cols <= 8192 else 128
    width = slots * GROUP_NODES
    return pl.pallas_call(
        functools.partial(far_kernel, layer=layer, total=total, own=own, node_total=node_total),
        grid=(node_total // nodes,),
        in_specs=[pl.BlockSpec(memory_space=pltpu.SMEM)] + build_specs(slots, depth, nodes, layer),
        out_specs=pl.BlockSpec((nodes, cols), lambda i: (i, 0)),
        out_shape=pltpu.HBM((node_total, cols), F8),
        scratch_shapes=[pltpu.VMEM((nodes, width), BF), pltpu.VMEM((nodes, width), F32)],
        compiler_params=params(),
        cost_estimate=pl.CostEstimate(
            flops=2 * node_total * cols * 256, bytes_accessed=node_total * cols, transcendentals=0
        ),
        name="build_far",
    )(me, in_hbm(ids), in_hbm(counts))


def near_kernel(ids_ref, cnt_ref, table_ref, part_ref, *refs, layer):
    *a_ref, base_ref, low_ref, rows_ref = refs
    one_hots(live_ids(ids_ref, cnt_ref, layer), base_ref, low_ref)
    nodes, cols = rows_ref.shape
    all_rows(nodes, cols // LO, base_ref, low_ref, [rows_ref, *a_ref], [BF, F8][: 1 + len(a_ref)])
    part_ref[...] = mm(rows_ref[...], table_ref[...], D10)


def near_step(ids, counts, table, layer):
    depth, slots, node_total = ids.shape
    feat = table.shape[1]
    nodes = NEAR_NODES
    width = slots * GROUP_NODES
    return pl.pallas_call(
        functools.partial(near_kernel, layer=layer),
        grid=(node_total // nodes,),
        in_specs=build_specs(slots, depth, nodes, layer) + [whole((node_total, feat))],
        out_specs=[
            pl.BlockSpec((nodes, feat), lambda i: (i, 0)),
            pl.BlockSpec((nodes, node_total), lambda i: (i, 0)),
        ][: 1 + (layer > 0)],
        out_shape=[
            jax.ShapeDtypeStruct((node_total, feat), F32),
            pltpu.HBM((node_total, node_total), F8),
        ][: 1 + (layer > 0)],
        scratch_shapes=[
            pltpu.VMEM((nodes, width), BF),
            pltpu.VMEM((nodes, width), F32),
            pltpu.VMEM((nodes, node_total), BF),
        ],
        compiler_params=params(),
        cost_estimate=pl.CostEstimate(
            flops=4 * node_total * node_total * 256, bytes_accessed=node_total * node_total, transcendentals=0
        ),
        name="near_step",
    )(in_hbm(ids), in_hbm(counts), table)


def columns(rows, width):
    nodes = rows[0].shape[1]
    pick = iota((16, nodes), 0)
    stacked = jnp.zeros((16, nodes), F32)
    for r, row in enumerate(rows):
        stacked = jnp.where(pick == r, row.astype(F32), stacked)
    stacked = stacked.astype(BF)
    outs = []
    for r in range(len(rows)):
        take = (iota((16, width), 0) == r).astype(F32).astype(BF)
        outs.append(mm(stacked, take, D00))
    return outs


def count_inverse(counts, width):
    (count,) = columns([counts], 128)
    return jnp.concatenate([1.0 / count] * (width // 128), axis=1)


def normalise(pre):
    centre = pre - jnp.mean(pre, axis=1, keepdims=True)
    inv = lax.rsqrt(jnp.mean(centre * centre, axis=1, keepdims=True) + NORM_EPS)
    return centre * inv, inv


def row_hot(brow, start, nodes):
    return (iota((nodes, brow.shape[1]), 0) + start == brow).astype(F32).astype(BF)


def in_turn(a_hbm, near_ref, far_ref, sum_ref, slots_ref, sems, finish):
    rows = slots_ref.shape[1]
    total = a_hbm.shape[0] // rows
    half = near_ref.shape[0]

    def at(i):
        return pl.ds(pl.multiple_of(i * rows, rows), rows)

    def fetch(i):
        slot = i % 2
        return pltpu.make_async_copy(a_hbm.at[at(i), :], slots_ref.at[slot], sems.at[slot])

    def sums(i):
        held = slots_ref.at[i % 2]
        part = mm(held[:, :half].astype(BF), near_ref[...], D10)
        sum_ref[...] = part + mm(held[:, half:].astype(BF), far_ref[...], D10)

    fetch(0).start()
    fetch(1).start()
    fetch(0).wait()
    sums(0)

    def body(i, carry):
        @pl.when(i + 1 < total)
        def _():
            fetch(i + 1).start()

        fetch(i).wait()
        before = sum_ref[...]
        sums(i)
        finish(at(i - 1), before)
        return carry

    lax.fori_loop(1, total, body, 0)
    finish(at(total - 1), sum_ref[...])


def before_norm(hidden, agg, weights_ref, layer):
    w_self, w_neigh = layer_weights(weights_ref, hidden.shape[1], layer)
    return mm(hidden, w_self, D11) + mm(agg, w_neigh, D11)


def forward_block(rows, summed, part_ref, hid_ref, cnt_ref, weights_ref, norm_ref, layer):
    feat = hid_ref.shape[1]
    hid = weights_ref.shape[0]
    share = count_inverse(cnt_ref[layer : layer + 1, rows], feat)
    agg = ((part_ref[rows, :] + summed) * share).astype(BF)
    unit, inv = normalise(before_norm(hid_ref[rows, :], agg, weights_ref, layer))
    y = unit * norm_ref[layer, 0:1, :] + norm_ref[layer, 1:2, :]
    return agg, unit, inv, y, share


def layer_kernel(
    a_hbm, near_ref, far_ref, part_ref, hid_ref, cnt_ref, weights_ref, norm_ref, brow_ref,
    next_ref, agg_ref, pub_ref, acc_ref, sum_ref, slots_ref, sems, *, layer
):
    acc_ref[...] = jnp.zeros_like(acc_ref)

    def finish(rows, summed):
        agg, _, _, y, _ = forward_block(
            rows, summed, part_ref, hid_ref, cnt_ref, weights_ref, norm_ref, layer
        )
        agg_ref[rows, :] = agg
        new = (y * jax.nn.sigmoid(y)).astype(BF)
        next_ref[rows, :] = new
        hot = row_hot(brow_ref[layer + 1 : layer + 2, :], rows.start, rows.size)
        acc_ref[...] += mm(hot, new, D00)

    in_turn(a_hbm, near_ref, far_ref, sum_ref, slots_ref, sems, finish)
    pub_ref[...] = acc_ref[...].astype(BF)


def weight_columns(layer, hid, first_wide):
    return 0 if layer == 0 else 2 * first_wide + 2 * hid * (layer - 1)


def layer_weights(weights_ref, feat, layer):
    at = weight_columns(layer, weights_ref.shape[0], weights_ref.shape[0] // 2)
    return weights_ref[:, at : at + feat], weights_ref[:, at + feat : at + 2 * feat]


def block_rows(bnd_total):
    return FWD_NODES if bnd_total <= 4096 else 128


def turn_scratch(bnd_total, feat):
    rows = block_rows(bnd_total)
    return [
        pltpu.VMEM((rows, feat), F32),
        pltpu.VMEM((2, rows, bnd_total), F8),
        pltpu.SemaphoreType.DMA((2,)),
    ]


HBM_SPEC = pl.BlockSpec(memory_space=pl.ANY)
VMEM_SPEC = pl.BlockSpec(memory_space=pltpu.VMEM)


def layer_forward(layer, a_bnd, shared, part, hidden, counts, weights, norms, boundary):
    node_total, feat = hidden.shape
    bnd_total = a_bnd.shape[1]
    hid = weights.shape[0]
    own = boundary.shape[1]
    return pl.pallas_call(
        functools.partial(layer_kernel, layer=layer),
        in_specs=[HBM_SPEC] + [VMEM_SPEC] * 8,
        out_specs=[VMEM_SPEC] * 3,
        out_shape=[
            jax.ShapeDtypeStruct((node_total, hid), BF),
            jax.ShapeDtypeStruct((node_total, feat), BF),
            jax.ShapeDtypeStruct((own, hid), BF),
        ],
        scratch_shapes=[pltpu.VMEM((own, hid), F32)] + turn_scratch(bnd_total, feat),
        compiler_params=params(bnd_total),
        cost_estimate=pl.CostEstimate(
            flops=2 * node_total * (bnd_total + 1024) * 256,
            bytes_accessed=node_total * (bnd_total + 4096),
            transcendentals=0,
        ),
        name="layer_step",
    )(in_hbm(a_bnd), *shared, part, hidden, counts, weights, norms, boundary)


def backward_block(d_hidden, unit, inv, y, gain):
    sig = jax.nn.sigmoid(y)
    d_out = d_hidden * sig * (1.0 + y * (1.0 - sig))
    d_gain = jnp.sum(d_out * unit, axis=0, keepdims=True)
    d_shift = jnp.sum(d_out, axis=0, keepdims=True)
    d_unit = d_out * gain
    d_pre = inv * (
        d_unit
        - jnp.mean(d_unit, axis=1, keepdims=True)
        - unit * jnp.mean(d_unit * unit, axis=1, keepdims=True)
    )
    return d_pre.astype(BF), d_gain, d_shift


def add_weight_sums(dw_ref, dnorm_ref, d_pre, hidden, agg, d_gain, d_shift):
    feat = hidden.shape[1]
    hid = d_pre.shape[1]
    dw_ref[0:hid, 0:feat] += mm(d_pre, hidden, D00)
    dw_ref[0:hid, feat : 2 * feat] += mm(d_pre, agg, D00)
    dnorm_ref[0:1, :] += d_gain
    dnorm_ref[1:2, :] += d_shift


def into_places(dw_ref, perm_ref):
    perm = perm_ref[...]
    rows = slice(0, perm.shape[0])
    rest = dw_ref[rows, :]
    moved = jnp.zeros_like(rest)
    for _ in range(3):
        term = rest.astype(BF)
        moved = moved + mm(perm, term, D00)
        rest = rest - term.astype(F32)
    dw_ref[rows, :] = moved


def top_kernel(
    a_hbm, near_ref, far_ref, part_ref, hid_ref, cnt_ref, weights_ref, norm_ref,
    lab_ref, mask_ref, marks_ref, bias_ref, perm_ref,
    ds_ref, da_ref, keep_ref, send_ref, dnorm_ref, dbias_ref, loss_ref, label_ref,
    dw_ref, lost_ref, sum_ref, slots_ref, sems, *, layer
):
    feat = hid_ref.shape[1]
    hid = weights_ref.shape[0]
    classes = bias_ref.shape[1]
    for ref in (dw_ref, dnorm_ref, dbias_ref, lost_ref):
        ref[...] = jnp.zeros_like(ref)
    marks = jnp.sum(marks_ref[...], axis=0, keepdims=True)
    label_ref[...] = 64.0 * marks[:, 0:1] + marks[:, 1:2]
    head_at = weight_columns(layer + 1, hid, hid // 2)

    def finish(rows, summed):
        agg, unit, inv, y, share = forward_block(
            rows, summed, part_ref, hid_ref, cnt_ref, weights_ref, norm_ref, layer
        )
        head = weights_ref[:, head_at : head_at + 128][:, :classes]
        top = (y * jax.nn.sigmoid(y)).astype(BF)
        logits = mm(top, head, D10) + bias_ref[...]
        label, live = columns([lab_ref[:, rows], mask_ref[:, rows]], classes)
        peak = jnp.max(logits, axis=1, keepdims=True)
        log_total = peak + jnp.log(jnp.sum(jnp.exp(logits - peak), axis=1, keepdims=True))
        hot = label == iota(label.shape, 1).astype(F32)
        lost_ref[...] += jnp.sum(jnp.where(hot, live * (log_total - logits), 0.0), axis=0, keepdims=True)
        probs = jnp.exp(logits - log_total)
        d_logits = ((probs - hot.astype(F32)) * live / label_ref[...]).astype(BF)
        dbias_ref[...] += jnp.sum(d_logits.astype(F32), axis=0, keepdims=True)
        d_hidden = mm(d_logits, head, D11)
        d_pre, d_gain, d_shift = backward_block(d_hidden, unit, inv, y, norm_ref[layer, 0:1, :])
        add_weight_sums(dw_ref, dnorm_ref, d_pre, hid_ref[rows, :], agg, d_gain, d_shift)
        dw_ref[:, 2 * feat : 2 * feat + classes] += mm(top, d_logits, D00)
        w_self, w_neigh = layer_weights(weights_ref, feat, layer)
        ds_ref[rows, :] = mm(d_pre, w_self, D10)
        da_ref[rows, :] = (mm(d_pre, w_neigh, D10) * share).astype(BF)

    in_turn(a_hbm, near_ref, far_ref, sum_ref, slots_ref, sems, finish)
    into_places(dw_ref, perm_ref)
    keep_ref[...] = dw_ref[: hid // 2, :]
    send_ref[...] = dw_ref[hid // 2 :, :]
    loss_ref[...] = jnp.sum(lost_ref[...], axis=1, keepdims=True)


def top_layer(layer, marks, a_bnd, shared, part, hidden, counts, weights, norms, labels, live, bias, perm):
    node_total, feat = hidden.shape
    bnd_total = a_bnd.shape[1]
    hid = weights.shape[0]
    classes = bias.shape[1]
    return pl.pallas_call(
        functools.partial(top_kernel, layer=layer),
        in_specs=[HBM_SPEC] + [VMEM_SPEC] * 12,
        out_specs=[VMEM_SPEC] * 8,
        out_shape=[
            jax.ShapeDtypeStruct((node_total, feat), F32),
            jax.ShapeDtypeStruct((node_total, feat), BF),
            jax.ShapeDtypeStruct((hid // 2, 3 * hid), F32),
            jax.ShapeDtypeStruct((hid // 2, 3 * hid), F32),
            jax.ShapeDtypeStruct((2, hid), F32),
            jax.ShapeDtypeStruct((1, classes), F32),
            jax.ShapeDtypeStruct((1, 1), F32),
            jax.ShapeDtypeStruct((1, 1), F32),
        ],
        scratch_shapes=[pltpu.VMEM((hid, 3 * hid), F32), pltpu.VMEM((1, classes), F32)]
        + turn_scratch(bnd_total, feat),
        compiler_params=params(bnd_total),
        cost_estimate=pl.CostEstimate(
            flops=2 * node_total * (bnd_total + 3072) * 256,
            bytes_accessed=node_total * (bnd_total + 4096),
            transcendentals=0,
        ),
        name="top_step",
    )(in_hbm(a_bnd), *shared, part, hidden, counts, weights, norms, labels, live, marks, bias, perm)


def lower_kernel(
    near_ref, dshared_ref, brow_ref, hid_ref, agg_ref, cnt_ref, norm_ref, perm_ref, weights_ref,
    *refs, layer
):
    node_total, hid = near_ref.shape
    feat = hid_ref.shape[1]
    if layer:
        dw_ref, dnorm_ref, ds_ref, da_ref = refs
    else:
        sums_ref, dw_ref, dnorm_ref = refs
    dw_ref[...] = jnp.zeros_like(dw_ref)
    dnorm_ref[...] = jnp.zeros_like(dnorm_ref)
    gain = norm_ref[layer, 0:1, :]
    shared = dshared_ref[...]
    shared_top = shared.astype(BF)
    shared_rest = (shared - shared_top.astype(F32)).astype(BF)

    def block(i, carry):
        rows = pl.ds(pl.multiple_of(i * LOWER_NODES, LOWER_NODES), LOWER_NODES)
        hot = row_hot(brow_ref[layer + 1 : layer + 2, :], rows.start, LOWER_NODES)
        d_hidden = near_ref[rows, :] + mm(hot, shared_top, D10) + mm(hot, shared_rest, D10)
        hidden = hid_ref[rows, :]
        agg = agg_ref[rows, :]
        unit, inv = normalise(before_norm(hidden, agg, weights_ref, layer))
        y = unit * gain + norm_ref[layer, 1:2, :]
        d_pre, d_gain, d_shift = backward_block(d_hidden, unit, inv, y, gain)
        add_weight_sums(dw_ref, dnorm_ref, d_pre, hidden, agg, d_gain, d_shift)
        if layer:
            share = count_inverse(cnt_ref[layer : layer + 1, rows], feat)
            w_self, w_neigh = layer_weights(weights_ref, feat, layer)
            ds_ref[rows, :] = mm(d_pre, w_self, D10)
            da_ref[rows, :] = (mm(d_pre, w_neigh, D10) * share).astype(BF)
        return carry

    lax.fori_loop(0, node_total // LOWER_NODES, block, 0, unroll=True)
    into_places(dw_ref, perm_ref)
    if not layer:
        dw_ref[hid : hid + 2, :] = dnorm_ref[...]
        dw_ref[hid + 2 :, :] = sums_ref[...]


def layer_backward(layer, d_near, d_shared, boundary, hidden, agg, counts, norms, perm, weights, sums=()):
    hid = d_near.shape[1]
    node_total, feat = hidden.shape
    tall = hid if layer else hid + 2 + sums[0].shape[0]
    out_shape = [jax.ShapeDtypeStruct((tall, 2 * feat), F32), jax.ShapeDtypeStruct((2, hid), F32)]
    if layer:
        out_shape += [
            jax.ShapeDtypeStruct((node_total, feat), F32),
            jax.ShapeDtypeStruct((node_total, feat), BF),
        ]
    return pl.pallas_call(
        functools.partial(lower_kernel, layer=layer),
        in_specs=[VMEM_SPEC] * (9 + len(sums)),
        out_specs=[VMEM_SPEC] * len(out_shape),
        out_shape=out_shape,
        compiler_params=params(),
        cost_estimate=pl.CostEstimate(
            flops=2 * node_total * 2048 * 256, bytes_accessed=node_total * 6144, transcendentals=0
        ),
        name="lower_step",
    )(d_near, d_shared, boundary, hidden, agg, counts, norms, perm, weights, *sums)


def spread_kernel(a_ref, d_ref, *refs, add):
    total = mm(a_ref[...].astype(BF), d_ref[...], D00)
    if add:
        total = total + refs[0][...]
    refs[-1][...] = total.astype(refs[-1].dtype)


def spread(a, d_rows, extra, kind, first, steps):
    node_total = a.shape[0]
    feat = d_rows.shape[1]
    specs = [pl.BlockSpec((node_total, BWD_COLS), lambda i: (0, i + first)), whole((node_total, feat))]
    specs += [pl.BlockSpec((BWD_COLS, feat), lambda i: (i + first, 0))] * len(extra)
    return pl.pallas_call(
        functools.partial(spread_kernel, add=len(extra) > 0),
        grid=(steps,),
        in_specs=specs,
        out_specs=pl.BlockSpec((BWD_COLS, feat), lambda i: (i, 0)),
        out_shape=jax.ShapeDtypeStruct((steps * BWD_COLS, feat), kind),
        compiler_params=params(),
        cost_estimate=pl.CostEstimate(
            flops=2 * node_total * steps * BWD_COLS * 256,
            bytes_accessed=node_total * steps * BWD_COLS,
            transcendentals=0,
        ),
        name="spread_near" if extra else "spread_far",
    )(in_hbm(a), d_rows, *extra)


def factored_step(weight, gradient, row_new, col_new, row_mean):
    estimate = row_new[..., None, :] * col_new[..., :, None] / row_mean[..., None, None]
    return weight - LEARN_RATE * gradient * lax.rsqrt(estimate)


def vector_step(param, gradient, state):
    state_new = 0.5 * state + 0.5 * (gradient * gradient + SQUARE_EPS)
    return (param - VECTOR_RATE * gradient * lax.rsqrt(state_new), state_new)


def on_device(
    features,
    labels,
    train_mask,
    boundary,
    neighbours,
    counts,
    first_weight,
    rest_weight,
    head_weight,
    norm_params,
    head_bias,
    first_row,
    first_col,
    rest_row,
    rest_col,
    head_row,
    head_col,
    norm_state,
    bias_state,
    *,
    total,
):
    me = lax.axis_index("dom").astype(I32)
    me_ref = me[None]
    depth = norm_params.shape[0]
    own = boundary.shape[1]
    node_total, f_in = features.shape
    hid = norm_params.shape[2]
    classes = head_bias.shape[0]
    cols_own = hid // total if hid >= total else 1

    first_t = first_weight.T
    rest_t = jnp.swapaxes(rest_weight, 1, 2)
    ids = jnp.swapaxes(neighbours, 1, 2)

    col = jnp.arange(hid, dtype=I32)
    position = place((col // cols_own) ^ me, total) * cols_own + col % cols_own
    perm = (position[:, None] == jnp.arange(hid, dtype=I32)[None, :]).astype(BF)

    (hidden, first_rows), tiles = first_message(
        features.T, boundary, first_t, rest_t, head_weight, train_mask[None]
    )
    f_wide = hidden.shape[1]

    tables = [[None, None] for _ in range(depth)]
    parts = [None] * depth

    def beside(layer, table):
        def far(wait):
            tables[layer][1] = build_far(after(me_ref, wait), ids, counts, layer, total, own)
            return tables[layer][1]

        def near(wait):
            parts[layer], *matrix = near_step(ids, counts, after(table, wait), layer)
            tables[layer][0] = matrix[0] if matrix else None
            return parts[layer]

        return [far, near, None]

    got = gather_rows(first_rows, total, beside(0, hidden))
    got = [g.reshape(total // 2, -1, 128) for g in got]
    shared = [g[:, :own].reshape(-1, 128) for g in got]
    both = jnp.concatenate([g[:, own:] for g in got], axis=0)
    packed = both[:, : tiles * cols_own].reshape(total, tiles, cols_own, 128)
    packed = jnp.swapaxes(packed, 1, 2).reshape(hid, tiles * 128)
    packed = mm(perm, packed, D10).astype(BF)
    marks = both[:, tiles * cols_own].astype(F32)
    weights, marks, perm = lax.optimization_barrier((packed, marks, perm))

    saved = []
    for layer in range(depth):
        if layer:
            shared = gather_rows(published, total, beside(layer, hidden))
        a_loc, a_bnd = tables[layer]
        if layer < depth - 1:
            new, agg, published = layer_forward(
                layer, a_bnd, shared, parts[layer], hidden, counts, weights, norm_params, boundary
            )
            saved.append((a_loc, a_bnd, hidden, agg))
            hidden = new
    ds, da, *dw, dnorm, dbias, loss, label_count = top_layer(
        depth - 1, marks, a_bnd, shared, parts[-1], hidden, counts, weights, norm_params,
        labels[None], train_mask[None], head_bias[None], perm,
    )
    d_norms = [None] * depth
    d_norms[-1] = dnorm
    grads = [None] * depth
    near_steps = node_total // BWD_COLS
    far_steps = a_bnd.shape[1] // BWD_COLS
    rounds = bit_groups(total)[::-1]
    for layer in reversed(range(depth - 1)):
        low, size = rounds[0]
        dw = swap(dw if isinstance(dw, list) else cut(dw, size), low, total)
        sent = spread(a_bnd, after(da, dw[0]), (), BF, far_steps // 2, far_steps // 2)
        dw = add_up(after_all(dw, sent))
        arrived = hop(sent, 1, total)
        kept = spread(a_bnd, after(da, sent), (), BF, 0, far_steps // 2)
        far = kept.astype(F32) + arrived.astype(F32)
        near = None
        for low, size in rounds[1:]:
            far, dw = cut(far, size), cut(dw, size)
            edge, width = far[0].shape
            tall = dw[0].shape[0]
            stacks = [
                jnp.concatenate([far[d]] + [dw[d][:, c : c + width] for c in range(0, dw[d].shape[1], width)], axis=0)
                for d in range(size)
            ]
            stacks = swap([stacks[0]] + [stack.astype(BF) for stack in stacks[1:]], low, total)
            if near is None:
                near = spread(a_loc, after(da, stacks[0]), (ds,), F32, 0, near_steps)
                stacks[0] = after(stacks[0], near)
            stack = add_up(stacks)
            far = stack[:edge]
            dw = jnp.concatenate([stack[r : r + tall] for r in range(edge, stack.shape[0], tall)], axis=1)
        grads[layer + 1] = dw
        a_loc, a_bnd, hidden, agg = saved[layer]
        sums = ()
        if not layer:
            wide = 2 * f_wide
            g_head = grads[-1][:, 2 * hid : 2 * hid + classes]
            g_rest = [g[:, : 2 * hid] for g in grads[1:]]
            sq_rest = [g * g + SQUARE_EPS for g in g_rest]
            sq_head = g_head * g_head + SQUARE_EPS
            head_row_new = 0.5 * head_row + 0.5 * jnp.mean(sq_head, axis=1)
            ends = jnp.concatenate(
                [jnp.sum(head_row_new, keepdims=True).reshape(1, 1), loss], axis=1
            )
            row = jnp.concatenate([dbias, jnp.sum(sq_head, axis=0, keepdims=True), ends], axis=1)
            row = jnp.pad(row, ((0, 0), (0, wide - row.shape[1])))
            squares = [jnp.sum(sq, axis=0, keepdims=True) for sq in sq_rest]
            squares = [sq[:, c : c + wide] for sq in squares for c in range(0, 2 * hid, wide)]
            rows = jnp.concatenate(d_norms[1:] + squares + [row], axis=0)
            sums = (jnp.pad(rows, ((0, -(rows.shape[0] + 2) % 16), (0, 0))),)
        outs = layer_backward(
            layer, near, far, boundary, hidden, agg, counts, norm_params, perm, weights, sums
        )
        dw = outs[0]
        if layer:
            d_norms[layer] = outs[1]
            ds, da = outs[2:]

    extra = dw.shape[0] - hid
    last = len(rounds) - 1
    for i, (low, size) in enumerate(rounds):
        sums = dw[-extra:]
        keep = cut(dw[:-extra], size)
        if i == last:
            keep = [jnp.concatenate([keep[p ^ d] for p in range(size)], axis=0) for d in range(size)]
        dw = add_up(swap([jnp.concatenate([part, sums], axis=0) for part in keep], low, total))
    sums, dw = dw[-extra:], dw[:-extra]
    first_sums = add_up([jnp.sum(block * block + SQUARE_EPS, axis=0, keepdims=True) for block in cut(dw, rounds[last][1])])
    for i, (low, size) in enumerate(rounds[:last]):
        mask = 1
        while mask < size:
            first_sums = first_sums + hop(first_sums, mask << low, total)
            if not i:
                sums = after(sums, first_sums)
            mask *= 2
    g_wide = dw[:cols_own]
    g_first = jnp.concatenate([g_wide[:, :f_in], g_wide[:, f_wide : f_wide + f_in]], axis=1)
    first_sums = jnp.concatenate([first_sums[0, :f_in], first_sums[0, f_wide : f_wide + f_in]])
    sq_first = g_first * g_first + SQUARE_EPS
    g_rest = jnp.stack(g_rest)
    sq_rest = jnp.stack(sq_rest)

    g_norms = sums[: 2 * depth].reshape(norm_params.shape)
    at = 2 * depth
    tall = (depth - 1) * 2 * hid // wide
    rest_sums = sums[at : at + tall].reshape(rest_row.shape)
    row = sums[at + tall]
    g_bias = row[:classes]
    head_sums = row[classes : 2 * classes]
    head_row_mean = row[2 * classes] / hid
    loss_sum = row[2 * classes + 1]

    first_row_new = 0.5 * first_row + 0.5 * first_sums / hid
    first_col_new = 0.5 * first_col + 0.5 * jnp.mean(sq_first, axis=1)
    rest_row_new = 0.5 * rest_row + 0.5 * rest_sums / hid
    rest_col_new = 0.5 * rest_col + 0.5 * jnp.mean(sq_rest, axis=2)
    head_col_new = 0.5 * head_col + 0.5 * head_sums / hid
    first_new = factored_step(first_t, g_first, first_row_new, first_col_new, jnp.mean(first_row_new))
    rest_new = factored_step(rest_t, g_rest, rest_row_new, rest_col_new, jnp.mean(rest_row_new, axis=1))
    head_new = head_weight - LEARN_RATE * g_head * lax.rsqrt(
        head_row_new[:, None] * head_col_new[None, :] / head_row_mean
    )
    norm_new, norm_state_new = vector_step(norm_params, g_norms, norm_state)
    bias_new, bias_state_new = vector_step(head_bias, g_bias, bias_state)
    first_new = first_new.T
    rest_new = jnp.swapaxes(rest_new, 1, 2)
    return (
        loss_sum,
        label_count[0, 0],
        first_new,
        rest_new,
        head_new,
        norm_new,
        bias_new,
        g_first.T,
        jnp.swapaxes(g_rest, 1, 2),
        g_head,
        g_norms,
        g_bias,
        first_row_new,
        first_col_new,
        rest_row_new,
        rest_col_new,
        head_row_new,
        head_col_new,
        norm_state_new,
        bias_state_new,
        first_new.astype(BF),
        rest_new.astype(BF),
        head_new.astype(BF),
        norm_new.astype(BF),
    )


def solution(mesh):
    placed = (
        P("dom", None),
        P("dom"),
        P("dom"),
        P(None, "dom"),
        P(None, "dom", None),
        P(None, "dom"),
        P(None, "dom"),
        P(None, None, "dom"),
        P("dom", None),
        P(),
        P(),
        P(),
        P("dom"),
        P(),
        P(None, "dom"),
        P("dom"),
        P(),
        P(),
        P(),
    )
    return jax.shard_map(
        functools.partial(on_device, total=mesh.shape["dom"]),
        mesh=mesh,
        in_specs=placed,
        out_specs=(
            P(),
            P(),
            P(None, "dom"),
            P(None, None, "dom"),
            P("dom", None),
            P(),
            P(),
            P(None, "dom"),
            P(None, None, "dom"),
            P("dom", None),
            P(),
            P(),
            P(),
            P("dom"),
            P(),
            P(None, "dom"),
            P("dom"),
            P(),
            P(),
            P(),
            P(None, "dom"),
            P(None, None, "dom"),
            P("dom", None),
            P(),
        ),
        check_vma=False,
    )
```

```python
import functools

import jax
import jax.numpy as jnp
from jax import lax
from jax.experimental import pallas as pl
from jax.experimental.pallas import tpu as pltpu
from jax.sharding import PartitionSpec as P

LEARN_RATE = 0.03
VECTOR_RATE = 0.25
SQUARE_EPS = 1e-30
NORM_EPS = 1e-05

BF = jnp.bfloat16
F32 = jnp.float32
F8 = jnp.float8_e4m3fn
I32 = jnp.int32

D00 = (((0,), (0,)), ((), ()))
D11 = (((1,), (1,)), ((), ()))
D10 = (((1,), (0,)), ((), ()))

LO = 256
NEAR_NODES = 512
FAR_NODES = 1024
GROUP_NODES = 16
FWD_NODES = 1024
LOWER_NODES = 2048
BWD_COLS = 1024
VMEM_LIMIT = 26 << 20


def mm(left, right, dims):
    return lax.dot_general(left, right, dims, preferred_element_type=F32)


def iota(shape, dim):
    return lax.broadcasted_iota(I32, shape, dim)


def params(bnd_total=0):
    return pltpu.CompilerParams(vmem_limit_bytes=VMEM_LIMIT if bnd_total <= 4096 else 60 << 20)


def in_hbm(value):
    return pltpu.with_memory_space_constraint(value, pltpu.HBM)


def whole(shape):
    return pl.BlockSpec(shape, lambda i: (0,) * len(shape))


def hop(value, mask, total):
    return lax.ppermute(value, "dom", [(i, i ^ mask) for i in range(total)])


def bit_groups(total):
    bits = total.bit_length() - 1
    groups = [(0, 2)]
    at = 1
    while at < bits:
        wide = min(2, bits - at)
        groups.append((at, 1 << wide))
        at += wide
    return groups[::-1]


def place(relative, total):
    out, scale = 0, 1
    for low, size in bit_groups(total):
        out = out + ((relative >> low) & (size - 1)) * scale
        scale *= size
    return out


def after(value, *others):
    return lax.optimization_barrier((value, *others))[0]


def after_all(parts, work):
    return parts if work is None else [after(parts[0], work)] + parts[1:]


def gather_rows(rows, total, works):
    groups = bit_groups(total)
    works = [None] * (len(groups) - len(works)) + list(works)
    for i, (low, size) in enumerate(groups):
        got = [hop(rows, d << low, total) for d in range(1, size)]
        done = works[i](rows) if works[i] else rows
        if i == len(groups) - 1:
            return rows, got[0]
        rows = after(jnp.concatenate([rows] + got, axis=0), done)


def cut(rows, size):
    step = rows.shape[0] // size
    return [rows[d * step : (d + 1) * step] for d in range(size)]


def swap(parts, low, total):
    return [parts[0]] + [hop(part, d << low, total) for d, part in enumerate(parts) if d]


def add_up(parts):
    kind = parts[0].dtype
    parts = [part.astype(F32) for part in parts]
    while len(parts) > 1:
        parts = [parts[i] + parts[i + 1] for i in range(0, len(parts), 2)]
    return parts[0].astype(kind)


def first_kernel(feat_ref, brow_ref, first_ref, rest_ref, head_ref, mask_ref, hid_ref, out_ref, rows_ref):
    f_in, nodes = feat_ref.shape
    own = brow_ref.shape[1]
    cols, classes = head_ref.shape
    turned = feat_ref[...].astype(BF)
    eye = (iota((f_in, 128), 0) == iota((f_in, 128), 1)).astype(F32).astype(BF)
    hid_ref[...] = mm(turned, eye, D00).astype(BF)
    hot = (iota((nodes, own), 0) == brow_ref[0:1, :]).astype(F32).astype(BF)
    rows_ref[...] = jnp.zeros_like(rows_ref)
    rows_ref[0:own, :] = mm(mm(turned, hot, D10).astype(BF), eye, D00)
    at = own
    rows_ref[at : at + cols, 0:f_in] = first_ref[:, 0:f_in]
    rows_ref[at + cols : at + 2 * cols, 0:f_in] = first_ref[:, f_in : 2 * f_in]
    at += 2 * cols
    for k in range(rest_ref.shape[0]):
        for c in range(0, rest_ref.shape[2], 128):
            rows_ref[at : at + cols, :] = rest_ref[k, :, c : c + 128]
            at += cols
    rows_ref[at : at + cols, 0:classes] = head_ref[...]
    at += cols
    count = jnp.sum(mask_ref[...].astype(F32), axis=1, keepdims=True)
    high = jnp.floor(count * (1.0 / 64.0))
    lane = iota((1, 128), 1)
    rows_ref[at : at + 1, :] = jnp.where(lane == 0, high, jnp.where(lane == 1, count - 64.0 * high, 0.0))
    out_ref[...] = rows_ref[...].astype(BF)


def first_message(feat_t, boundary, first_t, rest_t, head_weight, live):
    own = boundary.shape[1]
    cols = head_weight.shape[0]
    tiles = 3 + rest_t.shape[0] * rest_t.shape[2] // 128
    rows = -(-(own + tiles * cols + 1) // 16) * 16
    return pl.pallas_call(
        first_kernel,
        out_shape=[jax.ShapeDtypeStruct((feat_t.shape[1], 128), BF), jax.ShapeDtypeStruct((rows, 128), BF)],
        scratch_shapes=[pltpu.VMEM((rows, 128), F32)],
        compiler_params=params(),
        name="first_message",
    )(*map(in_hbm, (feat_t, boundary, first_t, rest_t, head_weight, live))), tiles


def one_hots(ids, base_ref, low_ref):
    slots, nodes = ids.shape
    high = (ids >> 8).astype(F32).astype(BF)
    low = (ids & 255).astype(F32).astype(BF)
    width = slots * GROUP_NODES
    shift = GROUP_NODES.bit_length() - 1
    widen = (iota((slots, width), 0) == iota((slots, width), 1) >> shift).astype(F32).astype(BF)
    same = iota((1, GROUP_NODES, width), 1) == iota((1, GROUP_NODES, width), 2) & (GROUP_NODES - 1)
    grouped = (nodes // GROUP_NODES, GROUP_NODES, width)
    base = jnp.where(same, mm(high, widen, D00).reshape(grouped), -1.0)
    base_ref[...] = base.reshape(nodes, width).astype(BF)
    low_ref[...] = jnp.where(same, mm(low, widen, D00).reshape(grouped), 0.0).reshape(nodes, width)


def count_rows(start, groups, blocks, base_ref, low_ref, outs, kinds):
    width = base_ref.shape[1]
    low_iota = iota((LO, width), 0).astype(F32).astype(BF)
    one = jnp.ones((), BF)
    zero = jnp.zeros((), BF)
    sums = []
    for g in range(groups):
        rows = pl.ds(start + g * GROUP_NODES, GROUP_NODES)
        base = base_ref[rows, :]
        low_row = jnp.sum(low_ref[rows, :], axis=0, keepdims=True).astype(BF)
        right = jnp.where(low_row == low_iota, one, zero)
        left = jnp.concatenate([jnp.where(base == jnp.asarray(h, BF), one, zero) for h in range(blocks)], axis=0)
        if len(kinds) == 1 and kinds[0] == BF:
            left, right = left.astype(F8), right.astype(F8)
        sums.append(mm(left, right, D11))
    for h in range(blocks):
        rows = jnp.concatenate([part[h * GROUP_NODES : (h + 1) * GROUP_NODES] for part in sums], axis=0)
        for out, kind in zip(outs, kinds):
            out[pl.ds(start, groups * GROUP_NODES), h * LO : (h + 1) * LO] = rows.astype(kind)


def live_ids(ids_ref, cnt_ref, layer):
    slots, nodes = ids_ref.shape[1:]
    return jnp.where(iota((slots, nodes), 0) < cnt_ref[layer : layer + 1, :], ids_ref[0], -1)


def all_rows(nodes, blocks, base_ref, low_ref, outs, kinds):
    step = 2 * GROUP_NODES
    if blocks <= 32:
        for start in range(0, nodes, step):
            count_rows(start, 2, blocks, base_ref, low_ref, outs, kinds)
    else:

        def body(i, carry):
            count_rows(pl.multiple_of(i * step, step), 2, blocks, base_ref, low_ref, outs, kinds)
            return carry

        lax.fori_loop(0, nodes // step, body, 0)


def far_kernel(me_ref, ids_ref, cnt_ref, out_ref, base_ref, low_ref, *, layer, total, own, node_total):
    ids = live_ids(ids_ref, cnt_ref, layer)
    table = ids - node_total
    moved = place((table >> own.bit_length() - 1) ^ me_ref[0], total) * own + (table & own - 1)
    one_hots(jnp.where(table < 0, -1, moved), base_ref, low_ref)
    all_rows(ids.shape[1], out_ref.shape[1] // LO, base_ref, low_ref, [out_ref], [F8])


def build_specs(slots, depth, nodes, layer):
    return [
        pl.BlockSpec((1, slots, nodes), lambda i: (layer, 0, i)),
        pl.BlockSpec((depth, nodes), lambda i: (0, i)),
    ]


def build_far(me, ids, counts, layer, total, own):
    depth, slots, node_total = ids.shape
    cols = total * own
    nodes = FAR_NODES if cols <= 8192 else 128
    width = slots * GROUP_NODES
    return pl.pallas_call(
        functools.partial(far_kernel, layer=layer, total=total, own=own, node_total=node_total),
        grid=(node_total // nodes,),
        in_specs=[pl.BlockSpec(memory_space=pltpu.SMEM)] + build_specs(slots, depth, nodes, layer),
        out_specs=pl.BlockSpec((nodes, cols), lambda i: (i, 0)),
        out_shape=pltpu.HBM((node_total, cols), F8),
        scratch_shapes=[pltpu.VMEM((nodes, width), BF), pltpu.VMEM((nodes, width), F32)],
        compiler_params=params(),
        cost_estimate=pl.CostEstimate(
            flops=2 * node_total * cols * 256, bytes_accessed=node_total * cols, transcendentals=0
        ),
        name="build_far",
    )(me, in_hbm(ids), in_hbm(counts))


def near_kernel(ids_ref, cnt_ref, table_ref, part_ref, *refs, layer):
    *a_ref, base_ref, low_ref, rows_ref = refs
    one_hots(live_ids(ids_ref, cnt_ref, layer), base_ref, low_ref)
    nodes, cols = rows_ref.shape
    kinds = [BF, F8][: 1 + len(a_ref)]
    for begin in range(0, nodes, NEAR_NODES):
        for start in range(begin, begin + NEAR_NODES, 2 * GROUP_NODES):
            count_rows(start, 2, cols // LO, base_ref, low_ref, [rows_ref, *a_ref], kinds)
        block = slice(begin, begin + NEAR_NODES)
        part_ref[block, :] = mm(rows_ref[block, :], table_ref[...], D10)


def near_step(ids, counts, table, layer):
    depth, slots, node_total = ids.shape
    feat = table.shape[1]
    nodes = NEAR_NODES if layer else 2 * NEAR_NODES
    width = slots * GROUP_NODES
    return pl.pallas_call(
        functools.partial(near_kernel, layer=layer),
        grid=(node_total // nodes,),
        in_specs=build_specs(slots, depth, nodes, layer) + [whole((node_total, feat))],
        out_specs=[
            pl.BlockSpec((nodes, feat), lambda i: (i, 0)),
            pl.BlockSpec((nodes, node_total), lambda i: (i, 0)),
        ][: 1 + (layer > 0)],
        out_shape=[
            jax.ShapeDtypeStruct((node_total, feat), F32),
            pltpu.HBM((node_total, node_total), F8),
        ][: 1 + (layer > 0)],
        scratch_shapes=[
            pltpu.VMEM((nodes, width), BF),
            pltpu.VMEM((nodes, width), F32),
            pltpu.VMEM((nodes, node_total), BF),
        ],
        compiler_params=params(),
        cost_estimate=pl.CostEstimate(
            flops=4 * node_total * node_total * 256, bytes_accessed=node_total * node_total, transcendentals=0
        ),
        name="near_step",
    )(in_hbm(ids), in_hbm(counts), table)


def columns(rows, width):
    nodes = rows[0].shape[1]
    pick = iota((16, nodes), 0)
    stacked = jnp.zeros((16, nodes), F32)
    for r, row in enumerate(rows):
        stacked = jnp.where(pick == r, row.astype(F32), stacked)
    stacked = stacked.astype(BF)
    outs = []
    for r in range(len(rows)):
        take = (iota((16, width), 0) == r).astype(F32).astype(BF)
        outs.append(mm(stacked, take, D00))
    return outs


def count_inverse(counts, width):
    (count,) = columns([counts], 128)
    return jnp.concatenate([1.0 / count] * (width // 128), axis=1)


def normalise(pre):
    centre = pre - jnp.mean(pre, axis=1, keepdims=True)
    inv = lax.rsqrt(jnp.mean(centre * centre, axis=1, keepdims=True) + NORM_EPS)
    return centre * inv, inv


def row_hot(brow, start, nodes):
    return (iota((nodes, brow.shape[1]), 0) + start == brow).astype(F32).astype(BF)


def in_turn(a_hbm, near_ref, far_ref, sum_ref, slots_ref, sems, finish):
    rows = slots_ref.shape[1]
    total = a_hbm.shape[0] // rows
    half = near_ref.shape[0]

    def at(i):
        return pl.ds(pl.multiple_of(i * rows, rows), rows)

    def fetch(i):
        slot = i % 2
        return pltpu.make_async_copy(a_hbm.at[at(i), :], slots_ref.at[slot], sems.at[slot])

    def sums(i):
        held = slots_ref.at[i % 2]
        part = mm(held[:, :half].astype(BF), near_ref[...], D10)
        sum_ref[...] = part + mm(held[:, half:].astype(BF), far_ref[...], D10)

    fetch(0).start()
    fetch(1).start()
    fetch(0).wait()
    sums(0)

    def body(i, carry):
        @pl.when(i + 1 < total)
        def _():
            fetch(i + 1).start()

        fetch(i).wait()
        before = sum_ref[...]
        sums(i)
        finish(at(i - 1), before)
        return carry

    lax.fori_loop(1, total, body, 0)
    finish(at(total - 1), sum_ref[...])


def before_norm(hidden, agg, weights_ref, layer):
    w_self, w_neigh = layer_weights(weights_ref, hidden.shape[1], layer)
    return mm(hidden, w_self, D11) + mm(agg, w_neigh, D11)


def forward_block(rows, summed, part_ref, hid_ref, cnt_ref, weights_ref, norm_ref, layer):
    feat = hid_ref.shape[1]
    hid = weights_ref.shape[0]
    share = count_inverse(cnt_ref[layer : layer + 1, rows], feat)
    agg = ((part_ref[rows, :] + summed) * share).astype(BF)
    unit, inv = normalise(before_norm(hid_ref[rows, :], agg, weights_ref, layer))
    y = unit * norm_ref[layer, 0:1, :] + norm_ref[layer, 1:2, :]
    return agg, unit, inv, y, share


def layer_kernel(
    a_hbm, near_ref, far_ref, part_ref, hid_ref, cnt_ref, weights_ref, norm_ref, brow_ref,
    next_ref, agg_ref, pub_ref, acc_ref, sum_ref, slots_ref, sems, *, layer
):
    acc_ref[...] = jnp.zeros_like(acc_ref)

    def finish(rows, summed):
        agg, _, _, y, _ = forward_block(
            rows, summed, part_ref, hid_ref, cnt_ref, weights_ref, norm_ref, layer
        )
        agg_ref[rows, :] = agg
        new = (y * jax.nn.sigmoid(y)).astype(BF)
        next_ref[rows, :] = new
        hot = row_hot(brow_ref[layer + 1 : layer + 2, :], rows.start, rows.size)
        acc_ref[...] += mm(hot, new, D00)

    in_turn(a_hbm, near_ref, far_ref, sum_ref, slots_ref, sems, finish)
    pub_ref[...] = acc_ref[...].astype(BF)


def weight_columns(layer, hid, first_wide):
    return 0 if layer == 0 else 2 * first_wide + 2 * hid * (layer - 1)


def layer_weights(weights_ref, feat, layer):
    at = weight_columns(layer, weights_ref.shape[0], weights_ref.shape[0] // 2)
    return weights_ref[:, at : at + feat], weights_ref[:, at + feat : at + 2 * feat]


def block_rows(bnd_total):
    return FWD_NODES if bnd_total <= 4096 else 128


def turn_scratch(bnd_total, feat):
    rows = block_rows(bnd_total)
    return [
        pltpu.VMEM((rows, feat), F32),
        pltpu.VMEM((2, rows, bnd_total), F8),
        pltpu.SemaphoreType.DMA((2,)),
    ]


HBM_SPEC = pl.BlockSpec(memory_space=pl.ANY)
VMEM_SPEC = pl.BlockSpec(memory_space=pltpu.VMEM)


def layer_forward(layer, a_bnd, shared, part, hidden, counts, weights, norms, boundary):
    node_total, feat = hidden.shape
    bnd_total = a_bnd.shape[1]
    hid = weights.shape[0]
    own = boundary.shape[1]
    return pl.pallas_call(
        functools.partial(layer_kernel, layer=layer),
        in_specs=[HBM_SPEC] + [VMEM_SPEC] * 8,
        out_specs=[VMEM_SPEC] * 3,
        out_shape=[
            jax.ShapeDtypeStruct((node_total, hid), BF),
            jax.ShapeDtypeStruct((node_total, feat), BF),
            jax.ShapeDtypeStruct((own, hid), BF),
        ],
        scratch_shapes=[pltpu.VMEM((own, hid), F32)] + turn_scratch(bnd_total, feat),
        compiler_params=params(bnd_total),
        cost_estimate=pl.CostEstimate(
            flops=2 * node_total * (bnd_total + 1024) * 256,
            bytes_accessed=node_total * (bnd_total + 4096),
            transcendentals=0,
        ),
        name="layer_step",
    )(in_hbm(a_bnd), *shared, part, hidden, counts, weights, norms, boundary)


def backward_block(d_hidden, unit, inv, y, gain):
    sig = jax.nn.sigmoid(y)
    d_out = d_hidden * sig * (1.0 + y * (1.0 - sig))
    d_gain = jnp.sum(d_out * unit, axis=0, keepdims=True)
    d_shift = jnp.sum(d_out, axis=0, keepdims=True)
    d_unit = d_out * gain
    d_pre = inv * (
        d_unit
        - jnp.mean(d_unit, axis=1, keepdims=True)
        - unit * jnp.mean(d_unit * unit, axis=1, keepdims=True)
    )
    return d_pre.astype(BF), d_gain, d_shift


def add_weight_sums(dw_ref, dnorm_ref, d_pre, hidden, agg, d_gain, d_shift):
    feat = hidden.shape[1]
    hid = d_pre.shape[1]
    dw_ref[0:hid, 0:feat] += mm(d_pre, hidden, D00)
    dw_ref[0:hid, feat : 2 * feat] += mm(d_pre, agg, D00)
    dnorm_ref[0:1, :] += d_gain
    dnorm_ref[1:2, :] += d_shift


def into_places(dw_ref, perm_ref):
    perm = perm_ref[...]
    rows = slice(0, perm.shape[0])
    rest = dw_ref[rows, :]
    moved = jnp.zeros_like(rest)
    for _ in range(3):
        term = rest.astype(BF)
        moved = moved + mm(perm, term, D00)
        rest = rest - term.astype(F32)
    dw_ref[rows, :] = moved


def top_kernel(
    a_hbm, near_ref, far_ref, part_ref, hid_ref, cnt_ref, weights_ref, norm_ref,
    lab_ref, mask_ref, marks_ref, bias_ref, perm_ref,
    ds_ref, da_ref, keep_ref, send_ref, dnorm_ref, dbias_ref, loss_ref, label_ref,
    dw_ref, lost_ref, sum_ref, slots_ref, sems, *, layer
):
    feat = hid_ref.shape[1]
    hid = weights_ref.shape[0]
    classes = bias_ref.shape[1]
    for ref in (dw_ref, dnorm_ref, dbias_ref, lost_ref):
        ref[...] = jnp.zeros_like(ref)
    marks = jnp.sum(marks_ref[...], axis=0, keepdims=True)
    label_ref[...] = 64.0 * marks[:, 0:1] + marks[:, 1:2]
    head_at = weight_columns(layer + 1, hid, hid // 2)

    def finish(rows, summed):
        agg, unit, inv, y, share = forward_block(
            rows, summed, part_ref, hid_ref, cnt_ref, weights_ref, norm_ref, layer
        )
        head = weights_ref[:, head_at : head_at + 128][:, :classes]
        top = (y * jax.nn.sigmoid(y)).astype(BF)
        logits = mm(top, head, D10) + bias_ref[...]
        label, live = columns([lab_ref[:, rows], mask_ref[:, rows]], classes)
        peak = jnp.max(logits, axis=1, keepdims=True)
        log_total = peak + jnp.log(jnp.sum(jnp.exp(logits - peak), axis=1, keepdims=True))
        hot = label == iota(label.shape, 1).astype(F32)
        lost_ref[...] += jnp.sum(jnp.where(hot, live * (log_total - logits), 0.0), axis=0, keepdims=True)
        probs = jnp.exp(logits - log_total)
        d_logits = ((probs - hot.astype(F32)) * live / label_ref[...]).astype(BF)
        dbias_ref[...] += jnp.sum(d_logits.astype(F32), axis=0, keepdims=True)
        d_hidden = mm(d_logits, head, D11)
        d_pre, d_gain, d_shift = backward_block(d_hidden, unit, inv, y, norm_ref[layer, 0:1, :])
        add_weight_sums(dw_ref, dnorm_ref, d_pre, hid_ref[rows, :], agg, d_gain, d_shift)
        dw_ref[:, 2 * feat : 2 * feat + classes] += mm(top, d_logits, D00)
        w_self, w_neigh = layer_weights(weights_ref, feat, layer)
        ds_ref[rows, :] = mm(d_pre, w_self, D10)
        da_ref[rows, :] = (mm(d_pre, w_neigh, D10) * share).astype(BF)

    in_turn(a_hbm, near_ref, far_ref, sum_ref, slots_ref, sems, finish)
    into_places(dw_ref, perm_ref)
    keep_ref[...] = dw_ref[: hid // 2, :]
    send_ref[...] = dw_ref[hid // 2 :, :]
    loss_ref[...] = jnp.sum(lost_ref[...], axis=1, keepdims=True)


def top_layer(layer, marks, a_bnd, shared, part, hidden, counts, weights, norms, labels, live, bias, perm):
    node_total, feat = hidden.shape
    bnd_total = a_bnd.shape[1]
    hid = weights.shape[0]
    classes = bias.shape[1]
    return pl.pallas_call(
        functools.partial(top_kernel, layer=layer),
        in_specs=[HBM_SPEC] + [VMEM_SPEC] * 12,
        out_specs=[VMEM_SPEC] * 8,
        out_shape=[
            jax.ShapeDtypeStruct((node_total, feat), F32),
            jax.ShapeDtypeStruct((node_total, feat), BF),
            jax.ShapeDtypeStruct((hid // 2, 3 * hid), F32),
            jax.ShapeDtypeStruct((hid // 2, 3 * hid), F32),
            jax.ShapeDtypeStruct((2, hid), F32),
            jax.ShapeDtypeStruct((1, classes), F32),
            jax.ShapeDtypeStruct((1, 1), F32),
            jax.ShapeDtypeStruct((1, 1), F32),
        ],
        scratch_shapes=[pltpu.VMEM((hid, 3 * hid), F32), pltpu.VMEM((1, classes), F32)]
        + turn_scratch(bnd_total, feat),
        compiler_params=params(bnd_total),
        cost_estimate=pl.CostEstimate(
            flops=2 * node_total * (bnd_total + 3072) * 256,
            bytes_accessed=node_total * (bnd_total + 4096),
            transcendentals=0,
        ),
        name="top_step",
    )(in_hbm(a_bnd), *shared, part, hidden, counts, weights, norms, labels, live, marks, bias, perm)


def lower_kernel(
    near_ref, dshared_ref, brow_ref, hid_ref, agg_ref, cnt_ref, norm_ref, perm_ref, weights_ref,
    *refs, layer
):
    node_total, hid = near_ref.shape
    feat = hid_ref.shape[1]
    if layer:
        dw_ref, dnorm_ref, ds_ref, da_ref = refs
    else:
        sums_ref, dw_ref, dnorm_ref = refs
    dw_ref[...] = jnp.zeros_like(dw_ref)
    dnorm_ref[...] = jnp.zeros_like(dnorm_ref)
    gain = norm_ref[layer, 0:1, :]
    shared = dshared_ref[...]
    shared_top = shared.astype(BF)
    shared_rest = (shared - shared_top.astype(F32)).astype(BF)

    def block(i, carry):
        rows = pl.ds(pl.multiple_of(i * LOWER_NODES, LOWER_NODES), LOWER_NODES)
        hot = row_hot(brow_ref[layer + 1 : layer + 2, :], rows.start, LOWER_NODES)
        d_hidden = near_ref[rows, :] + mm(hot, shared_top, D10) + mm(hot, shared_rest, D10)
        hidden = hid_ref[rows, :]
        agg = agg_ref[rows, :]
        unit, inv = normalise(before_norm(hidden, agg, weights_ref, layer))
        y = unit * gain + norm_ref[layer, 1:2, :]
        d_pre, d_gain, d_shift = backward_block(d_hidden, unit, inv, y, gain)
        add_weight_sums(dw_ref, dnorm_ref, d_pre, hidden, agg, d_gain, d_shift)
        if layer:
            share = count_inverse(cnt_ref[layer : layer + 1, rows], feat)
            w_self, w_neigh = layer_weights(weights_ref, feat, layer)
            ds_ref[rows, :] = mm(d_pre, w_self, D10)
            da_ref[rows, :] = (mm(d_pre, w_neigh, D10) * share).astype(BF)
        return carry

    lax.fori_loop(0, node_total // LOWER_NODES, block, 0, unroll=True)
    into_places(dw_ref, perm_ref)
    if not layer:
        dw_ref[hid : hid + 2, :] = dnorm_ref[...]
        dw_ref[hid + 2 :, :] = sums_ref[...]


def layer_backward(layer, d_near, d_shared, boundary, hidden, agg, counts, norms, perm, weights, sums=()):
    hid = d_near.shape[1]
    node_total, feat = hidden.shape
    tall = hid if layer else hid + 2 + sums[0].shape[0]
    out_shape = [jax.ShapeDtypeStruct((tall, 2 * feat), F32), jax.ShapeDtypeStruct((2, hid), F32)]
    if layer:
        out_shape += [
            jax.ShapeDtypeStruct((node_total, feat), F32),
            jax.ShapeDtypeStruct((node_total, feat), BF),
        ]
    return pl.pallas_call(
        functools.partial(lower_kernel, layer=layer),
        in_specs=[VMEM_SPEC] * (9 + len(sums)),
        out_specs=[VMEM_SPEC] * len(out_shape),
        out_shape=out_shape,
        compiler_params=params(),
        cost_estimate=pl.CostEstimate(
            flops=2 * node_total * 2048 * 256, bytes_accessed=node_total * 6144, transcendentals=0
        ),
        name="lower_step",
    )(d_near, d_shared, boundary, hidden, agg, counts, norms, perm, weights, *sums)


def spread_kernel(a_ref, d_ref, *refs, add):
    total = mm(a_ref[...].astype(BF), d_ref[...], D00)
    if add:
        total = total + refs[0][...]
    refs[-1][...] = total.astype(refs[-1].dtype)


def spread(a, d_rows, extra, kind, first, steps):
    node_total = a.shape[0]
    feat = d_rows.shape[1]
    specs = [pl.BlockSpec((node_total, BWD_COLS), lambda i: (0, i + first)), whole((node_total, feat))]
    specs += [pl.BlockSpec((BWD_COLS, feat), lambda i: (i + first, 0))] * len(extra)
    return pl.pallas_call(
        functools.partial(spread_kernel, add=len(extra) > 0),
        grid=(steps,),
        in_specs=specs,
        out_specs=pl.BlockSpec((BWD_COLS, feat), lambda i: (i, 0)),
        out_shape=jax.ShapeDtypeStruct((steps * BWD_COLS, feat), kind),
        compiler_params=params(),
        cost_estimate=pl.CostEstimate(
            flops=2 * node_total * steps * BWD_COLS * 256,
            bytes_accessed=node_total * steps * BWD_COLS,
            transcendentals=0,
        ),
        name="spread_near" if extra else "spread_far",
    )(in_hbm(a), d_rows, *extra)


def factored_step(weight, gradient, row_new, col_new, row_mean):
    estimate = row_new[..., None, :] * col_new[..., :, None] / row_mean[..., None, None]
    return weight - LEARN_RATE * gradient * lax.rsqrt(estimate)


def vector_step(param, gradient, state):
    state_new = 0.5 * state + 0.5 * (gradient * gradient + SQUARE_EPS)
    return (param - VECTOR_RATE * gradient * lax.rsqrt(state_new), state_new)


def on_device(
    features,
    labels,
    train_mask,
    boundary,
    neighbours,
    counts,
    first_weight,
    rest_weight,
    head_weight,
    norm_params,
    head_bias,
    first_row,
    first_col,
    rest_row,
    rest_col,
    head_row,
    head_col,
    norm_state,
    bias_state,
    *,
    total,
):
    me = lax.axis_index("dom").astype(I32)
    me_ref = me[None]
    depth = norm_params.shape[0]
    own = boundary.shape[1]
    node_total, f_in = features.shape
    hid = norm_params.shape[2]
    classes = head_bias.shape[0]
    cols_own = hid // total if hid >= total else 1

    first_t = first_weight.T
    rest_t = jnp.swapaxes(rest_weight, 1, 2)
    ids = jnp.swapaxes(neighbours, 1, 2)

    col = jnp.arange(hid, dtype=I32)
    position = place((col // cols_own) ^ me, total) * cols_own + col % cols_own
    perm = (position[:, None] == jnp.arange(hid, dtype=I32)[None, :]).astype(BF)

    (hidden, first_rows), tiles = first_message(
        features.T, boundary, first_t, rest_t, head_weight, train_mask[None]
    )
    f_wide = hidden.shape[1]

    tables = [[None, None] for _ in range(depth)]
    parts = [None] * depth

    def beside(layer, table):
        def far(wait):
            tables[layer][1] = build_far(after(me_ref, wait), ids, counts, layer, total, own)
            return tables[layer][1]

        def near(wait):
            parts[layer], *matrix = near_step(ids, counts, after(table, wait), layer)
            tables[layer][0] = matrix[0] if matrix else None
            return parts[layer]

        return [far, near, None]

    got = gather_rows(first_rows, total, beside(0, hidden))
    got = [g.reshape(total // 2, -1, 128) for g in got]
    shared = [g[:, :own].reshape(-1, 128) for g in got]
    both = jnp.concatenate([g[:, own:] for g in got], axis=0)
    packed = both[:, : tiles * cols_own].reshape(total, tiles, cols_own, 128)
    packed = jnp.swapaxes(packed, 1, 2).reshape(hid, tiles * 128)
    packed = mm(perm, packed, D10).astype(BF)
    marks = both[:, tiles * cols_own].astype(F32)
    weights, marks, perm = lax.optimization_barrier((packed, marks, perm))

    saved = []
    for layer in range(depth):
        if layer:
            shared = gather_rows(published, total, beside(layer, hidden))
        a_loc, a_bnd = tables[layer]
        if layer < depth - 1:
            new, agg, published = layer_forward(
                layer, a_bnd, shared, parts[layer], hidden, counts, weights, norm_params, boundary
            )
            saved.append((a_loc, a_bnd, hidden, agg))
            hidden = new
    ds, da, *dw, dnorm, dbias, loss, label_count = top_layer(
        depth - 1, marks, a_bnd, shared, parts[-1], hidden, counts, weights, norm_params,
        labels[None], train_mask[None], head_bias[None], perm,
    )
    d_norms = [None] * depth
    d_norms[-1] = dnorm
    grads = [None] * depth
    near_steps = node_total // BWD_COLS
    far_steps = a_bnd.shape[1] // BWD_COLS
    rounds = bit_groups(total)[::-1]
    for layer in reversed(range(depth - 1)):
        low, size = rounds[0]
        dw = swap(dw if isinstance(dw, list) else cut(dw, size), low, total)
        sent = spread(a_bnd, after(da, dw[0]), (), BF, far_steps // 2, far_steps // 2)
        dw = add_up(after_all(dw, sent))
        arrived = hop(sent, 1, total)
        kept = spread(a_bnd, after(da, sent), (), BF, 0, far_steps // 2)
        far = kept.astype(F32) + arrived.astype(F32)
        near = None
        for low, size in rounds[1:]:
            far, dw = cut(far, size), cut(dw, size)
            edge, width = far[0].shape
            tall = dw[0].shape[0]
            stacks = [
                jnp.concatenate([far[d]] + [dw[d][:, c : c + width] for c in range(0, dw[d].shape[1], width)], axis=0)
                for d in range(size)
            ]
            stacks = swap([stacks[0]] + [stack.astype(BF) for stack in stacks[1:]], low, total)
            if near is None:
                near = spread(a_loc, after(da, stacks[0]), (ds,), F32, 0, near_steps)
                stacks[0] = after(stacks[0], near)
            stack = add_up(stacks)
            far = stack[:edge]
            dw = jnp.concatenate([stack[r : r + tall] for r in range(edge, stack.shape[0], tall)], axis=1)
        grads[layer + 1] = dw
        a_loc, a_bnd, hidden, agg = saved[layer]
        sums = ()
        if not layer:
            wide = 2 * f_wide
            g_head = grads[-1][:, 2 * hid : 2 * hid + classes]
            g_rest = [g[:, : 2 * hid] for g in grads[1:]]
            sq_rest = [g * g + SQUARE_EPS for g in g_rest]
            sq_head = g_head * g_head + SQUARE_EPS
            head_row_new = 0.5 * head_row + 0.5 * jnp.mean(sq_head, axis=1)
            ends = jnp.concatenate(
                [jnp.sum(head_row_new, keepdims=True).reshape(1, 1), loss], axis=1
            )
            row = jnp.concatenate([dbias, jnp.sum(sq_head, axis=0, keepdims=True), ends], axis=1)
            row = jnp.pad(row, ((0, 0), (0, wide - row.shape[1])))
            squares = [jnp.sum(sq, axis=0, keepdims=True) for sq in sq_rest]
            squares = [sq[:, c : c + wide] for sq in squares for c in range(0, 2 * hid, wide)]
            rows = jnp.concatenate(d_norms[1:] + squares + [row], axis=0)
            sums = (jnp.pad(rows, ((0, -(rows.shape[0] + 2) % 16), (0, 0))),)
        outs = layer_backward(
            layer, near, far, boundary, hidden, agg, counts, norm_params, perm, weights, sums
        )
        dw = outs[0]
        if layer:
            d_norms[layer] = outs[1]
            ds, da = outs[2:]

    extra = dw.shape[0] - hid
    last = len(rounds) - 1
    for i, (low, size) in enumerate(rounds):
        sums = dw[-extra:]
        keep = cut(dw[:-extra], size)
        if i == last:
            keep = [jnp.concatenate([keep[p ^ d] for p in range(size)], axis=0) for d in range(size)]
        dw = add_up(swap([jnp.concatenate([part, sums], axis=0) for part in keep], low, total))
    sums, dw = dw[-extra:], dw[:-extra]
    first_sums = add_up([jnp.sum(block * block + SQUARE_EPS, axis=0, keepdims=True) for block in cut(dw, rounds[last][1])])
    for i, (low, size) in enumerate(rounds[:last]):
        mask = 1
        while mask < size:
            first_sums = first_sums + hop(first_sums, mask << low, total)
            if not i:
                sums = after(sums, first_sums)
            mask *= 2
    g_wide = dw[:cols_own]
    g_first = jnp.concatenate([g_wide[:, :f_in], g_wide[:, f_wide : f_wide + f_in]], axis=1)
    first_sums = jnp.concatenate([first_sums[0, :f_in], first_sums[0, f_wide : f_wide + f_in]])
    sq_first = g_first * g_first + SQUARE_EPS
    g_rest = jnp.stack(g_rest)
    sq_rest = jnp.stack(sq_rest)

    g_norms = sums[: 2 * depth].reshape(norm_params.shape)
    at = 2 * depth
    tall = (depth - 1) * 2 * hid // wide
    rest_sums = sums[at : at + tall].reshape(rest_row.shape)
    row = sums[at + tall]
    g_bias = row[:classes]
    head_sums = row[classes : 2 * classes]
    head_row_mean = row[2 * classes] / hid
    loss_sum = row[2 * classes + 1]

    first_row_new = 0.5 * first_row + 0.5 * first_sums / hid
    first_col_new = 0.5 * first_col + 0.5 * jnp.mean(sq_first, axis=1)
    rest_row_new = 0.5 * rest_row + 0.5 * rest_sums / hid
    rest_col_new = 0.5 * rest_col + 0.5 * jnp.mean(sq_rest, axis=2)
    head_col_new = 0.5 * head_col + 0.5 * head_sums / hid
    first_new = factored_step(first_t, g_first, first_row_new, first_col_new, jnp.mean(first_row_new))
    rest_new = factored_step(rest_t, g_rest, rest_row_new, rest_col_new, jnp.mean(rest_row_new, axis=1))
    head_new = head_weight - LEARN_RATE * g_head * lax.rsqrt(
        head_row_new[:, None] * head_col_new[None, :] / head_row_mean
    )
    norm_new, norm_state_new = vector_step(norm_params, g_norms, norm_state)
    bias_new, bias_state_new = vector_step(head_bias, g_bias, bias_state)
    first_new = first_new.T
    rest_new = jnp.swapaxes(rest_new, 1, 2)
    return (
        loss_sum,
        label_count[0, 0],
        first_new,
        rest_new,
        head_new,
        norm_new,
        bias_new,
        g_first.T,
        jnp.swapaxes(g_rest, 1, 2),
        g_head,
        g_norms,
        g_bias,
        first_row_new,
        first_col_new,
        rest_row_new,
        rest_col_new,
        head_row_new,
        head_col_new,
        norm_state_new,
        bias_state_new,
        first_new.astype(BF),
        rest_new.astype(BF),
        head_new.astype(BF),
        norm_new.astype(BF),
    )


def solution(mesh):
    placed = (
        P("dom", None),
        P("dom"),
        P("dom"),
        P(None, "dom"),
        P(None, "dom", None),
        P(None, "dom"),
        P(None, "dom"),
        P(None, None, "dom"),
        P("dom", None),
        P(),
        P(),
        P(),
        P("dom"),
        P(),
        P(None, "dom"),
        P("dom"),
        P(),
        P(),
        P(),
    )
    return jax.shard_map(
        functools.partial(on_device, total=mesh.shape["dom"]),
        mesh=mesh,
        in_specs=placed,
        out_specs=(
            P(),
            P(),
            P(None, "dom"),
            P(None, None, "dom"),
            P("dom", None),
            P(),
            P(),
            P(None, "dom"),
            P(None, None, "dom"),
            P("dom", None),
            P(),
            P(),
            P(),
            P("dom"),
            P(),
            P(None, "dom"),
            P("dom"),
            P(),
            P(),
            P(),
            P(None, "dom"),
            P(None, None, "dom"),
            P("dom", None),
            P(),
        ),
        check_vma=False,
    )
```

```python
import functools

import jax
import jax.numpy as jnp
from jax import lax
from jax.experimental import pallas as pl
from jax.experimental.pallas import tpu as pltpu
from jax.sharding import PartitionSpec as P

LEARN_RATE = 0.03
VECTOR_RATE = 0.25
SQUARE_EPS = 1e-30
NORM_EPS = 1e-05

BF = jnp.bfloat16
F32 = jnp.float32
F8 = jnp.float8_e4m3fn
I32 = jnp.int32

D00 = (((0,), (0,)), ((), ()))
D11 = (((1,), (1,)), ((), ()))
D10 = (((1,), (0,)), ((), ()))

LO = 256
NEAR_NODES = 512
FAR_NODES = 1024
GROUP_NODES = 16
FWD_NODES = 1024
LOWER_NODES = 2048
BWD_COLS = 1024
VMEM_LIMIT = 26 << 20


def mm(left, right, dims):
    return lax.dot_general(left, right, dims, preferred_element_type=F32)


def iota(shape, dim):
    return lax.broadcasted_iota(I32, shape, dim)


def params(bnd_total=0):
    return pltpu.CompilerParams(vmem_limit_bytes=VMEM_LIMIT if bnd_total <= 4096 else 60 << 20)


def in_hbm(value):
    return pltpu.with_memory_space_constraint(value, pltpu.HBM)


def whole(shape):
    return pl.BlockSpec(shape, lambda i: (0,) * len(shape))


def hop(value, mask, total):
    return lax.ppermute(value, "dom", [(i, i ^ mask) for i in range(total)])


def bit_groups(total):
    bits = total.bit_length() - 1
    groups = [(0, 2)]
    at = 1
    while at < bits:
        wide = min(2, bits - at)
        groups.append((at, 1 << wide))
        at += wide
    return groups[::-1]


def place(relative, total):
    out, scale = 0, 1
    for low, size in bit_groups(total):
        out = out + ((relative >> low) & (size - 1)) * scale
        scale *= size
    return out


def after(value, *others):
    return lax.optimization_barrier((value, *others))[0]


def after_all(parts, work):
    return parts if work is None else [after(parts[0], work)] + parts[1:]


def gather_rows(rows, total, works):
    groups = bit_groups(total)
    works = [None] * (len(groups) - len(works)) + list(works)
    for i, (low, size) in enumerate(groups):
        got = [hop(rows, d << low, total) for d in range(1, size)]
        done = works[i](rows) if works[i] else rows
        if i == len(groups) - 1:
            return rows, got[0]
        rows = after(jnp.concatenate([rows] + got, axis=0), done)


def cut(rows, size):
    step = rows.shape[0] // size
    return [rows[d * step : (d + 1) * step] for d in range(size)]


def swap(parts, low, total):
    return [parts[0]] + [hop(part, d << low, total) for d, part in enumerate(parts) if d]


def add_up(parts):
    kind = parts[0].dtype
    parts = [part.astype(F32) for part in parts]
    while len(parts) > 1:
        parts = [parts[i] + parts[i + 1] for i in range(0, len(parts), 2)]
    return parts[0].astype(kind)


def first_kernel(feat_ref, brow_ref, first_ref, rest_ref, head_ref, mask_ref, hid_ref, out_ref, rows_ref):
    f_in, nodes = feat_ref.shape
    own = brow_ref.shape[1]
    cols, classes = head_ref.shape
    turned = feat_ref[...].astype(BF)
    eye = (iota((f_in, 128), 0) == iota((f_in, 128), 1)).astype(F32).astype(BF)
    hid_ref[...] = mm(turned, eye, D00).astype(BF)
    hot = (iota((nodes, own), 0) == brow_ref[0:1, :]).astype(F32).astype(BF)
    rows_ref[...] = jnp.zeros_like(rows_ref)
    rows_ref[0:own, :] = mm(mm(turned, hot, D10).astype(BF), eye, D00)
    at = own
    rows_ref[at : at + cols, 0:f_in] = first_ref[:, 0:f_in]
    rows_ref[at + cols : at + 2 * cols, 0:f_in] = first_ref[:, f_in : 2 * f_in]
    at += 2 * cols
    for k in range(rest_ref.shape[0]):
        for c in range(0, rest_ref.shape[2], 128):
            rows_ref[at : at + cols, :] = rest_ref[k, :, c : c + 128]
            at += cols
    rows_ref[at : at + cols, 0:classes] = head_ref[...]
    at += cols
    count = jnp.sum(mask_ref[...].astype(F32), axis=1, keepdims=True)
    high = jnp.floor(count * (1.0 / 64.0))
    lane = iota((1, 128), 1)
    rows_ref[at : at + 1, :] = jnp.where(lane == 0, high, jnp.where(lane == 1, count - 64.0 * high, 0.0))
    out_ref[...] = rows_ref[...].astype(BF)


def first_message(feat_t, boundary, first_t, rest_t, head_weight, live):
    own = boundary.shape[1]
    cols = head_weight.shape[0]
    tiles = 3 + rest_t.shape[0] * rest_t.shape[2] // 128
    rows = -(-(own + tiles * cols + 1) // 16) * 16
    return pl.pallas_call(
        first_kernel,
        out_shape=[jax.ShapeDtypeStruct((feat_t.shape[1], 128), BF), jax.ShapeDtypeStruct((rows, 128), BF)],
        scratch_shapes=[pltpu.VMEM((rows, 128), F32)],
        compiler_params=params(),
        name="first_message",
    )(*map(in_hbm, (feat_t, boundary, first_t, rest_t, head_weight, live))), tiles


def one_hots(ids, base_ref, low_ref):
    slots, nodes = ids.shape
    high = (ids >> 8).astype(F32).astype(BF)
    low = (ids & 255).astype(F32).astype(BF)
    width = slots * GROUP_NODES
    shift = GROUP_NODES.bit_length() - 1
    widen = (iota((slots, width), 0) == iota((slots, width), 1) >> shift).astype(F32).astype(BF)
    same = iota((1, GROUP_NODES, width), 1) == iota((1, GROUP_NODES, width), 2) & (GROUP_NODES - 1)
    grouped = (nodes // GROUP_NODES, GROUP_NODES, width)
    base = jnp.where(same, mm(high, widen, D00).reshape(grouped), -1.0)
    base_ref[...] = base.reshape(nodes, width).astype(BF)
    low_ref[...] = jnp.where(same, mm(low, widen, D00).reshape(grouped), 0.0).reshape(nodes, width)


def count_rows(start, groups, blocks, base_ref, low_ref, outs, kinds):
    width = base_ref.shape[1]
    low_iota = iota((LO, width), 0).astype(F32).astype(BF)
    one = jnp.ones((), BF)
    zero = jnp.zeros((), BF)
    sums = []
    for g in range(groups):
        rows = pl.ds(start + g * GROUP_NODES, GROUP_NODES)
        base = base_ref[rows, :]
        low_row = jnp.sum(low_ref[rows, :], axis=0, keepdims=True).astype(BF)
        right = jnp.where(low_row == low_iota, one, zero)
        left = jnp.concatenate([jnp.where(base == jnp.asarray(h, BF), one, zero) for h in range(blocks)], axis=0)
        if len(kinds) == 1 and kinds[0] == BF:
            left, right = left.astype(F8), right.astype(F8)
        sums.append(mm(left, right, D11))
    for h in range(blocks):
        rows = jnp.concatenate([part[h * GROUP_NODES : (h + 1) * GROUP_NODES] for part in sums], axis=0)
        for out, kind in zip(outs, kinds):
            out[pl.ds(start, groups * GROUP_NODES), h * LO : (h + 1) * LO] = rows.astype(kind)


def live_ids(ids_ref, cnt_ref, layer):
    slots, nodes = ids_ref.shape[1:]
    return jnp.where(iota((slots, nodes), 0) < cnt_ref[layer : layer + 1, :], ids_ref[0], -1)


def all_rows(nodes, blocks, base_ref, low_ref, outs, kinds):
    step = 2 * GROUP_NODES
    if blocks <= 32:
        for start in range(0, nodes, step):
            count_rows(start, 2, blocks, base_ref, low_ref, outs, kinds)
    else:

        def body(i, carry):
            count_rows(pl.multiple_of(i * step, step), 2, blocks, base_ref, low_ref, outs, kinds)
            return carry

        lax.fori_loop(0, nodes // step, body, 0)


def far_kernel(me_ref, ids_ref, cnt_ref, out_ref, base_ref, low_ref, *, layer, total, own, node_total):
    ids = live_ids(ids_ref, cnt_ref, layer)
    table = ids - node_total
    moved = place((table >> own.bit_length() - 1) ^ me_ref[0], total) * own + (table & own - 1)
    one_hots(jnp.where(table < 0, -1, moved), base_ref, low_ref)
    all_rows(ids.shape[1], out_ref.shape[1] // LO, base_ref, low_ref, [out_ref], [F8])


def build_specs(slots, depth, nodes, layer):
    return [
        pl.BlockSpec((1, slots, nodes), lambda i: (layer, 0, i)),
        pl.BlockSpec((depth, nodes), lambda i: (0, i)),
    ]


def build_far(me, ids, counts, layer, total, own):
    depth, slots, node_total = ids.shape
    cols = total * own
    nodes = FAR_NODES if cols <= 8192 else 128
    width = slots * GROUP_NODES
    return pl.pallas_call(
        functools.partial(far_kernel, layer=layer, total=total, own=own, node_total=node_total),
        grid=(node_total // nodes,),
        in_specs=[pl.BlockSpec(memory_space=pltpu.SMEM)] + build_specs(slots, depth, nodes, layer),
        out_specs=pl.BlockSpec((nodes, cols), lambda i: (i, 0)),
        out_shape=pltpu.HBM((node_total, cols), F8),
        scratch_shapes=[pltpu.VMEM((nodes, width), BF), pltpu.VMEM((nodes, width), F32)],
        compiler_params=params(),
        cost_estimate=pl.CostEstimate(
            flops=2 * node_total * cols * 256, bytes_accessed=node_total * cols, transcendentals=0
        ),
        name="build_far",
    )(me, in_hbm(ids), in_hbm(counts))


def near_kernel(ids_ref, cnt_ref, table_ref, part_ref, *refs, layer):
    *a_ref, base_ref, low_ref, rows_ref = refs
    one_hots(live_ids(ids_ref, cnt_ref, layer), base_ref, low_ref)
    nodes, cols = rows_ref.shape
    kinds = [BF, F8][: 1 + len(a_ref)]
    for begin in range(0, nodes, NEAR_NODES):
        for start in range(begin, begin + NEAR_NODES, 2 * GROUP_NODES):
            count_rows(start, 2, cols // LO, base_ref, low_ref, [rows_ref, *a_ref], kinds)
        block = slice(begin, begin + NEAR_NODES)
        part_ref[block, :] = mm(rows_ref[block, :], table_ref[...], D10)


def near_step(ids, counts, table, layer):
    depth, slots, node_total = ids.shape
    feat = table.shape[1]
    nodes = NEAR_NODES if layer else 2 * NEAR_NODES
    width = slots * GROUP_NODES
    return pl.pallas_call(
        functools.partial(near_kernel, layer=layer),
        grid=(node_total // nodes,),
        in_specs=build_specs(slots, depth, nodes, layer) + [whole((node_total, feat))],
        out_specs=[
            pl.BlockSpec((nodes, feat), lambda i: (i, 0)),
            pl.BlockSpec((nodes, node_total), lambda i: (i, 0)),
        ][: 1 + (layer > 0)],
        out_shape=[
            jax.ShapeDtypeStruct((node_total, feat), F32),
            pltpu.HBM((node_total, node_total), F8),
        ][: 1 + (layer > 0)],
        scratch_shapes=[
            pltpu.VMEM((nodes, width), BF),
            pltpu.VMEM((nodes, width), F32),
            pltpu.VMEM((nodes, node_total), BF),
        ],
        compiler_params=params(),
        cost_estimate=pl.CostEstimate(
            flops=4 * node_total * node_total * 256, bytes_accessed=node_total * node_total, transcendentals=0
        ),
        name="near_step",
    )(in_hbm(ids), in_hbm(counts), table)


def columns(rows, width):
    nodes = rows[0].shape[1]
    pick = iota((16, nodes), 0)
    stacked = jnp.zeros((16, nodes), F32)
    for r, row in enumerate(rows):
        stacked = jnp.where(pick == r, row.astype(F32), stacked)
    stacked = stacked.astype(BF)
    outs = []
    for r in range(len(rows)):
        take = (iota((16, width), 0) == r).astype(F32).astype(BF)
        outs.append(mm(stacked, take, D00))
    return outs


def count_inverse(counts, width):
    (count,) = columns([counts], 128)
    return jnp.concatenate([1.0 / count] * (width // 128), axis=1)


def normalise(pre):
    centre = pre - jnp.mean(pre, axis=1, keepdims=True)
    inv = lax.rsqrt(jnp.mean(centre * centre, axis=1, keepdims=True) + NORM_EPS)
    return centre * inv, inv


def row_hot(brow, start, nodes):
    return (iota((nodes, brow.shape[1]), 0) + start == brow).astype(F32).astype(BF)


def in_turn(a_hbm, near_ref, far_ref, sum_ref, slots_ref, sems, finish):
    rows = slots_ref.shape[1]
    total = a_hbm.shape[0] // rows
    half = near_ref.shape[0]

    def at(i):
        return pl.ds(pl.multiple_of(i * rows, rows), rows)

    def fetch(i):
        slot = i % 2
        return pltpu.make_async_copy(a_hbm.at[at(i), :], slots_ref.at[slot], sems.at[slot])

    def sums(i):
        held = slots_ref.at[i % 2]
        part = mm(held[:, :half].astype(BF), near_ref[...], D10)
        sum_ref[...] = part + mm(held[:, half:].astype(BF), far_ref[...], D10)

    fetch(0).start()
    fetch(1).start()
    fetch(0).wait()
    sums(0)

    def body(i, carry):
        @pl.when(i + 1 < total)
        def _():
            fetch(i + 1).start()

        fetch(i).wait()
        before = sum_ref[...]
        sums(i)
        finish(at(i - 1), before)
        return carry

    lax.fori_loop(1, total, body, 0)
    finish(at(total - 1), sum_ref[...])


def before_norm(hidden, agg, weights_ref, layer):
    w_self, w_neigh = layer_weights(weights_ref, hidden.shape[1], layer)
    return mm(hidden, w_self, D11) + mm(agg, w_neigh, D11)


def forward_block(rows, summed, part_ref, hid_ref, cnt_ref, weights_ref, norm_ref, layer):
    feat = hid_ref.shape[1]
    hid = weights_ref.shape[0]
    share = count_inverse(cnt_ref[layer : layer + 1, rows], feat)
    agg = ((part_ref[rows, :] + summed) * share).astype(BF)
    unit, inv = normalise(before_norm(hid_ref[rows, :], agg, weights_ref, layer))
    y = unit * norm_ref[layer, 0:1, :] + norm_ref[layer, 1:2, :]
    return agg, unit, inv, y, share


def layer_kernel(
    a_hbm, near_ref, far_ref, part_ref, hid_ref, cnt_ref, weights_ref, norm_ref, brow_ref,
    next_ref, agg_ref, pub_ref, acc_ref, sum_ref, slots_ref, sems, *, layer
):
    acc_ref[...] = jnp.zeros_like(acc_ref)

    def finish(rows, summed):
        agg, _, _, y, _ = forward_block(
            rows, summed, part_ref, hid_ref, cnt_ref, weights_ref, norm_ref, layer
        )
        agg_ref[rows, :] = agg
        new = (y * jax.nn.sigmoid(y)).astype(BF)
        next_ref[rows, :] = new
        hot = row_hot(brow_ref[layer + 1 : layer + 2, :], rows.start, rows.size)
        acc_ref[...] += mm(hot, new, D00)

    in_turn(a_hbm, near_ref, far_ref, sum_ref, slots_ref, sems, finish)
    pub_ref[...] = acc_ref[...].astype(BF)


def weight_columns(layer, hid, first_wide):
    return 0 if layer == 0 else 2 * first_wide + 2 * hid * (layer - 1)


def layer_weights(weights_ref, feat, layer):
    at = weight_columns(layer, weights_ref.shape[0], weights_ref.shape[0] // 2)
    return weights_ref[:, at : at + feat], weights_ref[:, at + feat : at + 2 * feat]


def block_rows(bnd_total):
    return FWD_NODES if bnd_total <= 4096 else 128


def turn_scratch(bnd_total, feat):
    rows = block_rows(bnd_total)
    return [
        pltpu.VMEM((rows, feat), F32),
        pltpu.VMEM((2, rows, bnd_total), F8),
        pltpu.SemaphoreType.DMA((2,)),
    ]


HBM_SPEC = pl.BlockSpec(memory_space=pl.ANY)
VMEM_SPEC = pl.BlockSpec(memory_space=pltpu.VMEM)


def layer_forward(layer, a_bnd, shared, part, hidden, counts, weights, norms, boundary):
    node_total, feat = hidden.shape
    bnd_total = a_bnd.shape[1]
    hid = weights.shape[0]
    own = boundary.shape[1]
    return pl.pallas_call(
        functools.partial(layer_kernel, layer=layer),
        in_specs=[HBM_SPEC] + [VMEM_SPEC] * 8,
        out_specs=[VMEM_SPEC] * 3,
        out_shape=[
            jax.ShapeDtypeStruct((node_total, hid), BF),
            jax.ShapeDtypeStruct((node_total, feat), BF),
            jax.ShapeDtypeStruct((own, hid), BF),
        ],
        scratch_shapes=[pltpu.VMEM((own, hid), F32)] + turn_scratch(bnd_total, feat),
        compiler_params=params(bnd_total),
        cost_estimate=pl.CostEstimate(
            flops=2 * node_total * (bnd_total + 1024) * 256,
            bytes_accessed=node_total * (bnd_total + 4096),
            transcendentals=0,
        ),
        name="layer_step",
    )(in_hbm(a_bnd), *shared, part, hidden, counts, weights, norms, boundary)


def backward_block(d_hidden, unit, inv, y, gain):
    sig = jax.nn.sigmoid(y)
    d_out = d_hidden * sig * (1.0 + y * (1.0 - sig))
    d_gain = jnp.sum(d_out * unit, axis=0, keepdims=True)
    d_shift = jnp.sum(d_out, axis=0, keepdims=True)
    d_unit = d_out * gain
    d_pre = inv * (
        d_unit
        - jnp.mean(d_unit, axis=1, keepdims=True)
        - unit * jnp.mean(d_unit * unit, axis=1, keepdims=True)
    )
    return d_pre.astype(BF), d_gain, d_shift


def add_weight_sums(dw_ref, dnorm_ref, d_pre, hidden, agg, d_gain, d_shift):
    feat = hidden.shape[1]
    hid = d_pre.shape[1]
    dw_ref[0:hid, 0:feat] += mm(d_pre, hidden, D00)
    dw_ref[0:hid, feat : 2 * feat] += mm(d_pre, agg, D00)
    dnorm_ref[0:1, :] += d_gain
    dnorm_ref[1:2, :] += d_shift


def into_places(dw_ref, perm_ref):
    perm = perm_ref[...]
    rows = slice(0, perm.shape[0])
    rest = dw_ref[rows, :]
    moved = jnp.zeros_like(rest)
    for _ in range(3):
        term = rest.astype(BF)
        moved = moved + mm(perm, term, D00)
        rest = rest - term.astype(F32)
    dw_ref[rows, :] = moved


def top_kernel(
    a_hbm, near_ref, far_ref, part_ref, hid_ref, cnt_ref, weights_ref, norm_ref,
    lab_ref, mask_ref, marks_ref, bias_ref, perm_ref,
    ds_ref, da_ref, keep_ref, send_ref, dnorm_ref, dbias_ref, loss_ref, label_ref,
    dw_ref, lost_ref, sum_ref, slots_ref, sems, *, layer
):
    feat = hid_ref.shape[1]
    hid = weights_ref.shape[0]
    classes = bias_ref.shape[1]
    for ref in (dw_ref, dnorm_ref, dbias_ref, lost_ref):
        ref[...] = jnp.zeros_like(ref)
    marks = jnp.sum(marks_ref[...], axis=0, keepdims=True)
    label_ref[...] = 64.0 * marks[:, 0:1] + marks[:, 1:2]
    head_at = weight_columns(layer + 1, hid, hid // 2)

    def finish(rows, summed):
        agg, unit, inv, y, share = forward_block(
            rows, summed, part_ref, hid_ref, cnt_ref, weights_ref, norm_ref, layer
        )
        head = weights_ref[:, head_at : head_at + 128][:, :classes]
        top = (y * jax.nn.sigmoid(y)).astype(BF)
        logits = mm(top, head, D10) + bias_ref[...]
        label, live = columns([lab_ref[:, rows], mask_ref[:, rows]], classes)
        peak = jnp.max(logits, axis=1, keepdims=True)
        log_total = peak + jnp.log(jnp.sum(jnp.exp(logits - peak), axis=1, keepdims=True))
        hot = label == iota(label.shape, 1).astype(F32)
        lost_ref[...] += jnp.sum(jnp.where(hot, live * (log_total - logits), 0.0), axis=0, keepdims=True)
        probs = jnp.exp(logits - log_total)
        d_logits = ((probs - hot.astype(F32)) * (live * (1.0 / label_ref[...]))).astype(BF)
        dbias_ref[...] += jnp.sum(d_logits.astype(F32), axis=0, keepdims=True)
        d_hidden = mm(d_logits, head, D11)
        d_pre, d_gain, d_shift = backward_block(d_hidden, unit, inv, y, norm_ref[layer, 0:1, :])
        add_weight_sums(dw_ref, dnorm_ref, d_pre, hid_ref[rows, :], agg, d_gain, d_shift)
        dw_ref[:, 2 * feat : 2 * feat + classes] += mm(top, d_logits, D00)
        w_self, w_neigh = layer_weights(weights_ref, feat, layer)
        ds_ref[rows, :] = mm(d_pre, w_self, D10)
        da_ref[rows, :] = (mm(d_pre, w_neigh, D10) * share).astype(BF)

    in_turn(a_hbm, near_ref, far_ref, sum_ref, slots_ref, sems, finish)
    into_places(dw_ref, perm_ref)
    keep_ref[...] = dw_ref[: hid // 2, :]
    send_ref[...] = dw_ref[hid // 2 :, :]
    loss_ref[...] = jnp.sum(lost_ref[...], axis=1, keepdims=True)


def top_layer(layer, marks, a_bnd, shared, part, hidden, counts, weights, norms, labels, live, bias, perm):
    node_total, feat = hidden.shape
    bnd_total = a_bnd.shape[1]
    hid = weights.shape[0]
    classes = bias.shape[1]
    return pl.pallas_call(
        functools.partial(top_kernel, layer=layer),
        in_specs=[HBM_SPEC] + [VMEM_SPEC] * 12,
        out_specs=[VMEM_SPEC] * 8,
        out_shape=[
            jax.ShapeDtypeStruct((node_total, feat), F32),
            jax.ShapeDtypeStruct((node_total, feat), BF),
            jax.ShapeDtypeStruct((hid // 2, 3 * hid), F32),
            jax.ShapeDtypeStruct((hid // 2, 3 * hid), F32),
            jax.ShapeDtypeStruct((2, hid), F32),
            jax.ShapeDtypeStruct((1, classes), F32),
            jax.ShapeDtypeStruct((1, 1), F32),
            jax.ShapeDtypeStruct((1, 1), F32),
        ],
        scratch_shapes=[pltpu.VMEM((hid, 3 * hid), F32), pltpu.VMEM((1, classes), F32)]
        + turn_scratch(bnd_total, feat),
        compiler_params=params(bnd_total),
        cost_estimate=pl.CostEstimate(
            flops=2 * node_total * (bnd_total + 3072) * 256,
            bytes_accessed=node_total * (bnd_total + 4096),
            transcendentals=0,
        ),
        name="top_step",
    )(in_hbm(a_bnd), *shared, part, hidden, counts, weights, norms, labels, live, marks, bias, perm)


def lower_kernel(
    near_ref, dshared_ref, brow_ref, hid_ref, agg_ref, cnt_ref, norm_ref, perm_ref, weights_ref,
    *refs, layer
):
    node_total, hid = near_ref.shape
    feat = hid_ref.shape[1]
    if layer:
        dw_ref, dnorm_ref, ds_ref, da_ref = refs
    else:
        sums_ref, dw_ref, dnorm_ref = refs
    dw_ref[...] = jnp.zeros_like(dw_ref)
    dnorm_ref[...] = jnp.zeros_like(dnorm_ref)
    gain = norm_ref[layer, 0:1, :]
    shared = dshared_ref[...]
    shared_top = shared.astype(BF)
    shared_rest = (shared - shared_top.astype(F32)).astype(BF)

    def block(i, carry):
        rows = pl.ds(pl.multiple_of(i * LOWER_NODES, LOWER_NODES), LOWER_NODES)
        hot = row_hot(brow_ref[layer + 1 : layer + 2, :], rows.start, LOWER_NODES)
        d_hidden = near_ref[rows, :] + mm(hot, shared_top, D10) + mm(hot, shared_rest, D10)
        hidden = hid_ref[rows, :]
        agg = agg_ref[rows, :]
        unit, inv = normalise(before_norm(hidden, agg, weights_ref, layer))
        y = unit * gain + norm_ref[layer, 1:2, :]
        d_pre, d_gain, d_shift = backward_block(d_hidden, unit, inv, y, gain)
        add_weight_sums(dw_ref, dnorm_ref, d_pre, hidden, agg, d_gain, d_shift)
        if layer:
            share = count_inverse(cnt_ref[layer : layer + 1, rows], feat)
            w_self, w_neigh = layer_weights(weights_ref, feat, layer)
            ds_ref[rows, :] = mm(d_pre, w_self, D10)
            da_ref[rows, :] = (mm(d_pre, w_neigh, D10) * share).astype(BF)
        return carry

    lax.fori_loop(0, node_total // LOWER_NODES, block, 0, unroll=True)
    into_places(dw_ref, perm_ref)
    if not layer:
        dw_ref[hid : hid + 2, :] = dnorm_ref[...]
        dw_ref[hid + 2 :, :] = sums_ref[...]


def layer_backward(layer, d_near, d_shared, boundary, hidden, agg, counts, norms, perm, weights, sums=()):
    hid = d_near.shape[1]
    node_total, feat = hidden.shape
    tall = hid if layer else hid + 2 + sums[0].shape[0]
    out_shape = [jax.ShapeDtypeStruct((tall, 2 * feat), F32), jax.ShapeDtypeStruct((2, hid), F32)]
    if layer:
        out_shape += [
            jax.ShapeDtypeStruct((node_total, feat), F32),
            jax.ShapeDtypeStruct((node_total, feat), BF),
        ]
    return pl.pallas_call(
        functools.partial(lower_kernel, layer=layer),
        in_specs=[VMEM_SPEC] * (9 + len(sums)),
        out_specs=[VMEM_SPEC] * len(out_shape),
        out_shape=out_shape,
        compiler_params=params(),
        cost_estimate=pl.CostEstimate(
            flops=2 * node_total * 2048 * 256, bytes_accessed=node_total * 6144, transcendentals=0
        ),
        name="lower_step",
    )(d_near, d_shared, boundary, hidden, agg, counts, norms, perm, weights, *sums)


def spread_kernel(a_ref, d_ref, *refs, add):
    total = mm(a_ref[...].astype(BF), d_ref[...], D00)
    if add:
        total = total + refs[0][...]
    refs[-1][...] = total.astype(refs[-1].dtype)


def spread(a, d_rows, extra, kind, first, steps):
    node_total = a.shape[0]
    feat = d_rows.shape[1]
    specs = [pl.BlockSpec((node_total, BWD_COLS), lambda i: (0, i + first)), whole((node_total, feat))]
    specs += [pl.BlockSpec((BWD_COLS, feat), lambda i: (i + first, 0))] * len(extra)
    return pl.pallas_call(
        functools.partial(spread_kernel, add=len(extra) > 0),
        grid=(steps,),
        in_specs=specs,
        out_specs=pl.BlockSpec((BWD_COLS, feat), lambda i: (i, 0)),
        out_shape=jax.ShapeDtypeStruct((steps * BWD_COLS, feat), kind),
        compiler_params=params(),
        cost_estimate=pl.CostEstimate(
            flops=2 * node_total * steps * BWD_COLS * 256,
            bytes_accessed=node_total * steps * BWD_COLS,
            transcendentals=0,
        ),
        name="spread_near" if extra else "spread_far",
    )(in_hbm(a), d_rows, *extra)


def factored_step(weight, gradient, row_new, col_new, row_mean):
    estimate = row_new[..., None, :] * col_new[..., :, None] / row_mean[..., None, None]
    return weight - LEARN_RATE * gradient * lax.rsqrt(estimate)


def vector_step(param, gradient, state):
    state_new = 0.5 * state + 0.5 * (gradient * gradient + SQUARE_EPS)
    return (param - VECTOR_RATE * gradient * lax.rsqrt(state_new), state_new)


def on_device(
    features,
    labels,
    train_mask,
    boundary,
    neighbours,
    counts,
    first_weight,
    rest_weight,
    head_weight,
    norm_params,
    head_bias,
    first_row,
    first_col,
    rest_row,
    rest_col,
    head_row,
    head_col,
    norm_state,
    bias_state,
    *,
    total,
):
    me = lax.axis_index("dom").astype(I32)
    me_ref = me[None]
    depth = norm_params.shape[0]
    own = boundary.shape[1]
    node_total, f_in = features.shape
    hid = norm_params.shape[2]
    classes = head_bias.shape[0]
    cols_own = hid // total if hid >= total else 1

    first_t = first_weight.T
    rest_t = jnp.swapaxes(rest_weight, 1, 2)
    ids = jnp.swapaxes(neighbours, 1, 2)

    col = jnp.arange(hid, dtype=I32)
    position = place((col // cols_own) ^ me, total) * cols_own + col % cols_own
    perm = (position[:, None] == jnp.arange(hid, dtype=I32)[None, :]).astype(BF)

    (hidden, first_rows), tiles = first_message(
        features.T, boundary, first_t, rest_t, head_weight, train_mask[None]
    )
    f_wide = hidden.shape[1]

    tables = [[None, None] for _ in range(depth)]
    parts = [None] * depth

    def beside(layer, table):
        def far(wait):
            tables[layer][1] = build_far(after(me_ref, wait), ids, counts, layer, total, own)
            return tables[layer][1]

        def near(wait):
            parts[layer], *matrix = near_step(ids, counts, after(table, wait), layer)
            tables[layer][0] = matrix[0] if matrix else None
            return parts[layer]

        return [far, near, None]

    got = gather_rows(first_rows, total, beside(0, hidden))
    got = [g.reshape(total // 2, -1, 128) for g in got]
    shared = [g[:, :own].reshape(-1, 128) for g in got]
    both = jnp.concatenate([g[:, own:] for g in got], axis=0)
    packed = both[:, : tiles * cols_own].reshape(total, tiles, cols_own, 128)
    packed = jnp.swapaxes(packed, 1, 2).reshape(hid, tiles * 128)
    packed = mm(perm, packed, D10).astype(BF)
    marks = both[:, tiles * cols_own].astype(F32)
    weights, marks, perm = lax.optimization_barrier((packed, marks, perm))

    saved = []
    for layer in range(depth):
        if layer:
            shared = gather_rows(published, total, beside(layer, hidden))
        a_loc, a_bnd = tables[layer]
        if layer < depth - 1:
            new, agg, published = layer_forward(
                layer, a_bnd, shared, parts[layer], hidden, counts, weights, norm_params, boundary
            )
            saved.append((a_loc, a_bnd, hidden, agg))
            hidden = new
    ds, da, *dw, dnorm, dbias, loss, label_count = top_layer(
        depth - 1, marks, a_bnd, shared, parts[-1], hidden, counts, weights, norm_params,
        labels[None], train_mask[None], head_bias[None], perm,
    )
    d_norms = [None] * depth
    d_norms[-1] = dnorm
    grads = [None] * depth
    near_steps = node_total // BWD_COLS
    far_steps = a_bnd.shape[1] // BWD_COLS
    rounds = bit_groups(total)[::-1]
    for layer in reversed(range(depth - 1)):
        low, size = rounds[0]
        dw = swap(dw if isinstance(dw, list) else cut(dw, size), low, total)
        sent = spread(a_bnd, after(da, dw[0]), (), BF, far_steps // 2, far_steps // 2)
        dw = add_up(after_all(dw, sent))
        arrived = hop(sent, 1, total)
        kept = spread(a_bnd, after(da, sent), (), BF, 0, far_steps // 2)
        far = kept.astype(F32) + arrived.astype(F32)
        near = None
        for low, size in rounds[1:]:
            far, dw = cut(far, size), cut(dw, size)
            edge, width = far[0].shape
            tall = dw[0].shape[0]
            stacks = [
                jnp.concatenate([far[d]] + [dw[d][:, c : c + width] for c in range(0, dw[d].shape[1], width)], axis=0)
                for d in range(size)
            ]
            stacks = swap([stacks[0]] + [stack.astype(BF) for stack in stacks[1:]], low, total)
            if near is None:
                near = spread(a_loc, after(da, stacks[0]), (ds,), F32, 0, near_steps)
                stacks[0] = after(stacks[0], near)
            stack = add_up(stacks)
            far = stack[:edge]
            dw = jnp.concatenate([stack[r : r + tall] for r in range(edge, stack.shape[0], tall)], axis=1)
        grads[layer + 1] = dw
        a_loc, a_bnd, hidden, agg = saved[layer]
        sums = ()
        if not layer:
            wide = 2 * f_wide
            g_head = grads[-1][:, 2 * hid : 2 * hid + classes]
            g_rest = [g[:, : 2 * hid] for g in grads[1:]]
            sq_rest = [g * g + SQUARE_EPS for g in g_rest]
            sq_head = g_head * g_head + SQUARE_EPS
            head_row_new = 0.5 * head_row + 0.5 * jnp.mean(sq_head, axis=1)
            ends = jnp.concatenate(
                [jnp.sum(head_row_new, keepdims=True).reshape(1, 1), loss], axis=1
            )
            row = jnp.concatenate([dbias, jnp.sum(sq_head, axis=0, keepdims=True), ends], axis=1)
            row = jnp.pad(row, ((0, 0), (0, wide - row.shape[1])))
            squares = [jnp.sum(sq, axis=0, keepdims=True) for sq in sq_rest]
            squares = [sq[:, c : c + wide] for sq in squares for c in range(0, 2 * hid, wide)]
            rows = jnp.concatenate(d_norms[1:] + squares + [row], axis=0)
            sums = (jnp.pad(rows, ((0, -(rows.shape[0] + 2) % 16), (0, 0))),)
        outs = layer_backward(
            layer, near, far, boundary, hidden, agg, counts, norm_params, perm, weights, sums
        )
        dw = outs[0]
        if layer:
            d_norms[layer] = outs[1]
            ds, da = outs[2:]

    extra = dw.shape[0] - hid
    last = len(rounds) - 1
    for i, (low, size) in enumerate(rounds):
        sums = dw[-extra:]
        keep = cut(dw[:-extra], size)
        if i == last:
            keep = [jnp.concatenate([keep[p ^ d] for p in range(size)], axis=0) for d in range(size)]
        dw = add_up(swap([jnp.concatenate([part, sums], axis=0) for part in keep], low, total))
    sums, dw = dw[-extra:], dw[:-extra]
    first_sums = add_up([jnp.sum(block * block + SQUARE_EPS, axis=0, keepdims=True) for block in cut(dw, rounds[last][1])])
    for i, (low, size) in enumerate(rounds[:last]):
        mask = 1
        while mask < size:
            first_sums = first_sums + hop(first_sums, mask << low, total)
            if not i:
                sums = after(sums, first_sums)
            mask *= 2
    g_wide = dw[:cols_own]
    g_first = jnp.concatenate([g_wide[:, :f_in], g_wide[:, f_wide : f_wide + f_in]], axis=1)
    first_sums = jnp.concatenate([first_sums[0, :f_in], first_sums[0, f_wide : f_wide + f_in]])
    sq_first = g_first * g_first + SQUARE_EPS
    g_rest = jnp.stack(g_rest)
    sq_rest = jnp.stack(sq_rest)

    g_norms = sums[: 2 * depth].reshape(norm_params.shape)
    at = 2 * depth
    tall = (depth - 1) * 2 * hid // wide
    rest_sums = sums[at : at + tall].reshape(rest_row.shape)
    row = sums[at + tall]
    g_bias = row[:classes]
    head_sums = row[classes : 2 * classes]
    head_row_mean = row[2 * classes] / hid
    loss_sum = row[2 * classes + 1]

    first_row_new = 0.5 * first_row + 0.5 * first_sums / hid
    first_col_new = 0.5 * first_col + 0.5 * jnp.mean(sq_first, axis=1)
    rest_row_new = 0.5 * rest_row + 0.5 * rest_sums / hid
    rest_col_new = 0.5 * rest_col + 0.5 * jnp.mean(sq_rest, axis=2)
    head_col_new = 0.5 * head_col + 0.5 * head_sums / hid
    first_new = factored_step(first_t, g_first, first_row_new, first_col_new, jnp.mean(first_row_new))
    rest_new = factored_step(rest_t, g_rest, rest_row_new, rest_col_new, jnp.mean(rest_row_new, axis=1))
    head_new = head_weight - LEARN_RATE * g_head * lax.rsqrt(
        head_row_new[:, None] * head_col_new[None, :] / head_row_mean
    )
    norm_new, norm_state_new = vector_step(norm_params, g_norms, norm_state)
    bias_new, bias_state_new = vector_step(head_bias, g_bias, bias_state)
    first_new = first_new.T
    rest_new = jnp.swapaxes(rest_new, 1, 2)
    return (
        loss_sum,
        label_count[0, 0],
        first_new,
        rest_new,
        head_new,
        norm_new,
        bias_new,
        g_first.T,
        jnp.swapaxes(g_rest, 1, 2),
        g_head,
        g_norms,
        g_bias,
        first_row_new,
        first_col_new,
        rest_row_new,
        rest_col_new,
        head_row_new,
        head_col_new,
        norm_state_new,
        bias_state_new,
        first_new.astype(BF),
        rest_new.astype(BF),
        head_new.astype(BF),
        norm_new.astype(BF),
    )


def solution(mesh):
    placed = (
        P("dom", None),
        P("dom"),
        P("dom"),
        P(None, "dom"),
        P(None, "dom", None),
        P(None, "dom"),
        P(None, "dom"),
        P(None, None, "dom"),
        P("dom", None),
        P(),
        P(),
        P(),
        P("dom"),
        P(),
        P(None, "dom"),
        P("dom"),
        P(),
        P(),
        P(),
    )
    return jax.shard_map(
        functools.partial(on_device, total=mesh.shape["dom"]),
        mesh=mesh,
        in_specs=placed,
        out_specs=(
            P(),
            P(),
            P(None, "dom"),
            P(None, None, "dom"),
            P("dom", None),
            P(),
            P(),
            P(None, "dom"),
            P(None, None, "dom"),
            P("dom", None),
            P(),
            P(),
            P(),
            P("dom"),
            P(),
            P(None, "dom"),
            P("dom"),
            P(),
            P(),
            P(),
            P(None, "dom"),
            P(None, None, "dom"),
            P("dom", None),
            P(),
        ),
        check_vma=False,
    )
```
